128 devices in a mesh: pipe: 2 (over core), tensor: 2 (over x_hi), dp: 32 (over z, y, x_lo).
Axes of the slice: x: 4 (x_hi: 2, x_lo: 2; x = x_hi * 2 + x_lo), y: 4, z: 4, core: 2. Of those that a mesh axis runs over, the one named last changes fastest.
Arguments:
- hidden: bfloat16 [2, 32, 256, 1536], P(None, 'dp'), may hold values from -6 to 6
- segments: int32 [2, 32, 256], P(None, 'dp'), may hold values from 0 to 3, never falling along the last dimension, each value on 1 to 128 neighbouring positions
- cotangent: bfloat16 [2, 32, 256, 1536], P(None, 'dp'), may hold values from -6 to 6
- norm_gain: float32 [2, 1536], P('pipe'), may hold values from 0.5 to 1.5
- main_projection_weight: bfloat16 [2, 1536, 2, 3072], P('pipe', None, None, 'tensor'), may hold values from -0.15625 to 0.15625
- state_projection_weight: bfloat16 [2, 1536, 256], P('pipe'), may hold values from -0.15625 to 0.15625
- step_projection_weight: bfloat16 [2, 1536, 48], P('pipe', None, 'tensor'), may hold values from -0.078125 to 0.078125
- conv_main: float32 [2, 5, 3072], P('pipe', None, 'tensor'), may hold values from -0.5 to 0.5
- conv_state: float32 [2, 5, 256], P('pipe'), may hold values from -0.5 to 0.5
- step_bias: float32 [2, 48], P('pipe', 'tensor'), may hold values from -7 to -2.3
- decay_log: float32 [2, 48], P('pipe', 'tensor'), may hold values from 0 to 2.77
- skip_scale: float32 [2, 48], P('pipe', 'tensor'), may hold values from 0.5 to 1.5
- gate_gain: float32 [2, 3072], P('pipe', 'tensor'), may hold values from 0.5 to 1.5
- output_projection_weight: bfloat16 [2, 3072, 1536], P('pipe', 'tensor'), may hold values from -0.109375 to 0.109375
Outputs:
- hidden_states: bfloat16 [2, 2, 32, 256, 1536], P('pipe', None, 'dp')
- input_grads: bfloat16 [2, 2, 32, 256, 1536], P('pipe', None, 'dp')
- grad_norm_gain: float32 [2, 1536], P('pipe')
- grad_proj_main: float32 [2, 1536, 2, 3072], P('pipe', 'dp', None, 'tensor')
- grad_proj_state: float32 [2, 1536, 256], P('pipe', 'dp')
- grad_proj_step: float32 [2, 1536, 48], P('pipe', 'dp', 'tensor')
- grad_conv_main: float32 [2, 5, 3072], P('pipe', None, 'tensor')
- grad_conv_state: float32 [2, 5, 256], P('pipe')
- grad_step_bias: float32 [2, 48], P('pipe', 'tensor')
- derivative_of_fading_logarithm: float32 [2, 48], P('pipe', 'tensor')
- grad_skip_scale: float32 [2, 48], P('pipe', 'tensor')
- grad_gate_gain: float32 [2, 3072], P('pipe', 'tensor')
- grad_proj_out: float32 [2, 3072, 1536], P('pipe', ('tensor', 'dp'))
The draws below stay inside these ranges and needn't reach their ends.
Inputs may be any that keep to these rules, and one draw needn't show every extreme that they name: `segments`: ids never fall along a sequence; one document holds 1 to 128 tokens.
All inputs are finite; a program needn't handle non-finite values.
Results may differ from the reference program's by a relative error of at most 0.014.
Values may be sent and summed in bfloat16 or wider, within the bound.
No kernel may reach another device: no remote copies, remote signals or barrier semaphores. Data moves between devices by JAX's collectives and lax.ppermute only.
A program may use at most 192 MiB of HBM per device.

```python
import math
import jax
import jax.numpy as jnp
import numpy as np
from jax import lax

D = 1536
HEADS = 48
HEADDIM = 64
STATE = 128
CONV = 4
SEQ = 256
MICRO = 2
DI = 3072
BATCH = 32
N_PIPE = 2


def levels(key, shape, pieces, smallest, high):
    def one(dim, shards_of):
        draws = jax.random.uniform(jax.random.fold_in(jax.random.fold_in(key, 6), dim), (shards_of,), jnp.float32, smallest / len(pieces), high / len(pieces))
        return jnp.repeat(jnp.exp(draws), shape[dim] // shards_of).reshape((-1,) + (1,) * (len(shape) - dim - 1))

    gain = one(*pieces[0])
    for cut in pieces[1:]:
        gain = gain * one(*cut)
    return gain


def split_up(count, total, limit, skew):
    weights = [(1 << 20) // math.isqrt(grade ** skew) + 1 for grade in range(2, count + 1)]
    surplus, given = total - limit - (count - 1), [1] * (count - 1)
    while surplus > 0:
        candidates = [i for i in range(count - 1) if given[i] < limit]
        mass, budget = sum([weights[i] for i in candidates]), surplus
        for i in candidates:
            addition = min(limit - given[i], max(1, budget * weights[i] // mass), surplus)
            given[i] = given[i] + addition
            surplus = surplus - addition
    return np.array([limit] + given)


def ragged_sizes(own_key, amount, total, reach, lean):
    if amount == 2:
        one = jax.random.randint(own_key, (), max(1, total - reach), min(reach, total - 1) + 1)
        return jnp.stack([one, total - one])
    lengths = jnp.asarray(split_up(amount, total, reach, lean), jnp.int32)
    twos = (amount - 1) // 2
    donor, taker = lengths[1:1 + 2 * twos:2], lengths[2:2 + 2 * twos:2]
    room = jnp.minimum(donor - 1, reach - taker)
    shifted = jax.random.randint(jax.random.fold_in(own_key, 1), (twos,), 0, 1 << 20) % (room + 1)
    lengths = lengths.at[1:1 + 2 * twos:2].set(donor - shifted).at[2:2 + 2 * twos:2].set(taker + shifted)
    return lengths[jax.random.permutation(jax.random.fold_in(own_key, 2), amount)]


def bell_draw(key, shape, width, limit, pieces=(), held_as=jnp.bfloat16):
    values = jax.random.normal(key, shape, jnp.float32) * width
    if len(pieces) > 0:
        values = levels(key, shape, pieces, -0.22, 0.18) * values
    return jnp.clip(values, min=-limit, max=limit).astype(held_as)


def setup_inputs(seed: int = 0) -> dict:
    seeds = jax.random.split(jax.random.key(seed), 15)
    hidden = bell_draw(seeds[0], (MICRO, BATCH, SEQ, D), 1.0, 6.0, ((1, 32),))
    segments = jax.vmap(lambda own: jnp.searchsorted(jnp.cumsum(ragged_sizes(own, max(3, SEQ // 64), SEQ, SEQ // 2, 0)), jnp.arange(SEQ), side="right"))(jax.random.split(seeds[1], MICRO * BATCH)).reshape((MICRO, BATCH, SEQ)).astype(jnp.int32)
    cotangent = bell_draw(seeds[2], (MICRO, BATCH, SEQ, D), 1.0, 6.0, ((1, 32),))
    norm_gain = jnp.clip(1.0 + 0.1 * jax.random.normal(seeds[3], (N_PIPE, D), jnp.float32), 0.5, 1.5)
    main_projection_weight = bell_draw(seeds[4], (N_PIPE, D, 2, DI), D ** -0.5, 0.15625, ((0, 2), (3, 2)))
    state_projection_weight = bell_draw(seeds[5], (N_PIPE, D, 2 * STATE), D ** -0.5, 0.15625, ((0, 2),))
    step_projection_weight = bell_draw(seeds[6], (N_PIPE, D, HEADS), (4 * D) ** -0.5, 0.078125, ((0, 2), (2, 2)))
    conv_main = jnp.clip(jax.random.uniform(seeds[7], (N_PIPE, CONV + 1, DI), jnp.float32, -0.5, 0.5) * levels(seeds[7], (N_PIPE, CONV + 1, DI), ((0, 2), (2, 2)), -0.4, 0.0), -0.5, 0.5)
    conv_state = jnp.clip(jax.random.uniform(seeds[8], (N_PIPE, CONV + 1, 2 * STATE), jnp.float32, -0.5, 0.5) * levels(seeds[8], (N_PIPE, CONV + 1, 2 * STATE), ((0, 2),), -0.4, 0.0), -0.5, 0.5)
    step_bias = jnp.clip(-7.0 + 4.7 * jax.random.uniform(seeds[9], (N_PIPE, HEADS), jnp.float32) ** levels(seeds[9], (N_PIPE, HEADS), ((0, 2), (1, 2)), -0.2, 0.2), -7.0, -2.3)
    decay_log = jnp.clip(2.77 * jax.random.uniform(seeds[10], (N_PIPE, HEADS), jnp.float32) ** levels(seeds[10], (N_PIPE, HEADS), ((0, 2), (1, 2)), -0.2, 0.2), 0.0, 2.77)
    skip_scale = jnp.clip(0.5 + 1.0 * jax.random.uniform(seeds[11], (N_PIPE, HEADS), jnp.float32) ** levels(seeds[11], (N_PIPE, HEADS), ((0, 2), (1, 2)), -0.2, 0.2), 0.5, 1.5)
    gate_gain = jnp.clip(1.0 + 0.1 * jax.random.normal(seeds[12], (N_PIPE, DI), jnp.float32), 0.5, 1.5)
    output_projection_weight = bell_draw(seeds[13], (N_PIPE, DI, D), DI ** -0.5, 0.109375, ((0, 2), (1, 2)))
    return dict(hidden=hidden, segments=segments, cotangent=cotangent, norm_gain=norm_gain, main_projection_weight=main_projection_weight, state_projection_weight=state_projection_weight, step_projection_weight=step_projection_weight, conv_main=conv_main, conv_state=conv_state, step_bias=step_bias, decay_log=decay_log, skip_scale=skip_scale, gate_gain=gate_gain, output_projection_weight=output_projection_weight)


epsilon = 1e-05
highest = lax.Precision.HIGHEST

@jax.custom_vjp
def low(v):
    return lax.optimization_barrier(v.astype(jnp.bfloat16)).astype(jnp.float32)

@jax.custom_vjp
def low_back(v):
    return v

def low_keep(v):
    return (low(v), None)

def low_pass(kept, grad):
    return (grad,)

def back_keep(v):
    return (v, None)

def back_low(kept, grad):
    return (low(grad),)
low.defvjp(low_keep, low_pass)
low_back.defvjp(back_keep, back_low)

def causal_conv(values, weights, seg_ids):
    seq_len = values.shape[0]
    positions = jnp.arange(seq_len)
    summed = jnp.zeros_like(values) + weights[CONV]
    for shift_lag in range(CONV):
        moved = jnp.concatenate([jnp.zeros((shift_lag, values.shape[1]), values.dtype), values[:seq_len - shift_lag]], axis=0)
        earlier = jnp.concatenate([jnp.full((shift_lag,), -1, jnp.int32), seg_ids[:seq_len - shift_lag].astype(jnp.int32)], axis=0)
        same_doc = ((earlier == seg_ids) & (positions >= shift_lag)).astype(values.dtype)
        summed = summed + weights[CONV - 1 - shift_lag] * moved * same_doc[:, None]
    return jax.nn.silu(summed)

def layer(hidden_in, seg_ids, norm_gain, main_projection_weight, state_projection_weight, step_projection_weight, conv_main, conv_state, step_bias, decay_log, skip_scale, gate_gain, output_projection_weight):
    seq_len = hidden_in.shape[0]
    normed = hidden_in * lax.rsqrt(lax.optimization_barrier(jnp.mean(hidden_in * hidden_in, axis=-1, keepdims=True)) + epsilon) * norm_gain
    rounded_values = low(normed)
    gate_pre = low_back(jnp.dot(rounded_values, main_projection_weight[:, 0, :], precision=highest))
    inner_pre = low_back(jnp.dot(rounded_values, main_projection_weight[:, 1, :], precision=highest))
    state_preactivation = low_back(jnp.dot(rounded_values, state_projection_weight, precision=highest))
    unprocessed_step = low_back(jnp.dot(rounded_values, step_projection_weight, precision=highest))
    inner_conv = low(causal_conv(inner_pre, conv_main, seg_ids))
    state_conv = low(causal_conv(state_preactivation, conv_state, seg_ids))
    keys_b = state_conv[:, :STATE]
    query_c = state_conv[:, STATE:]
    intersection = low_back(jnp.dot(query_c, keys_b.T, precision=highest))
    discretization_interval = jax.nn.softplus(unprocessed_step + step_bias)
    decay_sum = jnp.cumsum(discretization_interval * -jnp.exp(decay_log), axis=0)
    positions = jnp.arange(seq_len)
    allowed = ((positions[:, None] >= positions[None, :]) & (seg_ids[:, None] == seg_ids[None, :]))[:, :, None]
    decay_gaps = decay_sum[:, None, :] - decay_sum[None, :, :]
    decay_term = jnp.where(allowed, jnp.exp(jnp.where(allowed, decay_gaps, 0.0)), 0.0)
    mixing = low(intersection[:, :, None] * decay_term * discretization_interval[None, :, :])
    head_values = inner_conv.reshape(seq_len, HEADS, HEADDIM)
    mixed_out = low_back(jnp.einsum('tsh,shp->thp', mixing, head_values, precision=highest))
    combined = (mixed_out + skip_scale[None, :, None] * head_values).reshape(seq_len, HEADS * HEADDIM)
    gated_out = combined * jax.nn.silu(gate_pre)
    scaled = gated_out * lax.rsqrt(lax.optimization_barrier(jnp.mean(gated_out * gated_out, axis=-1, keepdims=True)) + epsilon) * gate_gain
    branch = low_back(jnp.dot(low(scaled), output_projection_weight, precision=highest))
    return hidden_in + branch

def reference(hidden, segments, cotangent, norm_gain, main_projection_weight, state_projection_weight, step_projection_weight, conv_main, conv_state, step_bias, decay_log, skip_scale, gate_gain, output_projection_weight):
    weights_all = (norm_gain, main_projection_weight, state_projection_weight, step_projection_weight, conv_main, conv_state, step_bias, decay_log, skip_scale, gate_gain, output_projection_weight)
    lower_params = tuple((array[0].astype(jnp.float32) for array in weights_all))
    upper_params = tuple((array[1].astype(jnp.float32) for array in weights_all))
    total_seqs = MICRO * BATCH
    flat_hidden = hidden.reshape(total_seqs, SEQ, D)
    flat_segments = segments.reshape(total_seqs, SEQ)
    flat_cotangent = cotangent.reshape(total_seqs, SEQ, D)

    def one_sequence(carry, element):
        seq_hidden, seq_ids, seq_cotangent = element

        def apply_layer(hidden_in, *params):
            return layer(hidden_in, seq_ids, *params)
        lower_out, lower_pull = jax.vjp(apply_layer, seq_hidden.astype(jnp.float32), *lower_params)
        lower_round = lower_out.astype(jnp.bfloat16)
        upper_out, upper_pull = jax.vjp(apply_layer, lower_round.astype(jnp.float32), *upper_params)
        upper_grads = upper_pull(seq_cotangent.astype(jnp.float32))
        passed = upper_grads[0].astype(jnp.bfloat16)
        lower_grads = lower_pull(passed.astype(jnp.float32))
        lower_total = tuple((running + gradient for running, gradient in zip(carry[0], lower_grads[1:])))
        upper_total = tuple((running + gradient for running, gradient in zip(carry[1], upper_grads[1:])))
        return ((lower_total, upper_total), (lower_round, upper_out.astype(jnp.bfloat16), lower_grads[0].astype(jnp.bfloat16), passed))
    empty = tuple((jnp.zeros_like(array) for array in lower_params))
    (lower_sums, upper_sums), stacked = lax.scan(one_sequence, (empty, empty), (flat_hidden, flat_segments, flat_cotangent))
    shape_out = (MICRO, BATCH, SEQ, D)
    hidden_states = jnp.stack([stacked[0].reshape(shape_out), stacked[1].reshape(shape_out)])
    input_grads = jnp.stack([stacked[2].reshape(shape_out), stacked[3].reshape(shape_out)])
    grads = tuple((jnp.stack([lower_item, upper_item]) for lower_item, upper_item in zip(lower_sums, upper_sums)))
    return (hidden_states, input_grads, grads[0], grads[1], grads[2], grads[3], grads[4], grads[5], grads[6], grads[7], grads[8], grads[9], grads[10])
```

```python
import jax
import jax.numpy as jnp
from jax import lax
from jax.experimental import pallas as pl
from jax.experimental.pallas import tpu as pltpu
from jax.sharding import PartitionSpec as P

F32 = jnp.float32
BF16 = jnp.bfloat16
EPS = 1e-05
D = 1536
Q = 768
HQ = 12
DI = 3072
T = 256
HALF = 128
EXT = D + 128
TAIL = Q + 256 + 128
NZ = 640
NEG = -1e30


def dot(a, b):
    return lax.dot_general(a, b, (((1,), (0,)), ((), ())), preferred_element_type=F32)


def dot_nt(a, b):
    return lax.dot_general(a, b, (((1,), (1,)), ((), ())), preferred_element_type=F32)


def sigmoid(v):
    return 0.5 * jnp.tanh(0.5 * v) + 0.5


def softplus(v):
    e = jnp.exp(-jnp.abs(v))
    small = e * (1.0 - e * (0.5 - e * (1.0 / 3.0 - e * 0.25)))
    return jnp.maximum(v, 0.0) + jnp.where(e < 0.01, small, jnp.log(1.0 + e))


def iota(shape, dim):
    return lax.broadcasted_iota(jnp.int32, shape, dim)


def pieces(v):
    high = v.astype(BF16).astype(F32)
    mid = (v - high).astype(BF16).astype(F32)
    return high, mid, (v - high - mid).astype(BF16).astype(F32)


def lanes_of(v, first):
    lane = iota((v.shape[0], 128), 1)
    out = jnp.zeros((v.shape[0], 128), F32)
    for k, part in enumerate(pieces(v)):
        out = out + jnp.where(lane == first + k, part, 0.0)
    return out


def scalar_at(ext, first, count=3):
    lane = iota(ext.shape, 1)
    keep = (lane >= first) & (lane < first + count)
    return jnp.sum(jnp.where(keep, ext, 0.0), axis=1, keepdims=True)


def half_rows(which):
    return pl.ds(pl.multiple_of(which * HALF, HALF), HALF)


def whole(shape):
    return pl.BlockSpec(shape, lambda i: (0,) * len(shape))


def part(shape, at):
    return pl.BlockSpec(shape, lambda i: at)


ANY = pl.BlockSpec(memory_space=pl.ANY)


def kernel_call(body, ins, outs, scratch=(), flops=0, name=None, limit=40):
    arrays = [a for a, _ in ins]
    specs = [whole(a.shape) if s is None else s for a, s in ins]
    moved = sum(a.size * a.dtype.itemsize for a in arrays)
    return pl.pallas_call(
        body,
        grid=(1,),
        in_specs=specs,
        out_specs=[whole(s) for s, _ in outs],
        out_shape=[jax.ShapeDtypeStruct(s, d) for s, d in outs],
        scratch_shapes=list(scratch),
        compiler_params=pltpu.CompilerParams(vmem_limit_bytes=limit * 1024 * 1024),
        cost_estimate=pl.CostEstimate(flops=flops, bytes_accessed=moved, transcendentals=0),
        name=name,
    )(*arrays)


def start_either(mine, own, other, dst, sem):
    @pl.when(mine)
    def _():
        pltpu.make_async_copy(own, dst, sem).start()

    @pl.when(jnp.logical_not(mine))
    def _():
        pltpu.make_async_copy(other, dst, sem).start()


def wait_for(src, dst, sem):
    pltpu.make_async_copy(src, dst, sem).wait()


def pick(mine, own, other, dst):
    @pl.when(mine)
    def _():
        dst[...] = own[...]

    @pl.when(jnp.logical_not(mine))
    def _():
        dst[...] = other[...]


def join(p, own, other, dst, columns=slice(None)):
    dst[half_rows(p), :] = own[:, columns].astype(dst.dtype)
    dst[half_rows(1 - p), :] = other[:, columns].astype(dst.dtype)


TAPS, GATE, NORM, STAPS, SKIP, HEAD = 0, 5, 6, 8, 13, 16


def pack_kernel(ng, cm, cs, sb, dl, ss, gg, wd, own, other, wd_own, wd_other):
    p = lax.axis_index("pipe")
    for target, wd_target, which in ((own, wd_own, p), (other, wd_other, 1 - p)):
        lanes = pl.ds(pl.multiple_of(which * Q, Q), Q)
        target[...] = jnp.zeros(target.shape, F32)
        target[TAPS : TAPS + 5, :] = cm[:, lanes]
        target[GATE : GATE + 1, :] = gg[:, lanes]
        target[NORM : NORM + 1, :] = ng[:, :Q]
        target[NORM + 1 : NORM + 2, :] = ng[:, Q:]
        target[STAPS : STAPS + 5, :256] = cs[...]
        second = which == 1
        head = [jnp.where(second, v[:, HQ : 2 * HQ], v[:, :HQ]) for v in (sb, dl, ss)]
        row = jnp.concatenate([head[2], jnp.zeros((1, 128 - HQ), F32)], axis=1)
        column = jnp.broadcast_to(row, (128, 128)).T
        owner = iota((16, Q), 1) // 64 == iota((16, Q), 0)
        spread = jnp.where(owner, column[:16, :1], 0.0)
        target[SKIP : SKIP + 1, :] = jnp.sum(spread, axis=0, keepdims=True)
        rows = [jnp.concatenate([v, jnp.zeros((1, 128 - HQ), F32)], axis=1) for v in head[:2]]
        square = jnp.concatenate([rows[0], -jnp.exp(rows[1]), jnp.zeros((126, 128), F32)], axis=0)
        target[HEAD : HEAD + 16, :128] = square.T[:16, :]
        wide = wd[...].astype(F32)
        chosen = jnp.where(second, wide[HQ:, :], wide[:HQ, :])
        wd_target[...] = jnp.concatenate([chosen, jnp.zeros((4, D), F32)], axis=0).astype(BF16)


def project_body(layer, p, x, par, wd, ws, w_scr, waits, outs):
    rounded, rounded_t, pre, spre, raw = outs
    factor = lax.rsqrt(jnp.mean(x * x, axis=1, keepdims=True) + EPS)
    scaled = x * factor
    for c in range(2):
        cols = slice(c * Q, (c + 1) * Q)
        normed = scaled[:, cols] * par[NORM + c : NORM + c + 1, :]
        rounded[:, cols] = normed.astype(BF16)
        rounded_t[cols, :] = normed.T.astype(BF16)
    raw[...] = dot_nt(wd[...], rounded[...])
    waits[0]()
    spre[...] = dot(rounded[...], ws[...])
    waits[1]()
    for u in range(2):
        for c in range(3):
            cols = slice(c * 256, (c + 1) * 256)
            pre[:, u * Q + c * 256 : u * Q + (c + 1) * 256] = dot(rounded[...], w_scr[u, :, cols])


def project(layer, m, xs, pars, wds, wss, ws_main):
    first = layer == 0

    def body(*refs):
        xr = refs[: 1 if first else 2]
        par_o, par_r, wd_o, wd_r, ws_o, ws_r, wm_o, wm_r = refs[len(xr) : len(xr) + 8]
        rest = refs[len(xr) + 8 :]
        outs, scr = rest[: 5 if first else 6], rest[5 if first else 6 :]
        par, wd, ws, w_scr, sem = scr
        p = lax.axis_index("pipe")
        mine = p == layer
        own_main = wm_o.at[:, :, pl.ds(pl.multiple_of(p * Q, Q), Q)]
        start_either(mine, ws_o, ws_r, ws, sem.at[0])
        start_either(mine, own_main, wm_r, w_scr, sem.at[1])
        pick(mine, par_o, par_r, par)
        pick(mine, wd_o, wd_r, wd)
        if first:
            x = xr[0][0].astype(F32)
        else:
            join(p, xr[0], xr[1], outs[5], slice(0, D))
            x = outs[5][...].astype(F32)
        waits = (
            lambda: wait_for(ws_r, ws, sem.at[0]),
            lambda: wait_for(wm_r, w_scr, sem.at[1]),
        )
        project_body(layer, p, x, par, wd, ws, w_scr, waits, outs[:5])

    if first:
        ins = [(xs, part((1, T, D), (m, 0, 0)))]
    else:
        ins = [(xs[0], None), (xs[1], None)]
    ins += [(a, None) for a in pars] + [(a, None) for a in wds]
    ins += [(a, ANY) for a in wss] + [(a, ANY) for a in ws_main]
    outs = [((T, D), BF16), ((D, T), BF16), ((T, D), F32), ((T, T), F32), ((16, T), F32)]
    if not first:
        outs.append(((T, D), BF16))
    scratch = [
        pltpu.VMEM((32, Q), F32),
        pltpu.VMEM((16, D), BF16),
        pltpu.VMEM((D, 256), BF16),
        pltpu.VMEM((2, D, Q), BF16),
        pltpu.SemaphoreType.DMA((2,)),
    ]
    flops = 2 * T * D * (D + 256)
    return kernel_call(body, ins, outs, scratch, flops, f"project_{layer}_{m}")


def document_ids(seg_ref):
    row = jnp.broadcast_to(seg_ref[0].astype(F32), (T, T))
    return row.T, row


def same_document(by_token, lag):
    position = iota((T, T), 0)
    earlier = pltpu.roll(by_token, lag, 0)
    return jnp.where((earlier == by_token) & (position >= lag), 1.0, 0.0)


def convolve(values, taps, same):
    out = taps[4:5] + taps[3:4] * values
    for lag in range(1, 4):
        out = out + taps[3 - lag : 4 - lag] * (pltpu.roll(values, lag, 0) * same[lag])
    return out


def convolve_back(d_sum, values, taps, same):
    d_values = taps[3:4] * d_sum
    rows = [None] * 5
    rows[4] = jnp.sum(d_sum, axis=0, keepdims=True)
    rows[3] = jnp.sum(d_sum * values, axis=0, keepdims=True)
    for lag in range(1, 4):
        held = d_sum * same[lag]
        d_values = d_values + taps[3 - lag : 4 - lag] * pltpu.roll(held, T - lag, 0)
        moved = pltpu.roll(values, lag, 0)
        rows[3 - lag] = jnp.sum(held * moved, axis=0, keepdims=True)
    return d_values, jnp.concatenate(rows, axis=0)


def step_sizes(raw, par):
    before = raw[...] + par[HEAD : HEAD + 16, 0:1]
    step = softplus(before)
    total = step * par[HEAD : HEAD + 16, 1:2]
    lane = iota(total.shape, 1)
    shift = 1
    while shift < T:
        total = total + jnp.where(lane >= shift, pltpu.roll(total, shift, 1), 0.0)
        shift *= 2
    return before, step, total


def columns_of(rows):
    return jnp.concatenate([rows, jnp.zeros((112, T), F32)], axis=0).T


def mix(layer, m, pre, spre, raw, seg, pars, wos):
    def body(pre, spre, raw, seg, par_o, par_r, wo_o, wo_r, *rest):
        mixed, inner_out, send, keep, par, wo, gs, u_scr, sem = rest
        p, t = lax.axis_index("pipe"), lax.axis_index("tensor")
        mine = p == layer
        own = wo_o.at[pl.ds(pl.multiple_of(p * Q, Q), Q), :]
        start_either(mine, own, wo_r, wo, sem)
        pick(mine, par_o, par_r, par)
        by_token, by_row = document_ids(seg)
        same = [None] + [same_document(by_token, lag) for lag in range(1, 4)]
        allowed = (by_token == by_row) & (iota((T, T), 0) >= iota((T, T), 1))
        state = convolve(spre[...], par[STAPS : STAPS + 5, :256], same)
        state = (state * sigmoid(state)).astype(BF16)
        crossed = dot_nt(state[:, 128:], state[:, :128])
        _, step, total = step_sizes(raw, par)
        total_t = columns_of(total)
        low = iota((T, 128), 1) < 64
        squares = jnp.zeros((T, 1), F32)
        for g in range(3):
            cols = slice(g * 256, (g + 1) * 256)
            summed = convolve(pre[:, Q + g * 256 : Q + (g + 1) * 256], par[TAPS : TAPS + 5, cols], same)
            inner = (summed * sigmoid(summed)).astype(BF16)
            inner_out[:, cols] = inner
            for pair in range(2):
                at = slice(g * 256 + pair * 128, g * 256 + (pair + 1) * 128)
                values = inner[:, pair * 128 : (pair + 1) * 128]
                out = None
                for k in range(2):
                    h = g * 4 + pair * 2 + k
                    gap = total_t[:, h : h + 1] - total[h : h + 1, :]
                    decay = jnp.exp(jnp.where(allowed, gap, NEG))
                    mixing = (crossed * decay * step[h : h + 1, :]).astype(BF16)
                    chosen = jnp.where(low if k == 0 else ~low, values, jnp.zeros_like(values))
                    term = dot(mixing, chosen)
                    out = term if out is None else out + term
                mixed[:, at] = out
            combined = mixed[:, cols] + par[SKIP : SKIP + 1, cols] * inner.astype(F32)
            gate = pre[:, cols]
            gated = combined * (gate * sigmoid(gate))
            squares = squares + jnp.sum(gated * gated, axis=1, keepdims=True)
            gs[:, cols] = (gated * par[GATE : GATE + 1, cols]).astype(BF16)
        wait_for(wo_r, wo, sem)
        for c in range(3):
            cols = slice(c * 512, (c + 1) * 512)
            u_scr[:, cols] = dot(gs[...], wo[:, cols]).astype(BF16)
        u_scr[:, D:] = lanes_of(squares, 3 * (2 * p + t)).astype(BF16)
        send[...] = u_scr[half_rows(1 - p), :]
        keep[...] = u_scr[half_rows(p), :]

    ins = [(pre, None), (spre, None), (raw, None), (seg, part((1, 1, T), (m, 0, 0)))]
    ins += [(a, None) for a in pars] + [(a, ANY) for a in wos]
    outs = [((T, Q), F32), ((T, Q), BF16), ((HALF, EXT), BF16), ((HALF, EXT), BF16)]
    scratch = [
        pltpu.VMEM((32, Q), F32),
        pltpu.VMEM((Q, D), BF16),
        pltpu.VMEM((T, Q), BF16),
        pltpu.VMEM((T, EXT), BF16),
        pltpu.SemaphoreType.DMA,
    ]
    flops = 2 * T * Q * D + 2 * 12 * T * T * 128
    return kernel_call(body, ins, outs, scratch, flops, f"mix_{layer}_{m}")


def finish_forward(layer, m, chip, arrived, x, cot):
    def body(chip, arrived, x, *rest):
        p = lax.axis_index("pipe")
        out = rest[-1]
        total = chip[:, :D].astype(F32) + arrived[:, :D].astype(F32)
        ext = chip[:, D:].astype(F32) + arrived[:, D:].astype(F32)
        factor = lax.rsqrt(jnp.sum(ext, axis=1, keepdims=True) / DI + EPS)
        if layer == 0:
            before = x[0, half_rows(p), :].astype(F32)
        else:
            before = x[:, :D].astype(F32)
        out[:, :D] = (before + factor * total).astype(BF16)
        tail = lanes_of(factor, 0)
        if layer == 1:
            a = rest[0][0, half_rows(p), :].astype(F32)
            pull = factor * factor * factor * (jnp.sum(a * total, axis=1, keepdims=True) / DI)
            tail = tail + lanes_of(pull, 3)
        out[:, D:] = tail.astype(BF16)

    ins = [(chip, None), (arrived, None)]
    if layer == 0:
        ins += [(x, part((1, T, D), (m, 0, 0)))]
    else:
        ins += [(x, None), (cot, part((1, T, D), (m, 0, 0)))]
    return kernel_call(body, ins, [((HALF, EXT), BF16)], (), 0, f"finish_fwd_part_{layer}_{m}", 16)[0]


def gate_back(layer, m, a, scalars, pre, mixed, inner, pars, wos):
    lower = layer == 0

    def body(*refs):
        if lower:
            a_o, a_r, s_o, s_r = refs[:4]
            refs = refs[4:]
        else:
            a_f, s_o, s_r = refs[:3]
            refs = refs[3:]
        pre, mixed, inner, par_o, par_r, wo_o, wo_r = refs[:7]
        d_gate, d_comb, scaled_t, pack = refs[7:11]
        refs = refs[11:]
        if lower:
            a_all = refs[0]
            refs = refs[1:]
        par, wo, ext, ext2, sem = refs
        p = lax.axis_index("pipe")
        mine = p == layer
        own = wo_o.at[pl.ds(pl.multiple_of(p * Q, Q), Q), :]
        start_either(mine, own, wo_r, wo, sem)
        pick(mine, par_o, par_r, par)
        join(p, s_o, s_r, ext)
        factor = scalar_at(ext[...], 0)
        if lower:
            join(p, a_o, a_r, a_all, slice(0, D))
            join(p, a_o, a_r, ext2, slice(D, EXT))
            pull = scalar_at(ext2[...], 3)
            a = a_all[...]
        else:
            pull = scalar_at(ext[...], 3)
            a = a_f[0]
        wait_for(wo_r, wo, sem)
        pack[...] = jnp.zeros(pack.shape, F32)
        for g in range(3):
            cols = slice(g * 256, (g + 1) * 256)
            d_scaled = dot_nt(a, wo[cols, :])
            values = inner[:, cols].astype(F32)
            combined = mixed[:, cols] + par[SKIP : SKIP + 1, cols] * values
            gate = pre[:, cols]
            opened = sigmoid(gate)
            silu = gate * opened
            gated = combined * silu
            normed = gated * factor
            gain = par[GATE : GATE + 1, cols]
            scaled_t[cols, :] = (normed * gain).T.astype(BF16)
            pack[0:1, cols] = jnp.sum(d_scaled * normed, axis=0, keepdims=True)
            d_gated = d_scaled * gain * factor - gated * pull
            d_combined = d_gated * silu
            d_comb[:, cols] = d_combined
            pack[1:2, cols] = jnp.sum(d_combined * values, axis=0, keepdims=True)
            d_gate[:, cols] = (d_gated * combined * (opened * (1.0 + gate * (1.0 - opened)))).astype(BF16)

    last = part((HALF, 128), (0, D // 128))
    if lower:
        ins = [(a[0], None), (a[1], None)]
    else:
        ins = [(a, part((1, T, D), (m, 0, 0)))]
    ins += [(s, last) for s in scalars]
    ins += [(pre, part((T, Q), (0, 0))), (mixed, None), (inner, None)]
    ins += [(v, None) for v in pars] + [(v, ANY) for v in wos]
    outs = [((T, Q), BF16), ((T, Q), F32), ((Q, T), BF16), ((8, Q), F32)]
    if lower:
        outs.append(((T, D), BF16))
    scratch = [
        pltpu.VMEM((32, Q), F32),
        pltpu.VMEM((Q, D), BF16),
        pltpu.VMEM((T, 128), F32),
        pltpu.VMEM((T, 128), F32),
        pltpu.SemaphoreType.DMA,
    ]
    return kernel_call(body, ins, outs, scratch, 2 * T * Q * D, f"gate_back_{layer}_{m}")


def per_head(values):
    high = values.astype(BF16)
    rest = (values - high.astype(F32)).astype(BF16)
    owner = (iota((Q, 128), 0) // 64 == iota((Q, 128), 1)).astype(BF16)
    return dot(high, owner) + dot(rest, owner)


def mix_back(layer, m, d_comb, inner, pre, spre, raw, seg, mixed, pack_a, pars):
    def body(d_comb, inner, pre, spre, raw, seg, mixed, pack_a, par_o, par_r, *rest):
        d_tail, pack, par, gap_prod, col_prod = rest
        mine = lax.axis_index("pipe") == layer
        pick(mine, par_o, par_r, par)
        by_token, by_row = document_ids(seg)
        same = [None] + [same_document(by_token, lag) for lag in range(1, 4)]
        allowed = (by_token == by_row) & (iota((T, T), 1) >= iota((T, T), 0))
        summed_s = convolve(spre[...], par[STAPS : STAPS + 5, :256], same)
        opened_s = sigmoid(summed_s)
        state = (summed_s * opened_s).astype(BF16)
        keys, query = state[:, :128], state[:, 128:]
        crossed = dot_nt(keys, query)
        before, step, total = step_sizes(raw, par)
        total_t, step_t = columns_of(total), columns_of(step)
        low = iota((T, 128), 1) < 64
        d_cross = jnp.zeros((T, T), F32)
        pack[...] = jnp.zeros(pack.shape, F32)
        for g in range(3):
            cols = slice(g * 256, (g + 1) * 256)
            heads = []
            for pair in range(2):
                at = slice(g * 256 + pair * 128, g * 256 + (pair + 1) * 128)
                values = inner[:, at]
                d_mixed = d_comb[:, at].astype(BF16)
                d_heads = None
                for k in range(2):
                    h = g * 4 + pair * 2 + k
                    side = low if k == 0 else ~low
                    gap = total[h : h + 1, :] - total_t[:, h : h + 1]
                    decay = jnp.exp(jnp.where(allowed, gap, NEG)) * step_t[:, h : h + 1]
                    mixing = (crossed * decay).astype(BF16)
                    chosen = jnp.where(side, d_mixed, jnp.zeros_like(d_mixed))
                    d_mixing = dot_nt(values, chosen)
                    d_cross = d_cross + d_mixing * decay
                    term = dot(mixing, chosen)
                    d_heads = term if d_heads is None else d_heads + term
                heads.append(d_heads)
                along = values.astype(F32) * d_heads
                col_prod[:, at] = along
                gap_prod[:, at] = d_mixed.astype(F32) * mixed[:, at] - along
            taps = par[TAPS : TAPS + 5, cols]
            values = pre[:, cols]
            summed = convolve(values, taps, same)
            opened = sigmoid(summed)
            d_inner = jnp.concatenate(heads, axis=1) + par[SKIP : SKIP + 1, cols] * d_comb[:, cols]
            d_sum = d_inner * (opened * (1.0 + summed * (1.0 - opened)))
            d_values, rows = convolve_back(d_sum, values, taps, same)
            d_tail[:, cols] = d_values.astype(BF16)
            pack[0:5, cols] = rows
        pack[5:7, :] = pack_a[0:2, :]
        crossed_b = d_cross.astype(BF16)
        d_keys = dot(crossed_b, query)
        d_query = dot(d_cross.T.astype(BF16), keys)
        d_state = jnp.concatenate([d_keys, d_query], axis=1)
        d_sum = d_state * (opened_s * (1.0 + summed_s * (1.0 - opened_s)))
        d_values, rows = convolve_back(d_sum, spre[...], par[STAPS : STAPS + 5, :256], same)
        d_tail[:, Q : Q + 256] = d_values.astype(BF16)
        pack[8:13, :256] = rows
        d_gap = per_head(gap_prod[...]).T[:16, :]
        d_col = per_head(col_prod[...]).T[:16, :]
        lane = iota(d_gap.shape, 1)
        shift = 1
        while shift < T:
            d_gap = d_gap + jnp.where(lane < T - shift, pltpu.roll(d_gap, T - shift, 1), 0.0)
            shift *= 2
        rate = par[HEAD : HEAD + 16, 1:2]
        slope = sigmoid_small(before)
        ratio = jnp.where(step > 1e-30, slope / jnp.maximum(step, 1e-30), 1.0)
        d_raw = d_col * ratio + d_gap * rate * slope
        valid = iota((16, T), 0) < HQ
        d_raw = jnp.where(valid, d_raw, 0.0)
        d_log = jnp.where(valid, d_gap * step * rate, 0.0)
        d_tail[:, Q + 256 :] = columns_of(d_raw).astype(BF16)
        bias_row = jnp.broadcast_to(jnp.sum(d_raw, axis=1, keepdims=True), (16, 128))
        log_row = jnp.broadcast_to(jnp.sum(d_log, axis=1, keepdims=True), (16, 128))
        square = jnp.concatenate([bias_row, jnp.zeros((112, 128), F32)], axis=0).T
        pack[7:8, 0:128] = square[0:1, :]
        square = jnp.concatenate([log_row, jnp.zeros((112, 128), F32)], axis=0).T
        pack[7:8, 128:256] = square[0:1, :]

    ins = [(d_comb, None), (inner, None), (pre, part((T, Q), (0, 1))), (spre, None), (raw, None)]
    ins += [(seg, part((1, 1, T), (m, 0, 0))), (mixed, None), (pack_a, None)]
    ins += [(v, None) for v in pars]
    outs = [((T, TAIL), BF16), ((16, Q), F32)]
    scratch = [pltpu.VMEM((32, Q), F32), pltpu.VMEM((T, Q), F32), pltpu.VMEM((T, Q), F32)]
    return kernel_call(body, ins, outs, scratch, 4 * 12 * T * T * 128, f"mix_back_{layer}_{m}")


def sigmoid_small(v):
    e = jnp.exp(-jnp.abs(v))
    return jnp.where(v >= 0.0, 1.0, e) / (1.0 + e)


def project_back(layer, m, d_gate, d_tail, wds, wss, ws_main):
    def body(d_gate, d_tail, wd_o, wd_r, ws_o, ws_r, wm_o, wm_r, send, keep, wd, ws, w_scr, acc, sem):
        p = lax.axis_index("pipe")
        mine = p == layer
        own_main = wm_o.at[:, :, pl.ds(pl.multiple_of(p * Q, Q), Q)]
        start_either(mine, own_main, wm_r, w_scr, sem.at[1])
        start_either(mine, ws_o, ws_r, ws, sem.at[0])
        pick(mine, wd_o, wd_r, wd)
        wait_for(ws_r, ws, sem.at[0])
        wait_for(wm_r, w_scr, sem.at[1])
        for c in range(6):
            rows = slice(c * 256, (c + 1) * 256)
            out = dot_nt(d_gate[...], w_scr[0, rows, :])
            out = out + dot_nt(d_tail[:, :Q], w_scr[1, rows, :])
            out = out + dot_nt(d_tail[:, Q : Q + 256], ws[rows, :])
            out = out + dot(d_tail[:, Q + 256 : Q + 272], wd[:, rows])
            acc[:, rows] = out.astype(BF16)
        send[...] = acc[half_rows(1 - p), :]
        keep[...] = acc[half_rows(p), :]

    ins = [(d_gate, None), (d_tail, None)] + [(a, None) for a in wds]
    ins += [(a, ANY) for a in wss] + [(a, ANY) for a in ws_main]
    outs = [((HALF, D), BF16), ((HALF, D), BF16)]
    scratch = [
        pltpu.VMEM((16, D), BF16),
        pltpu.VMEM((D, 256), BF16),
        pltpu.VMEM((2, D, Q), BF16),
        pltpu.VMEM((T, D), BF16),
        pltpu.SemaphoreType.DMA((2,)),
    ]
    return kernel_call(body, ins, outs, scratch, 2 * T * D * (D + 256), f"project_back_{layer}_{m}")


def finish_back(layer, m, chip, arrived, x, a, pars, below):
    def body(*refs):
        chip, arrived, x, a, par_o, par_r = refs[:6]
        refs = refs[6:]
        if layer == 1:
            u_o, u_r, y = refs[:3]
            refs = refs[3:]
        out, pack, par = refs
        p = lax.axis_index("pipe")
        mine = p == layer
        pick(mine, par_o, par_r, par)
        d_rounded = chip[...].astype(F32) + arrived[...].astype(F32)
        if layer == 0:
            xv = x[0, half_rows(p), :].astype(F32)
            av = a[:, :D].astype(F32)
        else:
            xv = x[:, :D].astype(F32)
            av = a[0, half_rows(p), :].astype(F32)
        factor = lax.rsqrt(jnp.mean(xv * xv, axis=1, keepdims=True) + EPS)
        normed = xv * factor
        gain = jnp.concatenate([par[NORM : NORM + 1, :], par[NORM + 1 : NORM + 2, :]], axis=1)
        pulled = d_rounded * gain
        mean = jnp.mean(pulled * normed, axis=1, keepdims=True)
        result = (av + factor * (pulled - normed * mean)).astype(BF16)
        out[:, :D] = result
        pack[...] = jnp.zeros(pack.shape, F32)
        d_gain = jnp.sum(d_rounded * normed, axis=0, keepdims=True)
        pack[13:14, :] = d_gain[:, :Q]
        pack[14:15, :] = d_gain[:, Q:]
        if layer == 1:
            branch = u_o[...].astype(F32) + u_r[...].astype(F32)
            gated = scalar_at(y[...].astype(F32), 0)
            total = jnp.sum(result.astype(F32) * branch, axis=1, keepdims=True)
            out[:, D:] = lanes_of(gated * gated * gated * (total / DI), 3).astype(BF16)
        else:
            out[:, D:] = jnp.zeros((HALF, 128), BF16)

    ins = [(chip, None), (arrived, None)]
    if layer == 0:
        ins += [(x, part((1, T, D), (m, 0, 0))), (a, None)]
    else:
        ins += [(x, None), (a, part((1, T, D), (m, 0, 0)))]
    ins += [(v, None) for v in pars]
    if layer == 1:
        narrow = part((HALF, D), (0, 0))
        ins += [(below[0], narrow), (below[1], narrow), (x, part((HALF, 128), (0, D // 128)))]
    outs = [((HALF, EXT), BF16), ((16, Q), F32)]
    return kernel_call(body, ins, outs, [pltpu.VMEM((32, Q), F32)], 0, f"finish_back_{layer}_{m}", 16)


def position():
    dp = lax.axis_index("dp")
    return dp // 8, (dp // 2) % 4, dp % 2


def chunk_of(ref, axis, offset):
    z, y, _ = position()
    if axis == "z":
        rows = ref[lax.rem(z + offset, 4)]
    else:
        rows = ref[:, lax.rem(y + offset, 4)]
    return rows.reshape(-1, T)


def weight_stage(axis, stage, lefts, rights, columns, arrived, name):
    width = columns.stop - columns.start
    half = width // 2
    lead, rows = lefts[0].shape[0], 384 if lefts[0].shape[0] == 4 else 192

    def body(l0, l1, r0, r1, *rest):
        def piece(offset):
            first = dot(chunk_of(l0, axis, offset), r0[..., columns].reshape(T, width))
            return first + dot(chunk_of(l1, axis, offset), r1[..., columns].reshape(T, width))

        if stage == 0:
            out = piece(2)
            rest[0][...] = out[:, :half].astype(BF16)
            rest[1][...] = out[:, half:].astype(BF16)
        elif stage == 1:
            from_before, from_after, to_after, to_before = rest
            out = piece(1)
            to_after[:, :half] = (out[:, :half] + from_before[...].astype(F32)).astype(BF16)
            to_after[:, half:] = out[:, half:].astype(BF16)
            out = piece(3)
            to_before[:, :half] = out[:, :half].astype(BF16)
            to_before[:, half:] = (out[:, half:] + from_after[...].astype(F32)).astype(BF16)
        else:
            from_before, from_after = rest[:2]
            outs, total = rest[2:-1], rest[-1]
            z, y, x = position()
            out = piece(0) + from_before[...].astype(F32) + from_after[...].astype(F32)
            if lead == 4:
                total[...] = out.reshape(4, 96, width)
                at = y if axis == "z" else z
                outs[0][...] = total[at]
                for offset in range(1, 4):
                    outs[offset][...] = total[lax.rem(at + offset, 4)].astype(BF16)
            else:
                total[...] = out.reshape(2, 2, 48, width)
                outs[0][...] = total[:, x]
                outs[1][...] = total[:, 1 - x].astype(BF16)

    if stage == 0:
        outs = [((rows, half), BF16)] * 2
    elif stage == 1:
        outs = [((rows, width), BF16)] * 2
    elif lead == 4:
        outs = [((96, width), F32)] + [((96, width), BF16)] * 3
    else:
        outs = [((2, 48, width), F32), ((2, 48, width), BF16)]
    scratch = []
    if stage == 2:
        scratch = [pltpu.VMEM((4, 96, width) if lead == 4 else (2, 2, 48, width), F32)]
    ins = [(a, None) for a in lefts] + [(a, s) for a, s in rights] + [(a, None) for a in arrived]
    flops = 4 * rows * T * width * (2 if stage == 1 else 1)
    return kernel_call(body, ins, outs, scratch, flops, name)


def cut_rows(pieces_in, name):
    widths = [group[0].shape[1] for group in pieces_in]

    def body(*refs):
        _, _, x = position()
        ins, outs = refs[: 4 * len(widths)], refs[4 * len(widths) : 6 * len(widths)]
        total = refs[6 * len(widths) :]
        for n in range(len(widths)):
            group = ins[4 * n : 4 * n + 4]
            out = (group[0][...] + group[2][...].astype(F32)) + (group[1][...].astype(F32) + group[3][...].astype(F32))
            total[n][...] = out.reshape(2, 48, widths[n])
            outs[2 * n][...] = total[n][x]
            outs[2 * n + 1][...] = total[n][1 - x].astype(BF16)

    ins = [(a, None) for group in pieces_in for a in group]
    outs = []
    for w in widths:
        outs += [((48, w), F32), ((48, w), BF16)]
    scratch = [pltpu.VMEM((2, 48, w), F32) for w in widths]
    return kernel_call(body, ins, outs, scratch, 0, name, 16)


def dp_index(z, y, x):
    return ((z % 4) * 4 + y % 4) * 2 + x % 2


def dp_pairs(move):
    places = [(z, y, x) for z in range(4) for y in range(4) for x in range(2)]
    return [(dp_index(*at), dp_index(*move(*at))) for at in places]


def along(axis, offset):
    if axis == "z":
        return dp_pairs(lambda z, y, x: (z + offset, y, x))
    if axis == "y":
        return dp_pairs(lambda z, y, x: (z, y + offset, x))
    return dp_pairs(lambda z, y, x: (z, y, x + offset))


def shift(value, axis, offset):
    return lax.ppermute(value, "dp", along(axis, offset))


def swap(value, axis="pipe"):
    return lax.ppermute(value, axis, [(0, 1), (1, 0)])


def add_halves(a, b):
    return (a.astype(F32) + b.astype(F32)).astype(BF16)


def scatter(axis, lefts, rights, columns, name):
    two_a, two_b = weight_stage(axis, 0, lefts, rights, columns, (), name + "_0")
    arrived = shift(two_a, axis, 1), shift(two_b, axis, 3)
    after, before = weight_stage(axis, 1, lefts, rights, columns, arrived, name + "_1")
    arrived = shift(after, axis, 1), shift(before, axis, 3)
    return weight_stage(axis, 2, lefts, rights, columns, arrived, name + "_2")


def second_axis(axis, outs):
    own, one, two, three = outs
    return own, shift(one, axis, 1), shift(two, axis, 2), shift(three, axis, 3)


def scatter_rest(groups, name):
    gathered = [second_axis(axis, outs) for axis, outs in groups]
    cut = cut_rows(gathered, name)
    return [cut[2 * n] + shift(cut[2 * n + 1], "x", 1).astype(F32) for n in range(len(groups))]


def out_rest(outs):
    own, other = outs
    held = own + shift(other, "x", 1).astype(F32)
    p = lax.axis_index("pipe")
    z = lax.axis_index("dp") // 8
    sent = held.astype(BF16)
    at = lambda place: jnp.clip(lax.rem(place, 4) - 2 * p, 0, 1)
    total = lax.dynamic_index_in_dim(held, at(z), 0, keepdims=False)
    arrived = []
    for offset in range(1, 4):
        pairs = []
        for pipe in range(2):
            for zz in range(4):
                if (zz + offset) % 4 // 2 == pipe:
                    for yy in range(4):
                        for xx in range(2):
                            pairs.append(
                                (pipe * 32 + dp_index(zz, yy, xx), pipe * 32 + dp_index(zz + offset, yy, xx))
                            )
        piece = lax.dynamic_index_in_dim(sent, at(z + offset), 0, keepdims=False)
        arrived.append(lax.ppermute(piece, ("pipe", "dp"), pairs).astype(F32))
    return (total + arrived[1]) + (arrived[0] + arrived[2])


def assemble_kernel(lower, upper_own, upper_other, out):
    p = lax.axis_index("pipe")
    for m in range(2):
        @pl.when(p == 0)
        def _():
            out[m] = lower[m][...]

        @pl.when(p == 1)
        def _():
            join(p, upper_own[m], upper_other[m], out.at[m], slice(0, D))


def local(
    hidden,
    segments,
    cotangent,
    norm_gain,
    main_w,
    state_w,
    step_w,
    conv_main,
    conv_state,
    step_bias,
    decay_log,
    skip_scale,
    gate_gain,
    out_w,
):
    p = lax.axis_index("pipe")
    hidden = hidden.reshape(2, T, D)
    cotangent = cotangent.reshape(2, T, D)
    seg = segments.reshape(2, 1, T)

    main_own = jnp.transpose(main_w[0], (1, 0, 2))
    main_got = swap(lax.dynamic_slice(main_own, (0, 0, (1 - p) * Q), (2, D, Q)))
    out_own = out_w[0]
    out_got = swap(lax.dynamic_slice(out_own, ((1 - p) * Q, 0), (Q, D)))
    state_own = state_w[0]
    state_got = swap(state_own)
    wd = jnp.transpose(step_w[0], (1, 0))
    small = [norm_gain, conv_main[0], conv_state[0], step_bias, decay_log, skip_scale, gate_gain, wd]
    par_own, par_sent, wd_own, wd_sent = kernel_call(
        pack_kernel,
        [(a, None) for a in small],
        [((32, Q), F32), ((32, Q), F32), ((16, D), BF16), ((16, D), BF16)],
        name="pack",
        limit=16,
    )
    pars = (par_own, swap(par_sent))
    wds = (wd_own, swap(wd_sent))
    wss = (state_own, state_got)
    mains = (main_own, main_got)
    wos = (out_own, out_got)

    micros = range(2)
    kept = [[None] * 2, [None] * 2]
    result = [[None] * 2, [None] * 2]
    sums = [None] * 2
    for layer in range(2):
        for m in micros:
            xs = hidden if layer == 0 else result[0][m]
            outs = project(layer, m, xs, pars, wds, wss, mains)
            rounded, rounded_t, pre, spre, raw = outs[:5]
            x_all = outs[5] if layer == 1 else None
            mixed, inner, send, keep = mix(layer, m, pre, spre, raw, seg, pars, wos)
            chip = add_halves(keep, swap(send))
            arrived = swap(chip, "tensor")
            if layer == 0:
                sums[m] = (chip, arrived)
                done = finish_forward(0, m, chip, arrived, hidden, None)
            else:
                done = finish_forward(1, m, chip, arrived, result[0][m][0], cotangent)
            result[layer][m] = (done, swap(done))
            kept[layer][m] = (rounded_t, pre, spre, raw, mixed, inner, x_all)

    main_parts = [None] * 2
    out_parts = [None] * 2
    packs = [None] * 2
    grads = [[None] * 2, [None] * 2]
    lower_a = [None] * 2
    for layer in (1, 0):
        lefts, outs_t, d_gates, d_tails, small_parts, a_all = [], [], [], [], [], []
        for m in micros:
            rounded_t, pre, spre, raw, mixed, inner, _ = kept[layer][m]
            if layer == 1:
                d_gate, d_comb, scaled_t, pack_a = gate_back(
                    1, m, cotangent, result[1][m], pre, mixed, inner, pars, wos
                )
            else:
                d_gate, d_comb, scaled_t, pack_a, whole_a = gate_back(
                    0, m, grads[1][m], result[0][m], pre, mixed, inner, pars, wos
                )
                a_all.append(whole_a)
            d_tail, pack = mix_back(layer, m, d_comb, inner, pre, spre, raw, seg, mixed, pack_a, pars)
            send, keep = project_back(layer, m, d_gate, d_tail, wds, wss, mains)
            chip = add_halves(keep, swap(send))
            arrived = swap(chip, "tensor")
            if layer == 1:
                done, pack_n = finish_back(1, m, chip, arrived, result[0][m][0], cotangent, pars, sums[m])
            else:
                done, pack_n = finish_back(0, m, chip, arrived, hidden, grads[1][m][0], pars, None)
            grads[layer][m] = (done, swap(done))
            lefts.append(rounded_t.reshape(4, 4, 96, T))
            outs_t.append(scaled_t.reshape(2, 4, 96, T))
            d_gates.append((d_gate, None))
            d_tails.append((d_tail, None))
            small_parts += [pack, pack_n]
        if layer == 1:
            rights = [(cotangent, part((1, T, D), (m, 0, 0))) for m in micros]
        else:
            rights = [(a, None) for a in a_all]
            lower_a = a_all
        out_parts[layer] = out_rest(scatter("y", outs_t, rights, slice(0, D), f"grad_out_{layer}"))
        gate = scatter("z", lefts, d_gates, slice(0, Q), f"grad_gate_{layer}")
        tail_z = scatter("z", lefts, d_tails, slice(0, NZ), f"grad_tail_z_{layer}")
        tail_y = scatter("y", lefts, d_tails, slice(NZ, TAIL), f"grad_tail_y_{layer}")
        done = scatter_rest([("y", gate), ("y", tail_z), ("z", tail_y)], f"cut_{layer}")
        main_parts[layer] = jnp.concatenate(done, axis=1)
        packs[layer] = (small_parts[0] + small_parts[2]) + (small_parts[1] + small_parts[3])

    first = p == 0
    own_main = jnp.where(first, main_parts[0], main_parts[1])
    got_main = swap(jnp.where(first, main_parts[1], main_parts[0]))
    lower_main = jnp.where(first, own_main, got_main)
    upper_main = jnp.where(first, got_main, own_main)
    grad_main = jnp.stack(
        [
            jnp.concatenate([lower_main[:, :Q], upper_main[:, :Q]], axis=1),
            jnp.concatenate([lower_main[:, Q : 2 * Q], upper_main[:, Q : 2 * Q]], axis=1),
        ],
        axis=1,
    )
    state_part = own_main[:, 2 * Q : 2 * Q + 256] + got_main[:, 2 * Q : 2 * Q + 256]
    grad_state = state_part + swap(state_part, "tensor")
    at = 2 * Q + 256
    grad_step = jnp.concatenate([lower_main[:, at : at + HQ], upper_main[:, at : at + HQ]], axis=1)

    own_out = jnp.where(first, out_parts[0], out_parts[1])
    got_out = swap(jnp.where(first, out_parts[1], out_parts[0]))
    z = lax.axis_index("dp") // 8
    grad_out = jnp.where(z // 2 == p, own_out, got_out)

    own_pack = jnp.where(first, packs[0], packs[1])
    got_pack = swap(jnp.where(first, packs[1], packs[0]))
    joint = jnp.stack([jnp.where(first, own_pack, got_pack), jnp.where(first, got_pack, own_pack)])
    for axis in ("z", "y"):
        one, two, three = (shift(joint, axis, k) for k in (1, 2, 3))
        joint = (joint + two) + (one + three)
    joint = joint + shift(joint, "x", 1)
    both = joint[0] + joint[1]
    taps_state = both[8:13, :256]
    taps_state = taps_state + swap(taps_state, "tensor")
    joined = lambda row, count=1: jnp.concatenate([joint[0, row : row + count], joint[1, row : row + count]], axis=1)
    heads = lambda at: jnp.concatenate([joint[0, 7:8, at : at + HQ], joint[1, 7:8, at : at + HQ]], axis=1)
    grad_norm = jnp.concatenate([both[13:14], both[14:15]], axis=1)
    grad_skip = jnp.sum(joined(6).reshape(1, 2 * HQ, 64), axis=2)

    def assemble(name, lower, upper):
        def body(l0, l1, uo0, uo1, ur0, ur1, out):
            assemble_kernel((l0, l1), (uo0, uo1), (ur0, ur1), out)

        arrays = list(lower) + [u[0] for u in upper] + [u[1] for u in upper]
        return kernel_call(body, [(a, None) for a in arrays], [((2, T, D), BF16)], (), 0, name, 24)[0]

    def assemble_grads(lower, upper):
        def body(lo0, lo1, lr0, lr1, u0, u1, out):
            q = lax.axis_index("pipe")
            for m, (lo, lr, u) in enumerate(((lo0, lr0, u0), (lo1, lr1, u1))):
                @pl.when(q == 0)
                def _():
                    join(q, lo, lr, out.at[m], slice(0, D))

                @pl.when(q == 1)
                def _():
                    out[m] = u[...]

        arrays = [l[0] for l in lower] + [l[1] for l in lower] + list(upper)
        return kernel_call(body, [(a, None) for a in arrays], [((2, T, D), BF16)], (), 0, "input_grads", 24)[0]

    lower_x = [kept[1][m][6] for m in micros]
    states = assemble("hidden_states", lower_x, result[1])
    input_grads = assemble_grads(grads[0], lower_a)
    return (
        states.reshape(1, 2, 1, T, D),
        input_grads.reshape(1, 2, 1, T, D),
        grad_norm,
        grad_main[None],
        grad_state[None],
        grad_step[None],
        joined(0, 5)[None],
        taps_state[None],
        heads(0),
        heads(128),
        grad_skip,
        joined(5),
        grad_out[None],
    )


def solution(mesh):
    in_specs = (
        P(None, "dp", None, None),
        P(None, "dp", None),
        P(None, "dp", None, None),
        P("pipe", None),
        P("pipe", None, None, "tensor"),
        P("pipe", None, None),
        P("pipe", None, "tensor"),
        P("pipe", None, "tensor"),
        P("pipe", None, None),
        P("pipe", "tensor"),
        P("pipe", "tensor"),
        P("pipe", "tensor"),
        P("pipe", "tensor"),
        P("pipe", "tensor", None),
    )
    out_specs = (
        P("pipe", None, "dp", None, None),
        P("pipe", None, "dp", None, None),
        P("pipe", None),
        P("pipe", "dp", None, "tensor"),
        P("pipe", "dp", None),
        P("pipe", "dp", "tensor"),
        P("pipe", None, "tensor"),
        P("pipe", None, None),
        P("pipe", "tensor"),
        P("pipe", "tensor"),
        P("pipe", "tensor"),
        P("pipe", "tensor"),
        P("pipe", ("tensor", "dp"), None),
    )
    return jax.shard_map(local, mesh=mesh, in_specs=in_specs, out_specs=out_specs, check_vma=False)
```

```python
import jax
import jax.numpy as jnp
from jax import lax
from jax.experimental import pallas as pl
from jax.experimental.pallas import tpu as pltpu
from jax.sharding import PartitionSpec as P

F32 = jnp.float32
BF16 = jnp.bfloat16
EPS = 1e-05
D = 1536
Q = 768
HQ = 12
DI = 3072
T = 256
HALF = 128
EXT = D + 128
NEG = -1e30


def dot(a, b):
    return lax.dot_general(a, b, (((1,), (0,)), ((), ())), preferred_element_type=F32)


def dot_nt(a, b):
    return lax.dot_general(a, b, (((1,), (1,)), ((), ())), preferred_element_type=F32)


def sigmoid(v):
    return 0.5 * jnp.tanh(0.5 * v) + 0.5


def softplus(v):
    e = jnp.exp(-jnp.abs(v))
    small = e * (1.0 - e * (0.5 - e * (1.0 / 3.0 - e * 0.25)))
    return jnp.maximum(v, 0.0) + jnp.where(e < 0.01, small, jnp.log(1.0 + e))


def iota(shape, dim):
    return lax.broadcasted_iota(jnp.int32, shape, dim)


def pieces(v):
    high = v.astype(BF16).astype(F32)
    mid = (v - high).astype(BF16).astype(F32)
    return high, mid, (v - high - mid).astype(BF16).astype(F32)


def lanes_of(v, first):
    lane = iota((v.shape[0], 128), 1)
    out = jnp.zeros((v.shape[0], 128), F32)
    for k, part in enumerate(pieces(v)):
        out = out + jnp.where(lane == first + k, part, 0.0)
    return out


def scalar_at(ext, first, count=3):
    lane = iota(ext.shape, 1)
    keep = (lane >= first) & (lane < first + count)
    return jnp.sum(jnp.where(keep, ext, 0.0), axis=1, keepdims=True)


def half_rows(which):
    return pl.ds(pl.multiple_of(which * HALF, HALF), HALF)


def whole(shape):
    return pl.BlockSpec(shape, lambda i: (0,) * len(shape))


def part(shape, at):
    return pl.BlockSpec(shape, lambda i: at)


ANY = pl.BlockSpec(memory_space=pl.ANY)


ORDER = []


def kernel_call(body, ins, outs, scratch=(), name=None, limit=22, after=()):
    after = tuple(ORDER) + tuple(after)
    if after:
        inner, count, skip = body, len(ins), len(after)
        body = lambda *refs: inner(*refs[:count], *refs[count + skip :])
        ins = list(ins) + [(a, ANY) for a in after]
    arrays = [a for a, _ in ins]
    specs = [whole(a.shape) if s is None else s for a, s in ins]
    results = pl.pallas_call(
        body,
        grid=(1,),
        in_specs=specs,
        out_specs=[whole(s) for s, _ in outs],
        out_shape=[jax.ShapeDtypeStruct(s, d) for s, d in outs],
        scratch_shapes=list(scratch),
        compiler_params=pltpu.CompilerParams(vmem_limit_bytes=limit * 1024 * 1024),
        cost_estimate=pl.CostEstimate(flops=10**10, bytes_accessed=1 << 10, transcendentals=0),
        name=name,
    )(*arrays)
    ORDER[:] = [min(results, key=lambda r: r.size * r.dtype.itemsize)]
    return results


def meanwhile(*arrays):
    ORDER.extend(arrays)


def start_either(mine, own, other, dst, sem):
    @pl.when(mine)
    def _():
        pltpu.make_async_copy(own, dst, sem).start()

    @pl.when(jnp.logical_not(mine))
    def _():
        pltpu.make_async_copy(other, dst, sem).start()


def wait_for(src, dst, sem):
    pltpu.make_async_copy(src, dst, sem).wait()


def pick(mine, own, other, dst):
    @pl.when(mine)
    def _():
        dst[...] = own[...]

    @pl.when(jnp.logical_not(mine))
    def _():
        dst[...] = other[...]


def join(p, own, other, dst, columns=slice(None)):
    dst[half_rows(p), :] = own[:, columns].astype(dst.dtype)
    dst[half_rows(1 - p), :] = other[:, columns].astype(dst.dtype)


TAPS, GATE, NORM, STAPS, SKIP, HEAD = 0, 5, 6, 8, 13, 16


def pack_kernel(ng, cm, cs, sb, dl, ss, gg, wd, own, other, wd_own, wd_other):
    p = lax.axis_index("pipe")
    for target, wd_target, which in ((own, wd_own, p), (other, wd_other, 1 - p)):
        lanes = pl.ds(pl.multiple_of(which * Q, Q), Q)
        target[...] = jnp.zeros(target.shape, F32)
        target[TAPS : TAPS + 5, :] = cm[:, lanes]
        target[GATE : GATE + 1, :] = gg[:, lanes]
        target[NORM : NORM + 1, :] = ng[:, :Q]
        target[NORM + 1 : NORM + 2, :] = ng[:, Q:]
        target[STAPS : STAPS + 5, :256] = cs[...]
        second = which == 1
        head = [jnp.where(second, v[:, HQ : 2 * HQ], v[:, :HQ]) for v in (sb, dl, ss)]
        row = jnp.concatenate([head[2], jnp.zeros((1, 128 - HQ), F32)], axis=1)
        column = jnp.broadcast_to(row, (128, 128)).T
        owner = iota((16, Q), 1) // 64 == iota((16, Q), 0)
        spread = jnp.where(owner, column[:16, :1], 0.0)
        target[SKIP : SKIP + 1, :] = jnp.sum(spread, axis=0, keepdims=True)
        rows = [jnp.concatenate([v, jnp.zeros((1, 128 - HQ), F32)], axis=1) for v in head[:2]]
        square = jnp.concatenate([rows[0], -jnp.exp(rows[1]), jnp.zeros((126, 128), F32)], axis=0)
        target[HEAD : HEAD + 16, :128] = square.T[:16, :]
        wide = wd[...].astype(F32)
        chosen = jnp.where(second, wide[HQ:, :], wide[:HQ, :])
        wd_target[...] = jnp.concatenate([chosen, jnp.zeros((4, D), F32)], axis=0).astype(BF16)


def project_body(layer, p, x, par, wd, ws, w_scr, waits, outs):
    rounded, pre, spre, raw = outs
    factor = lax.rsqrt(jnp.mean(x * x, axis=1, keepdims=True) + EPS)
    scaled = x * factor
    for c in range(2):
        cols = slice(c * Q, (c + 1) * Q)
        normed = scaled[:, cols] * par[NORM + c : NORM + c + 1, :]
        rounded[:, cols] = normed.astype(BF16)
    raw[...] = dot_nt(wd[...], rounded[...])
    waits[0]()
    spre[...] = dot(rounded[...], ws[...])
    waits[1]()
    for u in range(2):
        for c in range(3):
            cols = slice(c * 256, (c + 1) * 256)
            pre[:, u * Q + c * 256 : u * Q + (c + 1) * 256] = dot(rounded[...], w_scr[u, :, cols])


def project(layer, m, xs, pars, wds, wss, ws_main):
    first = layer == 0

    def body(*refs):
        xr = refs[: 1 if first else 2]
        par_o, par_r, wd_o, wd_r, ws_o, ws_r, wm_o, wm_r = refs[len(xr) : len(xr) + 8]
        rest = refs[len(xr) + 8 :]
        outs, scr = rest[: 4 if first else 5], rest[4 if first else 5 :]
        par, wd, ws, w_scr, sem = scr
        p = lax.axis_index("pipe")
        mine = p == layer
        own_main = wm_o.at[:, :, pl.ds(pl.multiple_of(p * Q, Q), Q)]
        start_either(mine, ws_o, ws_r, ws, sem.at[0])
        start_either(mine, own_main, wm_r, w_scr, sem.at[1])
        pick(mine, par_o, par_r, par)
        pick(mine, wd_o, wd_r, wd)
        if first:
            x = xr[0][0].astype(F32)
        else:
            join(p, xr[0], xr[1], outs[4], slice(0, D))
            x = outs[4][...].astype(F32)
        waits = (
            lambda: wait_for(ws_r, ws, sem.at[0]),
            lambda: wait_for(wm_r, w_scr, sem.at[1]),
        )
        project_body(layer, p, x, par, wd, ws, w_scr, waits, outs[:4])

    if first:
        ins = [(xs, part((1, T, D), (m, 0, 0)))]
    else:
        ins = [(xs[0], None), (xs[1], None)]
    ins += [(a, None) for a in pars] + [(a, None) for a in wds]
    ins += [(a, ANY) for a in wss] + [(a, ANY) for a in ws_main]
    outs = [((T, D), BF16), ((T, D), F32), ((T, T), F32), ((16, T), F32)]
    if not first:
        outs.append(((T, D), BF16))
    scratch = [
        pltpu.VMEM((32, Q), F32),
        pltpu.VMEM((16, D), BF16),
        pltpu.VMEM((D, 256), BF16),
        pltpu.VMEM((2, D, Q), BF16),
        pltpu.SemaphoreType.DMA((2,)),
    ]
    return kernel_call(body, ins, outs, scratch, f"project_{layer}_{m}")


def turn(layer, m, rounded):
    def body(rounded, out):
        for c in range(6):
            cols = slice(c * 256, (c + 1) * 256)
            out[cols, :] = rounded[:, cols].T

    return kernel_call(body, [(rounded, None)], [((D, T), BF16)], (), f"turn_{layer}_{m}", 16)[0]


def document_ids(seg_ref):
    row = jnp.broadcast_to(seg_ref[0].astype(F32), (T, T))
    return row.T, row


def same_document(by_token, lag):
    position = iota((T, T), 0)
    earlier = pltpu.roll(by_token, lag, 0)
    return jnp.where((earlier == by_token) & (position >= lag), 1.0, 0.0)


def convolve(values, taps, same):
    out = taps[4:5] + taps[3:4] * values
    for lag in range(1, 4):
        out = out + taps[3 - lag : 4 - lag] * (pltpu.roll(values, lag, 0) * same[lag])
    return out


def convolve_back(d_sum, values, taps, same):
    d_values = taps[3:4] * d_sum
    rows = [None] * 5
    rows[4] = jnp.sum(d_sum, axis=0, keepdims=True)
    rows[3] = jnp.sum(d_sum * values, axis=0, keepdims=True)
    for lag in range(1, 4):
        held = d_sum * same[lag]
        d_values = d_values + taps[3 - lag : 4 - lag] * pltpu.roll(held, T - lag, 0)
        moved = pltpu.roll(values, lag, 0)
        rows[3 - lag] = jnp.sum(held * moved, axis=0, keepdims=True)
    return d_values, jnp.concatenate(rows, axis=0)


def step_sizes(raw, par):
    before = raw[...] + par[HEAD : HEAD + 16, 0:1]
    step = softplus(before)
    total = step * par[HEAD : HEAD + 16, 1:2]
    lane = iota(total.shape, 1)
    shift = 1
    while shift < T:
        total = total + jnp.where(lane >= shift, pltpu.roll(total, shift, 1), 0.0)
        shift *= 2
    return before, step, total


def columns_of(rows):
    return jnp.concatenate([rows, jnp.zeros((112, T), F32)], axis=0).T


def mix(layer, m, pre, spre, raw, seg, pars, wos):
    def body(pre, spre, raw, seg, par_o, par_r, wo_o, wo_r, *rest):
        mixed, inner_out, send, keep, par, wo, gs, u_scr, sem = rest
        p, t = lax.axis_index("pipe"), lax.axis_index("tensor")
        mine = p == layer
        own = wo_o.at[pl.ds(pl.multiple_of(p * Q, Q), Q), :]
        start_either(mine, own, wo_r, wo, sem)
        pick(mine, par_o, par_r, par)
        by_token, by_row = document_ids(seg)
        same = [None] + [same_document(by_token, lag) for lag in range(1, 4)]
        allowed = (by_token == by_row) & (iota((T, T), 0) >= iota((T, T), 1))
        state = convolve(spre[...], par[STAPS : STAPS + 5, :256], same)
        state = (state * sigmoid(state)).astype(BF16)
        crossed = dot_nt(state[:, 128:], state[:, :128])
        _, step, total = step_sizes(raw, par)
        total_t = columns_of(total)
        low = iota((T, 128), 1) < 64
        squares = jnp.zeros((T, 1), F32)
        for g in range(3):
            cols = slice(g * 256, (g + 1) * 256)
            summed = convolve(pre[:, Q + g * 256 : Q + (g + 1) * 256], par[TAPS : TAPS + 5, cols], same)
            inner = (summed * sigmoid(summed)).astype(BF16)
            inner_out[:, cols] = inner
            for pair in range(2):
                at = slice(g * 256 + pair * 128, g * 256 + (pair + 1) * 128)
                values = inner[:, pair * 128 : (pair + 1) * 128]
                out = None
                for k in range(2):
                    h = g * 4 + pair * 2 + k
                    gap = total_t[:, h : h + 1] - total[h : h + 1, :]
                    decay = jnp.exp(jnp.where(allowed, gap, NEG))
                    mixing = (crossed * decay * step[h : h + 1, :]).astype(BF16)
                    chosen = jnp.where(low if k == 0 else ~low, values, jnp.zeros_like(values))
                    term = dot(mixing, chosen)
                    out = term if out is None else out + term
                mixed[:, at] = out
            combined = mixed[:, cols] + par[SKIP : SKIP + 1, cols] * inner.astype(F32)
            gate = pre[:, cols]
            gated = combined * (gate * sigmoid(gate))
            squares = squares + jnp.sum(gated * gated, axis=1, keepdims=True)
            gs[:, cols] = (gated * par[GATE : GATE + 1, cols]).astype(BF16)
        wait_for(wo_r, wo, sem)
        for c in range(3):
            cols = slice(c * 512, (c + 1) * 512)
            u_scr[:, cols] = dot(gs[...], wo[:, cols]).astype(BF16)
        u_scr[:, D:] = lanes_of(squares, 3 * (2 * p + t)).astype(BF16)
        send[...] = u_scr[half_rows(1 - p), :]
        keep[...] = u_scr[half_rows(p), :]

    ins = [(pre, None), (spre, None), (raw, None), (seg, part((1, 1, T), (m, 0, 0)))]
    ins += [(a, None) for a in pars] + [(a, ANY) for a in wos]
    outs = [((T, Q), F32), ((T, Q), BF16), ((HALF, EXT), BF16), ((HALF, EXT), BF16)]
    scratch = [
        pltpu.VMEM((32, Q), F32),
        pltpu.VMEM((Q, D), BF16),
        pltpu.VMEM((T, Q), BF16),
        pltpu.VMEM((T, EXT), BF16),
        pltpu.SemaphoreType.DMA,
    ]
    return kernel_call(body, ins, outs, scratch, f"mix_{layer}_{m}")


def finish_forward(layer, m, chip, arrived, x, cot):
    def body(chip, arrived, x, *rest):
        p = lax.axis_index("pipe")
        out = rest[-1]
        total = chip[:, :D].astype(F32) + arrived[:, :D].astype(F32)
        ext = chip[:, D:].astype(F32) + arrived[:, D:].astype(F32)
        factor = lax.rsqrt(jnp.sum(ext, axis=1, keepdims=True) / DI + EPS)
        if layer == 0:
            before = x[0, half_rows(p), :].astype(F32)
        else:
            before = x[:, :D].astype(F32)
        out[:, :D] = (before + factor * total).astype(BF16)
        tail = lanes_of(factor, 0)
        if layer == 1:
            a = rest[0][0, half_rows(p), :].astype(F32)
            pull = factor * factor * factor * (jnp.sum(a * total, axis=1, keepdims=True) / DI)
            tail = tail + lanes_of(pull, 3)
        out[:, D:] = tail.astype(BF16)

    ins = [(chip, None), (arrived, None)]
    if layer == 0:
        ins += [(x, part((1, T, D), (m, 0, 0)))]
    else:
        ins += [(x, None), (cot, part((1, T, D), (m, 0, 0)))]
    return kernel_call(body, ins, [((HALF, EXT), BF16)], (), f"finish_out_{layer}_{m}", 16)[0]


def gate_back(layer, m, a, scalars, pre, mixed, inner, pars, wos):
    lower = layer == 0

    def body(*refs):
        if lower:
            a_o, a_r, s_o, s_r = refs[:4]
            refs = refs[4:]
        else:
            a_f, s_o, s_r = refs[:3]
            refs = refs[3:]
        pre, mixed, inner, par_o, par_r, wo_o, wo_r = refs[:7]
        d_gate, d_comb, scaled_t, cross, pack = refs[7:12]
        refs = refs[12:]
        if lower:
            a_all = refs[0]
            refs = refs[1:]
        par, wo, ext, ext2, sem = refs
        p = lax.axis_index("pipe")
        mine = p == layer
        own = wo_o.at[pl.ds(pl.multiple_of(p * Q, Q), Q), :]
        start_either(mine, own, wo_r, wo, sem)
        pick(mine, par_o, par_r, par)
        join(p, s_o, s_r, ext)
        factor = scalar_at(ext[...], 0)
        if lower:
            join(p, a_o, a_r, a_all, slice(0, D))
            join(p, a_o, a_r, ext2, slice(D, EXT))
            pull = scalar_at(ext2[...], 3)
            a = a_all[...]
        else:
            pull = scalar_at(ext[...], 3)
            a = a_f[0]
        wait_for(wo_r, wo, sem)
        pack[...] = jnp.zeros(pack.shape, F32)
        for g in range(3):
            cols = slice(g * 256, (g + 1) * 256)
            d_scaled = dot_nt(a, wo[cols, :])
            values = inner[:, cols].astype(F32)
            combined = mixed[:, cols] + par[SKIP : SKIP + 1, cols] * values
            gate = pre[:, cols]
            opened = sigmoid(gate)
            silu = gate * opened
            gated = combined * silu
            normed = gated * factor
            gain = par[GATE : GATE + 1, cols]
            scaled = (normed * gain).T.astype(BF16)
            scaled_t[cols, :] = scaled
            pack[0:1, cols] = jnp.sum(d_scaled * normed, axis=0, keepdims=True)
            d_gated = d_scaled * gain * factor - gated * pull
            d_combined = d_gated * silu
            d_comb[:, cols] = d_combined
            pack[1:2, cols] = jnp.sum(d_combined * values, axis=0, keepdims=True)
            d_open = d_gated * combined * (opened * (1.0 + gate * (1.0 - opened)))
            d_gate[:, cols] = d_open.astype(BF16)
            cross[cols, :] = jnp.where(p == 0, scaled, d_open.T.astype(BF16))

    last = part((HALF, 128), (0, D // 128))
    if lower:
        ins = [(a[0], None), (a[1], None)]
    else:
        ins = [(a, part((1, T, D), (m, 0, 0)))]
    ins += [(s, last) for s in scalars]
    ins += [(pre, part((T, Q), (0, 0))), (mixed, None), (inner, None)]
    ins += [(v, None) for v in pars] + [(v, ANY) for v in wos]
    outs = [((T, Q), BF16), ((T, Q), F32), ((Q, T), BF16), ((Q, T), BF16), ((8, Q), F32)]
    if lower:
        outs.append(((T, D), BF16))
    scratch = [
        pltpu.VMEM((32, Q), F32),
        pltpu.VMEM((Q, D), BF16),
        pltpu.VMEM((T, 128), F32),
        pltpu.VMEM((T, 128), F32),
        pltpu.SemaphoreType.DMA,
    ]
    return kernel_call(body, ins, outs, scratch, f"gate_back_{layer}_{m}")


def per_head(values):
    high = values.astype(BF16)
    rest = (values - high.astype(F32)).astype(BF16)
    owner = (iota((Q, 128), 0) // 64 == iota((Q, 128), 1)).astype(BF16)
    return dot(high, owner) + dot(rest, owner)


def mix_back(layer, m, d_comb, inner, pre, spre, raw, seg, mixed, pack_a, pars):
    def body(d_comb, inner, pre, spre, raw, seg, mixed, pack_a, par_o, par_r, *rest):
        d_tail, d_small, d_raw_out, pack, par, gap_prod, col_prod = rest
        p = lax.axis_index("pipe")
        mine = p == layer
        pick(mine, par_o, par_r, par)
        by_token, by_row = document_ids(seg)
        same = [None] + [same_document(by_token, lag) for lag in range(1, 4)]
        allowed = (by_token == by_row) & (iota((T, T), 1) >= iota((T, T), 0))
        summed_s = convolve(spre[...], par[STAPS : STAPS + 5, :256], same)
        opened_s = sigmoid(summed_s)
        state = (summed_s * opened_s).astype(BF16)
        keys, query = state[:, :128], state[:, 128:]
        crossed = dot_nt(keys, query)
        before, step, total = step_sizes(raw, par)
        total_t, step_t = columns_of(total), columns_of(step)
        low = iota((T, 128), 1) < 64
        d_cross = jnp.zeros((T, T), F32)
        pack[...] = jnp.zeros(pack.shape, F32)
        for g in range(3):
            cols = slice(g * 256, (g + 1) * 256)
            heads = []
            for pair in range(2):
                at = slice(g * 256 + pair * 128, g * 256 + (pair + 1) * 128)
                values = inner[:, at]
                d_mixed = d_comb[:, at].astype(BF16)
                d_heads = None
                for k in range(2):
                    h = g * 4 + pair * 2 + k
                    side = low if k == 0 else ~low
                    gap = total[h : h + 1, :] - total_t[:, h : h + 1]
                    decay = jnp.exp(jnp.where(allowed, gap, NEG)) * step_t[:, h : h + 1]
                    mixing = (crossed * decay).astype(BF16)
                    chosen = jnp.where(side, d_mixed, jnp.zeros_like(d_mixed))
                    d_mixing = dot_nt(values, chosen)
                    d_cross = d_cross + d_mixing * decay
                    term = dot(mixing, chosen)
                    d_heads = term if d_heads is None else d_heads + term
                heads.append(d_heads)
                along = values.astype(F32) * d_heads
                col_prod[:, at] = along
                gap_prod[:, at] = d_mixed.astype(F32) * mixed[:, at] - along
            taps = par[TAPS : TAPS + 5, cols]
            values = pre[:, cols]
            summed = convolve(values, taps, same)
            opened = sigmoid(summed)
            d_inner = jnp.concatenate(heads, axis=1) + par[SKIP : SKIP + 1, cols] * d_comb[:, cols]
            d_sum = d_inner * (opened * (1.0 + summed * (1.0 - opened)))
            d_values, rows = convolve_back(d_sum, values, taps, same)
            d_tail[:, cols] = d_values.astype(BF16)
            pack[0:5, cols] = rows
        pack[5:7, :] = pack_a[0:2, :]
        crossed_b = d_cross.astype(BF16)
        d_keys = dot(crossed_b, query)
        d_query = dot(d_cross.T.astype(BF16), keys)
        d_state = jnp.concatenate([d_keys, d_query], axis=1)
        d_sum = d_state * (opened_s * (1.0 + summed_s * (1.0 - opened_s)))
        d_values, rows = convolve_back(d_sum, spre[...], par[STAPS : STAPS + 5, :256], same)
        d_small[:, :256] = d_values.astype(BF16)
        pack[8:13, :256] = rows
        d_gap = per_head(gap_prod[...]).T[:16, :]
        d_col = per_head(col_prod[...]).T[:16, :]
        lane = iota(d_gap.shape, 1)
        shift = 1
        while shift < T:
            d_gap = d_gap + jnp.where(lane < T - shift, pltpu.roll(d_gap, T - shift, 1), 0.0)
            shift *= 2
        rate = par[HEAD : HEAD + 16, 1:2]
        slope = sigmoid_small(before)
        ratio = jnp.where(step > 1e-30, slope / jnp.maximum(step, 1e-30), 1.0)
        d_raw = d_col * ratio + d_gap * rate * slope
        valid = iota((16, T), 0) < HQ
        d_raw = jnp.where(valid, d_raw, 0.0)
        d_log = jnp.where(valid, d_gap * step * rate, 0.0)
        raw_t = columns_of(d_raw)
        d_raw_out[...] = raw_t.astype(BF16)
        d_small[:, 256:] = jnp.where(p == 1, pltpu.roll(raw_t, HQ, 1), raw_t).astype(BF16)
        bias_row = jnp.broadcast_to(jnp.sum(d_raw, axis=1, keepdims=True), (16, 128))
        log_row = jnp.broadcast_to(jnp.sum(d_log, axis=1, keepdims=True), (16, 128))
        square = jnp.concatenate([bias_row, jnp.zeros((112, 128), F32)], axis=0).T
        pack[7:8, 0:128] = square[0:1, :]
        square = jnp.concatenate([log_row, jnp.zeros((112, 128), F32)], axis=0).T
        pack[7:8, 128:256] = square[0:1, :]

    ins = [(d_comb, None), (inner, None), (pre, part((T, Q), (0, 1))), (spre, None), (raw, None)]
    ins += [(seg, part((1, 1, T), (m, 0, 0))), (mixed, None), (pack_a, None)]
    ins += [(v, None) for v in pars]
    outs = [((T, Q), BF16), ((T, 384), BF16), ((T, 128), BF16), ((16, Q), F32)]
    scratch = [pltpu.VMEM((32, Q), F32), pltpu.VMEM((T, Q), F32), pltpu.VMEM((T, Q), F32)]
    return kernel_call(body, ins, outs, scratch, f"mix_back_{layer}_{m}")


def sigmoid_small(v):
    e = jnp.exp(-jnp.abs(v))
    return jnp.where(v >= 0.0, 1.0, e) / (1.0 + e)


def project_back(layer, m, d_gate, d_inner, d_small, d_raw, wds, wss, ws_main):
    def body(d_gate, d_inner, d_small, d_raw, wd_o, wd_r, ws_o, ws_r, wm_o, wm_r, send, keep, wd, ws, w_scr, acc, sem):
        p = lax.axis_index("pipe")
        mine = p == layer
        own_main = wm_o.at[:, :, pl.ds(pl.multiple_of(p * Q, Q), Q)]
        start_either(mine, own_main, wm_r, w_scr, sem.at[1])
        start_either(mine, ws_o, ws_r, ws, sem.at[0])
        pick(mine, wd_o, wd_r, wd)
        wait_for(ws_r, ws, sem.at[0])
        wait_for(wm_r, w_scr, sem.at[1])
        for c in range(6):
            rows = slice(c * 256, (c + 1) * 256)
            out = dot_nt(d_gate[...], w_scr[0, rows, :])
            out = out + dot_nt(d_inner[...], w_scr[1, rows, :])
            out = out + dot_nt(d_small[:, :256], ws[rows, :])
            out = out + dot(d_raw[:, :16], wd[:, rows])
            acc[:, rows] = out.astype(BF16)
        send[...] = acc[half_rows(1 - p), :]
        keep[...] = acc[half_rows(p), :]

    ins = [(d_gate, None), (d_inner, None), (d_small, None), (d_raw, None)] + [(a, None) for a in wds]
    ins += [(a, ANY) for a in wss] + [(a, ANY) for a in ws_main]
    outs = [((HALF, D), BF16), ((HALF, D), BF16)]
    scratch = [
        pltpu.VMEM((16, D), BF16),
        pltpu.VMEM((D, 256), BF16),
        pltpu.VMEM((2, D, Q), BF16),
        pltpu.VMEM((T, D), BF16),
        pltpu.SemaphoreType.DMA((2,)),
    ]
    return kernel_call(body, ins, outs, scratch, f"project_back_{layer}_{m}")


def finish_back(layer, m, chip, arrived, x, a, pars, below):
    def body(*refs):
        chip, arrived, x, a, par_o, par_r = refs[:6]
        refs = refs[6:]
        if layer == 1:
            u_o, u_r, y = refs[:3]
            refs = refs[3:]
        out, pack, par = refs
        p = lax.axis_index("pipe")
        mine = p == layer
        pick(mine, par_o, par_r, par)
        d_rounded = chip[...].astype(F32) + arrived[...].astype(F32)
        if layer == 0:
            xv = x[0, half_rows(p), :].astype(F32)
            av = a[:, :D].astype(F32)
        else:
            xv = x[:, :D].astype(F32)
            av = a[0, half_rows(p), :].astype(F32)
        factor = lax.rsqrt(jnp.mean(xv * xv, axis=1, keepdims=True) + EPS)
        normed = xv * factor
        gain = jnp.concatenate([par[NORM : NORM + 1, :], par[NORM + 1 : NORM + 2, :]], axis=1)
        pulled = d_rounded * gain
        mean = jnp.mean(pulled * normed, axis=1, keepdims=True)
        result = (av + factor * (pulled - normed * mean)).astype(BF16)
        out[:, :D] = result
        pack[...] = jnp.zeros(pack.shape, F32)
        d_gain = jnp.sum(d_rounded * normed, axis=0, keepdims=True)
        pack[13:14, :] = d_gain[:, :Q]
        pack[14:15, :] = d_gain[:, Q:]
        if layer == 1:
            branch = u_o[...].astype(F32) + u_r[...].astype(F32)
            gated = scalar_at(y[...].astype(F32), 0)
            total = jnp.sum(result.astype(F32) * branch, axis=1, keepdims=True)
            out[:, D:] = lanes_of(gated * gated * gated * (total / DI), 3).astype(BF16)
        else:
            out[:, D:] = jnp.zeros((HALF, 128), BF16)

    ins = [(chip, None), (arrived, None)]
    if layer == 0:
        ins += [(x, part((1, T, D), (m, 0, 0))), (a, None)]
    else:
        ins += [(x, None), (a, part((1, T, D), (m, 0, 0)))]
    ins += [(v, None) for v in pars]
    if layer == 1:
        narrow = part((HALF, D), (0, 0))
        ins += [(below[0], narrow), (below[1], narrow), (x, part((HALF, 128), (0, D // 128)))]
    outs = [((HALF, EXT), BF16), ((16, Q), F32)]
    return kernel_call(body, ins, outs, [pltpu.VMEM((32, Q), F32)], f"finish_back_{layer}_{m}", 16)


def position():
    dp = lax.axis_index("dp")
    return dp // 8, (dp // 2) % 4, dp % 2


UNIT = 384
BLOCK = 256
WIDE = 2 * D - 512
BACK = WIDE // 2


def weight_stage(stage, layer, left, grads, arrived):
    ins = [(v, None) for v in left]
    for group in grads:
        ins += [(v, None) for v in group["near"]] + [(v, ANY) for v in group["far"]]
    count = len(ins)

    def body(*refs):
        lefts, per, rest = refs[:2], (refs[2:9], refs[9:16]), refs[count:]
        rest, (gate_s, wide_s, cot_s, sem) = rest[:-4], rest[-4:]
        p = lax.axis_index("pipe")
        z, y, x = position()

        def copies(core):
            out = []
            for m in range(2):
                gate, wide, cot = per[m][4:]
                if core == 0:
                    out.append(pltpu.make_async_copy(gate, gate_s.at[m], sem.at[m]))
                else:
                    cot = cot.at[m] if layer == 1 else cot
                    out.append(pltpu.make_async_copy(wide, wide_s.at[m], sem.at[m]))
                    out.append(pltpu.make_async_copy(cot, cot_s.at[m], sem.at[2 + m]))
            return out

        def products(core, offset):
            inner = [per[m][0] for m in range(2)]
            cross = [per[m][1] for m in range(2)]
            cols = slice(0, 256) if core == 0 else slice(256, 384)
            small = [add_halves(per[m][2][:, cols], per[m][3][:, cols]) for m in range(2)]
            if core == 0:
                rows = [v[lax.rem(z + offset, 4)].reshape(UNIT, T) for v in lefts]
                yield 0, [dot(rows[m], gate_s[m]) for m in range(2)]
                yield Q, [dot_nt(rows[m], cross[m][...].reshape(Q, T)) for m in range(2)]
                yield 2 * Q, [dot(rows[m], inner[m][...]) for m in range(2)]
                yield 3 * Q, [dot(rows[m], small[m]) for m in range(2)]
            else:
                at = lax.rem(y + offset, 4)
                rows = [v[:, at].reshape(UNIT, T) for v in lefts]
                both = [
                    jnp.concatenate([v[:, at].reshape(UNIT // 2, T) for v in (cross[m], wide_s.at[m])], axis=0)
                    for m in range(2)
                ]
                for n in range(2):
                    yield n * Q, [dot(both[m], cot_s[m, :, n * Q : (n + 1) * Q]) for m in range(2)]
                yield 2 * Q, [dot(rows[m], inner[m][...]) for m in range(2)]
                raw = [dot(rows[m], small[m]) for m in range(2)]
                yield 3 * Q, [jnp.concatenate([v, jnp.zeros((UNIT, 128), F32)], axis=1) for v in raw]

        def blocks(core, offset):
            for start, parts in products(core, offset):
                value = parts[0] + parts[1]
                for n in range(value.shape[1] // BLOCK):
                    at = start + n * BLOCK
                    yield slice(at, at + BLOCK), value[:, n * BLOCK : (n + 1) * BLOCK]

        def shifted(cols):
            return slice(cols.start - BACK, cols.stop - BACK)

        def run(core):
            if stage == 0:
                for cols, value in blocks(core, 2):
                    if cols.start < BACK:
                        rest[0][:, cols] = value.astype(BF16)
                    else:
                        rest[1][:, shifted(cols)] = value.astype(BF16)
            elif stage == 1:
                from_before, from_after, to_after, to_before = rest
                for cols, value in blocks(core, 1):
                    if cols.start < BACK:
                        value = value + from_before[:, cols].astype(F32)
                    to_after[:, cols] = value.astype(BF16)
                for cols, value in blocks(core, 3):
                    if cols.start >= BACK:
                        value = value + from_after[:, shifted(cols)].astype(F32)
                    to_before[:, cols] = value.astype(BF16)
            else:
                from_before, from_after = rest[:2]
                outs, total = rest[2:-1], rest[-1]
                for cols, value in blocks(core, 0):
                    value = value + from_before[:, cols].astype(F32) + from_after[:, cols].astype(F32)
                    total[:, :, cols] = value.reshape(4, 96, BLOCK)
                here = y if core == 0 else z
                outs[0][...] = total[here]
                for offset in range(1, 4):
                    outs[offset][...] = total[lax.rem(here + offset, 4)].astype(BF16)

        for core in range(2):
            @pl.when(p == core)
            def _():
                moves = copies(core)
                for move in moves:
                    move.start()
                for move in moves:
                    move.wait()
                run(core)

    if stage == 0:
        outs = [((UNIT, BACK), BF16)] * 2
    elif stage == 1:
        outs = [((UNIT, WIDE), BF16)] * 2
    else:
        outs = [((96, WIDE), F32)] + [((96, WIDE), BF16)] * 3
    scratch = [pltpu.VMEM((4, 96, WIDE), F32)] if stage == 2 else []
    scratch += [
        pltpu.VMEM((2, T, Q), BF16),
        pltpu.VMEM((2, 2, 4, 96, T), BF16),
        pltpu.VMEM((2, T, D), BF16),
        pltpu.SemaphoreType.DMA((4,)),
    ]
    ins += [(a, None) for a in arrived]
    return kernel_call(body, ins, outs, scratch, f"grad_{layer}_{stage}")


def cut_rows(group, layer):
    def body(own, one, two, three, mine, other, state_mine, state_other, total):
        _, _, x = position()
        out = (own[...] + two[...].astype(F32)) + (one[...].astype(F32) + three[...].astype(F32))
        total[...] = out.reshape(2, 48, WIDE)
        mine[...] = total[x]
        other[...] = total[1 - x].astype(BF16)
        state_mine[...] = total[x, :, 3 * Q :].astype(BF16)
        state_other[...] = total[1 - x, :, 3 * Q :].astype(BF16)

    outs = [((48, WIDE), F32), ((48, WIDE), BF16), ((48, 256), BF16), ((48, 256), BF16)]
    ins = [(a, None) for a in group]
    return kernel_call(body, ins, outs, [pltpu.VMEM((2, 48, WIDE), F32)], f"grad_cut_{layer}", 24)


def dp_index(z, y, x):
    return ((z % 4) * 4 + y % 4) * 2 + x % 2


def dp_pairs(move):
    places = [(z, y, x) for z in range(4) for y in range(4) for x in range(2)]
    return [(dp_index(*at), dp_index(*move(*at))) for at in places]


def along(axis, offset):
    if axis == "z":
        return dp_pairs(lambda z, y, x: (z + offset, y, x))
    if axis == "y":
        return dp_pairs(lambda z, y, x: (z, y + offset, x))
    return dp_pairs(lambda z, y, x: (z, y, x + offset))


NEXT = {"z": lambda z, y, x: (z ^ 1, y, x), "y": lambda z, y, x: (z, y ^ 1, x)}


def shift(value, axis, offset):
    return lax.ppermute(value, "dp", along(axis, offset))


def core_shift(value, axes, offset):
    pairs = [(32 * p + a, 32 * p + b) for p in range(2) for a, b in along(axes[p], offset)]
    return lax.ppermute(value, ("pipe", "dp"), pairs)


def swap(value, axis="pipe"):
    return lax.ppermute(value, axis, [(0, 1), (1, 0)])


def add_halves(a, b):
    return (a.astype(F32) + b.astype(F32)).astype(BF16)


def scatter(layer, stage, args, arrived=()):
    sent = weight_stage(stage, layer, *args, arrived)
    if stage < 2:
        return core_shift(sent[0], "zy", 1), core_shift(sent[1], "zy", 3)
    return (sent[0],) + tuple(core_shift(sent[n], "yz", n) for n in (1, 2, 3))


def scatter_rows(layer, group):
    own, sent, state_own, state_sent = cut_rows(group, layer)
    places = [(t, d) for t in range(2) for d in range(32)]
    flat = lambda t, d: t * 32 + d
    names = ("pipe", "tensor", "dp")
    across = [(flat(t, d), flat(1 - t, d)) for t, d in places]
    corner = [(flat(t, d), flat(1 - t, d ^ 1)) for t, d in places]
    return (
        own,
        core_shift(sent, "xx", 1),
        lax.ppermute(state_own, names, across),
        lax.ppermute(state_sent, names, corner),
    )


def sum_rows(layer, own, got, across, corner):
    def body(own, got, across, corner, out):
        out[:, : 3 * Q] = own[:, : 3 * Q] + got[:, : 3 * Q].astype(F32)
        at = slice(3 * Q, WIDE)
        mine = own[:, at].astype(BF16).astype(F32) + got[:, at].astype(F32)
        out[:, at] = mine + (across[...].astype(F32) + corner[...].astype(F32))

    ins = [(own, None), (got, None), (across, None), (corner, None)]
    return kernel_call(body, ins, [((48, WIDE), F32)], (), f"grad_rows_{layer}", 16)[0]


def finish_weights(lower, upper):
    def body(own_0, got_0, own_1, got_1, main, state, step, out):
        p = lax.axis_index("pipe")
        for layer, (first, second) in enumerate(((own_0, got_0), (got_1, own_1))):
            @pl.when(p == layer)
            def _():
                main[:, 0, :] = first[:, : 2 * Q]
                main[:, 1, :Q] = first[:, 2 * Q : 3 * Q]
                main[:, 1, Q:] = second[:, 2 * Q : 3 * Q]
                state[...] = first[:, 3 * Q :]
                step[...] = second[:, 3 * Q : 3 * Q + 2 * HQ]
                out[...] = second[:, : 2 * Q]

    ins = [(a, None) for group in (lower, upper) for a in group]
    outs = [((48, 2, D), F32), ((48, 256), F32), ((48, 2 * HQ), F32), ((48, D), F32)]
    return kernel_call(body, ins, outs, (), "grad_finish", 24)


def join_sums(layer, m, keep, got):
    def body(keep, got, out):
        out[...] = add_halves(keep[...], got[...])

    return kernel_call(body, [(keep, None), (got, None)], [(keep.shape, BF16)], (), f"add_{layer}_{m}", 16)[0]


def sum_packs(packs):
    def body(*refs):
        out, rows = refs[8:]
        for layer in range(2):
            one = refs[4 * layer : 4 * layer + 4]
            out[layer] = (one[0][...] + one[1][...]) + (one[2][...] + one[3][...])
            rows[layer] = out[layer, 8:16, :256]

    ins = [(a, None) for layer in packs for a in layer]
    return kernel_call(body, ins, [((2, 16, Q), F32), ((2, 8, 256), F32)], (), "pack_sum", 16)


def add_state_rows(pack, rows):
    def body(pack, rows, out):
        out[...] = pack[...]
        for layer in range(2):
            out[layer, 8:13, :256] = pack[layer, 8:13, :256] + rows[layer, :5, :]

    return kernel_call(body, [(pack, None), (rows, None)], [((2, 16, Q), F32)], (), "pack_state", 16)[0]


def sum_four(own, arrived, name):
    def body(own, one, two, three, out):
        out[...] = (own[...] + two[...]) + (one[...] + three[...])

    return kernel_call(body, [(a, None) for a in (own, *arrived)], [((2, 16, Q), F32)], (), name, 16)[0]


def finish_packs(own, arrived):
    def body(own, arrived, norm, taps, state, bias, log, skip, gain):
        p = lax.axis_index("pipe")
        owner = (iota((Q, 128), 0) // 64 == iota((Q, 128), 1)).astype(F32)
        for core in range(2):
            @pl.when(p == core)
            def _():
                mine = own[core]
                other = arrived[core]
                pair = (mine, other) if core == 0 else (other, mine)
                both = pair[0] + pair[1]
                norm[:, :Q] = both[13:14]
                norm[:, Q:] = both[14:15]
                state[...] = both[8:13, :256]
                for n in range(2):
                    taps[:, n * Q : (n + 1) * Q] = pair[n][0:5]
                    gain[:, n * Q : (n + 1) * Q] = pair[n][5:6]
                sums = [
                    lax.dot_general(
                        pair[n][0:8],
                        owner,
                        (((1,), (0,)), ((), ())),
                        precision=lax.Precision.HIGHEST,
                        preferred_element_type=F32,
                    )
                    for n in range(2)
                ]
                skip[...] = jnp.concatenate([sums[0][6:7, :HQ], sums[1][6:7, :HQ]], axis=1)
                bias[...] = jnp.concatenate([pair[0][7:8, :HQ], pair[1][7:8, :HQ]], axis=1)
                log[...] = jnp.concatenate([pair[0][7:8, 128 : 128 + HQ], pair[1][7:8, 128 : 128 + HQ]], axis=1)

    outs = [(1, D), (5, D), (5, 256), (1, 2 * HQ), (1, 2 * HQ), (1, 2 * HQ), (1, D)]
    ins = [(own, None), (arrived, None)]
    return kernel_call(body, ins, [(s, F32) for s in outs], (), "pack_finish", 16)


def add_two(a, b, name):
    def body(a, b, out):
        out[...] = a[...] + b[...]

    return kernel_call(body, [(a, None), (b, None)], [(a.shape, F32)], (), name, 16)[0]


def assemble_states(lower, upper):
    def body(l0, l1, uo0, uo1, ur0, ur1, out):
        p = lax.axis_index("pipe")
        for m, (low, own, other) in enumerate(((l0, uo0, ur0), (l1, uo1, ur1))):
            @pl.when(p == 0)
            def _():
                out[m] = low[...]

            @pl.when(p == 1)
            def _():
                join(p, own, other, out.at[m], slice(0, D))

    arrays = list(lower) + [u[0] for u in upper] + [u[1] for u in upper]
    return kernel_call(body, [(a, None) for a in arrays], [((2, T, D), BF16)], (), "hidden_states", 24)[0]


def assemble_grads(lower, upper):
    def body(lo0, lo1, lr0, lr1, u0, u1, out):
        p = lax.axis_index("pipe")
        for m, (own, other, up) in enumerate(((lo0, lr0, u0), (lo1, lr1, u1))):
            @pl.when(p == 0)
            def _():
                join(p, own, other, out.at[m], slice(0, D))

            @pl.when(p == 1)
            def _():
                out[m] = up[...]

    arrays = [l[0] for l in lower] + [l[1] for l in lower] + list(upper)
    return kernel_call(body, [(a, None) for a in arrays], [((2, T, D), BF16)], (), "input_grads", 24)[0]


def local(
    hidden,
    segments,
    cotangent,
    norm_gain,
    main_w,
    state_w,
    step_w,
    conv_main,
    conv_state,
    step_bias,
    decay_log,
    skip_scale,
    gate_gain,
    out_w,
):
    ORDER.clear()
    p = lax.axis_index("pipe")
    hidden = hidden.reshape(2, T, D)
    cotangent = cotangent.reshape(2, T, D)
    seg = segments.reshape(2, 1, T)

    main_sent = lax.dynamic_slice(main_w[0], (0, 0, (1 - p) * Q), (D, 2, Q))
    main_got = jnp.transpose(swap(main_sent), (1, 0, 2))
    main_own = jnp.transpose(main_w[0], (1, 0, 2))
    out_own = out_w[0]
    out_got = swap(lax.dynamic_slice(out_own, ((1 - p) * Q, 0), (Q, D)))
    state_own = state_w[0]
    state_got = swap(state_own)
    wd = jnp.transpose(step_w[0], (1, 0))
    small = [norm_gain, conv_main[0], conv_state[0], step_bias, decay_log, skip_scale, gate_gain, wd]
    par_own, par_sent, wd_own, wd_sent = kernel_call(
        pack_kernel,
        [(a, None) for a in small],
        [((32, Q), F32), ((32, Q), F32), ((16, D), BF16), ((16, D), BF16)],
        name="pack",
        limit=16,
    )
    pars = (par_own, swap(par_sent))
    wds = (wd_own, swap(wd_sent))
    wss = (state_own, state_got)
    mains = (main_own, main_got)
    wos = (out_own, out_got)

    both = lambda: [None, None]
    projected, turned, mixes, chips, sums, result = ([both(), both()] for _ in range(6))
    gates, tails, crossed, smalls, back, back_sums, grads, packs = ([both(), both()] for _ in range(8))
    lower_a = both()

    def forward_project(layer, m):
        xs = hidden if layer == 0 else result[0][m]
        projected[layer][m] = project(layer, m, xs, pars, wds, wss, mains)

    def forward_mix(layer, m):
        _, pre, spre, raw = projected[layer][m][:4]
        mixed, inner, send, keep = mix(layer, m, pre, spre, raw, seg, pars, wos)
        mixes[layer][m] = (mixed, inner)
        chips[layer][m] = (keep, swap(send))

    def forward_add(layer, m):
        sums[layer][m] = join_sums(f"out_{layer}", m, *chips[layer][m])

    def forward_finish(layer, m):
        sums[layer][m] = (sums[layer][m], swap(sums[layer][m], "tensor"))
        if layer == 0:
            done = finish_forward(0, m, *sums[0][m], hidden, None)
        else:
            done = finish_forward(1, m, *sums[1][m], result[0][m][0], cotangent)
        result[layer][m] = (done, swap(done))

    def forward_turn(layer, m):
        turned[layer][m] = turn(layer, m, projected[layer][m][0])

    def backward_gate(layer, m):
        pre = projected[layer][m][1]
        mixed, inner = mixes[layer][m]
        if layer == 1:
            outs = gate_back(1, m, cotangent, result[1][m], pre, mixed, inner, pars, wos)
        else:
            *outs, lower_a[m] = gate_back(0, m, grads[1][m], result[0][m], pre, mixed, inner, pars, wos)
        gates[layer][m] = outs
        crossed[layer][m] = swap(outs[3])

    def backward_mix(layer, m):
        _, pre, spre, raw = projected[layer][m][:4]
        mixed, inner = mixes[layer][m]
        d_comb, pack_a = gates[layer][m][1], gates[layer][m][4]
        tails[layer][m] = mix_back(layer, m, d_comb, inner, pre, spre, raw, seg, mixed, pack_a, pars)
        smalls[layer][m] = swap(tails[layer][m][1])
        packs[layer][m] = [tails[layer][m][3]]

    def backward_project(layer, m):
        d_inner, d_small, d_raw, _ = tails[layer][m]
        send, keep = project_back(layer, m, gates[layer][m][0], d_inner, d_small, d_raw, wds, wss, mains)
        back[layer][m] = (keep, swap(send))

    def backward_add(layer, m):
        back_sums[layer][m] = join_sums(f"in_{layer}", m, *back[layer][m])

    def backward_finish(layer, m):
        back_sums[layer][m] = (back_sums[layer][m], swap(back_sums[layer][m], "tensor"))
        if layer == 1:
            done, pack = finish_back(1, m, *back_sums[1][m], result[0][m][0], cotangent, pars, sums[0][m])
        else:
            done, pack = finish_back(0, m, *back_sums[0][m], hidden, grads[1][m][0], pars, None)
        grads[layer][m] = (done, swap(done))
        packs[layer][m].append(pack)

    def operands(layer):
        lefts = [turned[layer][m].reshape(4, 4, 96, T) for m in range(2)]
        groups = []
        for m in range(2):
            d_gate, _, scaled_t = gates[layer][m][:3]
            cross = crossed[layer][m].reshape(2, 4, 96, T)
            cot = cotangent if layer == 1 else lower_a[m]
            groups.append(
                {
                    "near": (tails[layer][m][0], cross, tails[layer][m][1], smalls[layer][m]),
                    "far": (d_gate, scaled_t.reshape(2, 4, 96, T), cot),
                }
            )
        return lefts, groups

    forward_project(0, 0)
    forward_mix(0, 0)
    forward_project(0, 1)
    forward_add(0, 0)
    forward_mix(0, 1)
    forward_turn(0, 0)
    forward_add(0, 1)
    forward_finish(0, 0)
    forward_turn(0, 1)
    forward_project(1, 0)
    forward_mix(1, 0)
    forward_finish(0, 1)
    forward_add(1, 0)
    forward_project(1, 1)
    forward_mix(1, 1)
    forward_turn(1, 0)
    forward_add(1, 1)
    forward_finish(1, 0)
    forward_turn(1, 1)
    backward_gate(1, 0)
    backward_mix(1, 0)
    forward_finish(1, 1)
    meanwhile(crossed[1][0])
    backward_project(1, 0)
    meanwhile(smalls[1][0])
    backward_gate(1, 1)
    backward_add(1, 0)
    backward_mix(1, 1)
    meanwhile(crossed[1][1])
    backward_project(1, 1)
    backward_finish(1, 0)
    backward_add(1, 1)
    upper = operands(1)
    upper_moved = scatter(1, 0, upper)
    backward_gate(0, 0)
    backward_mix(0, 0)
    backward_finish(1, 1)
    meanwhile(crossed[0][0])
    upper_moved = scatter(1, 1, upper, upper_moved)
    meanwhile(smalls[0][0])
    backward_project(0, 0)
    backward_gate(0, 1)
    backward_add(0, 0)
    backward_mix(0, 1)
    meanwhile(crossed[0][1])
    backward_project(0, 1)
    lower = operands(0)
    lower_moved = scatter(0, 0, lower)
    backward_add(0, 1)
    backward_finish(0, 0)
    upper_moved = scatter(1, 2, upper, upper_moved)
    states = assemble_states([projected[1][m][4] for m in range(2)], result[1])
    backward_finish(0, 1)
    pack, pack_rows = sum_packs([packs[layer][0] + packs[layer][1] for layer in range(2)])
    pack_rows = swap(pack_rows, "tensor")
    lower_moved = scatter(0, 1, lower, lower_moved)
    input_grads = assemble_grads(grads[0], lower_a)
    pack = add_state_rows(pack, pack_rows)
    pack_got = [shift(pack, "z", k) for k in (1, 2, 3)]
    upper_moved = scatter_rows(1, upper_moved)
    upper_done = sum_rows(1, *upper_moved)
    upper_done = (upper_done, swap(upper_done))
    lower_moved = scatter(0, 2, lower, lower_moved)
    pack = sum_four(pack, pack_got, "pack_z")
    pack_got = [shift(pack, "y", k) for k in (1, 2, 3)]
    meanwhile(upper_done[1])
    lower_moved = scatter_rows(0, lower_moved)
    pack = sum_four(pack, pack_got, "pack_y")
    pack = add_two(pack, shift(pack, "x", 1), "pack_x")
    lower_done = sum_rows(0, *lower_moved)
    lower_done = (lower_done, swap(lower_done))
    outs = finish_packs(pack, swap(pack))
    grad_norm, grad_taps, grad_state_taps, grad_bias, grad_log, grad_skip, grad_gain = outs
    grad_main, grad_state, grad_step, grad_out = finish_weights(lower_done, upper_done)
    return (
        states.reshape(1, 2, 1, T, D),
        input_grads.reshape(1, 2, 1, T, D),
        grad_norm,
        grad_main[None],
        grad_state[None],
        grad_step[None],
        grad_taps[None],
        grad_state_taps[None],
        grad_bias,
        grad_log,
        grad_skip,
        grad_gain,
        grad_out[None],
    )


def solution(mesh):
    in_specs = (
        P(None, "dp", None, None),
        P(None, "dp", None),
        P(None, "dp", None, None),
        P("pipe", None),
        P("pipe", None, None, "tensor"),
        P("pipe", None, None),
        P("pipe", None, "tensor"),
        P("pipe", None, "tensor"),
        P("pipe", None, None),
        P("pipe", "tensor"),
        P("pipe", "tensor"),
        P("pipe", "tensor"),
        P("pipe", "tensor"),
        P("pipe", "tensor", None),
    )
    out_specs = (
        P("pipe", None, "dp", None, None),
        P("pipe", None, "dp", None, None),
        P("pipe", None),
        P("pipe", "dp", None, "tensor"),
        P("pipe", "dp", None),
        P("pipe", "dp", "tensor"),
        P("pipe", None, "tensor"),
        P("pipe", None, None),
        P("pipe", "tensor"),
        P("pipe", "tensor"),
        P("pipe", "tensor"),
        P("pipe", "tensor"),
        P("pipe", ("tensor", "dp"), None),
    )
    return jax.shard_map(local, mesh=mesh, in_specs=in_specs, out_specs=out_specs, check_vma=False)
```

```python
import jax
import jax.numpy as jnp
from jax import lax
from jax.experimental import pallas as pl
from jax.experimental.pallas import tpu as pltpu
from jax.sharding import PartitionSpec as P

F32 = jnp.float32
BF16 = jnp.bfloat16
EPS = 1e-05
D = 1536
Q = 768
HQ = 12
DI = 3072
T = 256
HALF = 128
EXT = D + 128
NEG = -1e30
PAIR = Q + 384


def dot(a, b):
    return lax.dot_general(a, b, (((1,), (0,)), ((), ())), preferred_element_type=F32)


def dot_nt(a, b):
    return lax.dot_general(a, b, (((1,), (1,)), ((), ())), preferred_element_type=F32)


def sigmoid(v):
    return 0.5 * jnp.tanh(0.5 * v) + 0.5


def softplus(v):
    e = jnp.exp(-jnp.abs(v))
    small = e * (1.0 - e * (0.5 - e * (1.0 / 3.0 - e * 0.25)))
    return jnp.maximum(v, 0.0) + jnp.where(e < 0.01, small, jnp.log(1.0 + e))


def iota(shape, dim):
    return lax.broadcasted_iota(jnp.int32, shape, dim)


def pieces(v):
    high = v.astype(BF16).astype(F32)
    mid = (v - high).astype(BF16).astype(F32)
    return high, mid, (v - high - mid).astype(BF16).astype(F32)


def lanes_of(v, first):
    lane = iota((v.shape[0], 128), 1)
    out = jnp.zeros((v.shape[0], 128), F32)
    for k, part in enumerate(pieces(v)):
        out = out + jnp.where(lane == first + k, part, 0.0)
    return out


def scalar_at(ext, first, count=3):
    lane = iota(ext.shape, 1)
    keep = (lane >= first) & (lane < first + count)
    return jnp.sum(jnp.where(keep, ext, 0.0), axis=1, keepdims=True)


def half_rows(which):
    return pl.ds(pl.multiple_of(which * HALF, HALF), HALF)


def whole(shape):
    return pl.BlockSpec(shape, lambda i: (0,) * len(shape))


def part(shape, at):
    return pl.BlockSpec(shape, lambda i: at)


ANY = pl.BlockSpec(memory_space=pl.ANY)
HBM = pl.BlockSpec(memory_space=pltpu.HBM)


COST = [30]
ORDER = []


def kernel_call(body, ins, outs, scratch=(), name=None, limit=22, after=(), placed=0, onto=()):
    after = tuple(ORDER) + tuple(after)
    if after or onto:
        inner, count, skip = body, len(ins), len(after) + len(onto)
        body = lambda *refs: inner(*refs[:count], *refs[count + skip :])
        ins = list(ins) + [(a, ANY) for a in after] + [(a, HBM) for a in onto]
    arrays = [a for a, _ in ins]
    specs = [whole(a.shape) if s is None else s for a, s in ins]
    results = pl.pallas_call(
        body,
        grid=(1,),
        in_specs=specs,
        out_specs=[whole(s) for s, _ in outs[: len(outs) - placed]] + [HBM] * placed,
        out_shape=[jax.ShapeDtypeStruct(s, d) for s, d in outs],
        scratch_shapes=list(scratch),
        input_output_aliases={len(ins) - len(onto) + n: len(outs) - placed + n for n in range(len(onto))},
        compiler_params=pltpu.CompilerParams(vmem_limit_bytes=limit * 1024 * 1024),
        cost_estimate=pl.CostEstimate(flops=int(COST[0] * 10**9), bytes_accessed=1 << 10, transcendentals=0),
        name=name,
    )(*arrays)
    ORDER[:] = [min(results, key=lambda r: r.size * r.dtype.itemsize)]
    return results


def meanwhile(*arrays):
    ORDER.extend(arrays)


def start_either(mine, own, other, dst, sem):
    @pl.when(mine)
    def _():
        pltpu.make_async_copy(own, dst, sem).start()

    @pl.when(jnp.logical_not(mine))
    def _():
        pltpu.make_async_copy(other, dst, sem).start()


def wait_for(src, dst, sem):
    pltpu.make_async_copy(src, dst, sem).wait()


def pick(mine, own, other, dst):
    @pl.when(mine)
    def _():
        dst[...] = own[...]

    @pl.when(jnp.logical_not(mine))
    def _():
        dst[...] = other[...]


def join(p, own, other, dst, columns=slice(None)):
    dst[half_rows(p), :] = own[:, columns].astype(dst.dtype)
    dst[half_rows(1 - p), :] = other[:, columns].astype(dst.dtype)


TAPS, GATE, NORM, STAPS, SKIP, HEAD = 0, 5, 6, 8, 13, 16


def slice_kernel(main, sent, mine, sem):
    p = lax.axis_index("pipe")
    far = pl.ds(pl.multiple_of((1 - p) * Q, Q), Q)
    near = pl.ds(pl.multiple_of(p * Q, Q), Q)
    moves = [
        pltpu.make_async_copy(main.at[:, :, far], sent, sem.at[0]),
        pltpu.make_async_copy(main.at[:, :, near], mine, sem.at[1]),
    ]
    for move in moves:
        move.start()
    for move in moves:
        move.wait()


def pack_kernel(ng, cm, cs, sb, dl, ss, gg, wd, own, other, wd_own, wd_other):
    p = lax.axis_index("pipe")
    for target, wd_target, which in ((own, wd_own, p), (other, wd_other, 1 - p)):
        lanes = pl.ds(pl.multiple_of(which * Q, Q), Q)
        target[...] = jnp.zeros(target.shape, F32)
        target[TAPS : TAPS + 5, :] = cm[:, lanes]
        target[GATE : GATE + 1, :] = gg[:, lanes]
        target[NORM : NORM + 1, :] = ng[:, :Q]
        target[NORM + 1 : NORM + 2, :] = ng[:, Q:]
        target[STAPS : STAPS + 5, :256] = cs[...]
        second = which == 1
        head = [jnp.where(second, v[:, HQ : 2 * HQ], v[:, :HQ]) for v in (sb, dl, ss)]
        row = jnp.concatenate([head[2], jnp.zeros((1, 128 - HQ), F32)], axis=1)
        column = jnp.broadcast_to(row, (128, 128)).T
        owner = iota((16, Q), 1) // 64 == iota((16, Q), 0)
        spread = jnp.where(owner, column[:16, :1], 0.0)
        target[SKIP : SKIP + 1, :] = jnp.sum(spread, axis=0, keepdims=True)
        rows = [jnp.concatenate([v, jnp.zeros((1, 128 - HQ), F32)], axis=1) for v in head[:2]]
        square = jnp.concatenate([rows[0], -jnp.exp(rows[1]), jnp.zeros((126, 128), F32)], axis=0)
        target[HEAD : HEAD + 16, :128] = square.T[:16, :]
        wide = wd[...].astype(F32)
        chosen = jnp.where(second, wide[HQ:, :], wide[:HQ, :])
        wd_target[...] = jnp.concatenate([chosen, jnp.zeros((4, D), F32)], axis=0).astype(BF16)


def project_body(layer, p, x, par, wd, ws, w_scr, waits, outs):
    rounded, pre, spre, raw = outs
    factor = lax.rsqrt(jnp.mean(x * x, axis=1, keepdims=True) + EPS)
    scaled = x * factor
    for c in range(2):
        cols = slice(c * Q, (c + 1) * Q)
        normed = scaled[:, cols] * par[NORM + c : NORM + c + 1, :]
        rounded[:, cols] = normed.astype(BF16)
    raw[...] = dot_nt(wd[...], rounded[...])
    waits[0]()
    spre[...] = dot(rounded[...], ws[...])
    waits[1]()
    for u in range(2):
        for c in range(3):
            cols = slice(c * 256, (c + 1) * 256)
            pre[:, u * Q + c * 256 : u * Q + (c + 1) * 256] = dot(rounded[...], w_scr[u, :, cols])


def project(layer, m, xs, pars, wds, wss, ws_main):
    first = layer == 0

    def body(*refs):
        xr = refs[: 1 if first else 2]
        par_o, par_r, wd_o, wd_r, ws_o, ws_r, wm_o, wm_r = refs[len(xr) : len(xr) + 8]
        rest = refs[len(xr) + 8 :]
        outs, scr = rest[: 4 if first else 5], rest[4 if first else 5 :]
        par, wd, ws, w_scr, sem = scr
        p = lax.axis_index("pipe")
        mine = p == layer
        start_either(mine, ws_o, ws_r, ws, sem.at[0])
        start_either(mine, wm_o, wm_r, w_scr, sem.at[1])
        pick(mine, par_o, par_r, par)
        pick(mine, wd_o, wd_r, wd)
        if first:
            x = xr[0][0].astype(F32)
        else:
            join(p, xr[0], xr[1], outs[4], slice(0, D))
            x = outs[4][...].astype(F32)
        waits = (
            lambda: wait_for(ws_r, ws, sem.at[0]),
            lambda: wait_for(wm_r, w_scr, sem.at[1]),
        )
        project_body(layer, p, x, par, wd, ws, w_scr, waits, outs[:4])

    if first:
        ins = [(xs, part((1, T, D), (m, 0, 0)))]
    else:
        ins = [(xs[0], None), (xs[1], None)]
    ins += [(a, None) for a in pars] + [(a, None) for a in wds]
    ins += [(a, ANY) for a in wss] + [(a, ANY) for a in ws_main]
    outs = [((T, D), BF16), ((T, D), F32), ((T, T), F32), ((16, T), F32)]
    if not first:
        outs.append(((T, D), BF16))
    scratch = [
        pltpu.VMEM((32, Q), F32),
        pltpu.VMEM((16, D), BF16),
        pltpu.VMEM((D, 256), BF16),
        pltpu.VMEM((2, D, Q), BF16),
        pltpu.SemaphoreType.DMA((2,)),
    ]
    return kernel_call(body, ins, outs, scratch, f"project_{layer}_{m}")


def turn(layer, m, rounded):
    def body(rounded, out):
        for c in range(6):
            cols = slice(c * 256, (c + 1) * 256)
            out[cols, :] = rounded[:, cols].T

    return kernel_call(body, [(rounded, None)], [((D, T), BF16)], (), f"turn_{layer}_{m}", 16)[0]


def document_ids(seg_ref):
    row = jnp.broadcast_to(seg_ref[0].astype(F32), (T, T))
    return row.T, row


def same_document(by_token, lag):
    position = iota((T, T), 0)
    earlier = pltpu.roll(by_token, lag, 0)
    return jnp.where((earlier == by_token) & (position >= lag), 1.0, 0.0)


def convolve(values, taps, same):
    out = taps[4:5] + taps[3:4] * values
    for lag in range(1, 4):
        out = out + taps[3 - lag : 4 - lag] * (pltpu.roll(values, lag, 0) * same[lag])
    return out


def convolve_back(d_sum, values, taps, same):
    d_values = taps[3:4] * d_sum
    rows = [None] * 5
    rows[4] = jnp.sum(d_sum, axis=0, keepdims=True)
    rows[3] = jnp.sum(d_sum * values, axis=0, keepdims=True)
    for lag in range(1, 4):
        held = d_sum * same[lag]
        d_values = d_values + taps[3 - lag : 4 - lag] * pltpu.roll(held, T - lag, 0)
        moved = pltpu.roll(values, lag, 0)
        rows[3 - lag] = jnp.sum(held * moved, axis=0, keepdims=True)
    return d_values, jnp.concatenate(rows, axis=0)


def step_sizes(raw, par):
    before = raw[...] + par[HEAD : HEAD + 16, 0:1]
    step = softplus(before)
    total = step * par[HEAD : HEAD + 16, 1:2]
    lane = iota(total.shape, 1)
    shift = 1
    while shift < T:
        total = total + jnp.where(lane >= shift, pltpu.roll(total, shift, 1), 0.0)
        shift *= 2
    return before, step, total


def columns_of(rows):
    return jnp.concatenate([rows, jnp.zeros((112, T), F32)], axis=0).T


def mix(layer, m, pre, spre, raw, seg, pars, wos):
    def body(pre, spre, raw, seg, par_o, par_r, wo_o, wo_r, *rest):
        mixed, inner_out, send, keep, par, wo, gs, u_scr, sem = rest
        p, t = lax.axis_index("pipe"), lax.axis_index("tensor")
        mine = p == layer
        own = wo_o.at[pl.ds(pl.multiple_of(p * Q, Q), Q), :]
        start_either(mine, own, wo_r, wo, sem)
        pick(mine, par_o, par_r, par)
        by_token, by_row = document_ids(seg)
        same = [None] + [same_document(by_token, lag) for lag in range(1, 4)]
        allowed = (by_token == by_row) & (iota((T, T), 0) >= iota((T, T), 1))
        state = convolve(spre[...], par[STAPS : STAPS + 5, :256], same)
        state = (state * sigmoid(state)).astype(BF16)
        crossed = dot_nt(state[:, 128:], state[:, :128])
        _, step, total = step_sizes(raw, par)
        total_t = columns_of(total)
        low = iota((T, 128), 1) < 64
        squares = jnp.zeros((T, 1), F32)
        for g in range(3):
            cols = slice(g * 256, (g + 1) * 256)
            summed = convolve(pre[:, Q + g * 256 : Q + (g + 1) * 256], par[TAPS : TAPS + 5, cols], same)
            inner = (summed * sigmoid(summed)).astype(BF16)
            inner_out[:, cols] = inner
            for pair in range(2):
                at = slice(g * 256 + pair * 128, g * 256 + (pair + 1) * 128)
                values = inner[:, pair * 128 : (pair + 1) * 128]
                out = None
                for k in range(2):
                    h = g * 4 + pair * 2 + k
                    gap = total_t[:, h : h + 1] - total[h : h + 1, :]
                    decay = jnp.exp(jnp.where(allowed, gap, NEG))
                    mixing = (crossed * decay * step[h : h + 1, :]).astype(BF16)
                    chosen = jnp.where(low if k == 0 else ~low, values, jnp.zeros_like(values))
                    term = dot(mixing, chosen)
                    out = term if out is None else out + term
                mixed[:, at] = out
            combined = mixed[:, cols] + par[SKIP : SKIP + 1, cols] * inner.astype(F32)
            gate = pre[:, cols]
            gated = combined * (gate * sigmoid(gate))
            squares = squares + jnp.sum(gated * gated, axis=1, keepdims=True)
            gs[:, cols] = (gated * par[GATE : GATE + 1, cols]).astype(BF16)
        wait_for(wo_r, wo, sem)
        for c in range(3):
            cols = slice(c * 512, (c + 1) * 512)
            u_scr[:, cols] = dot(gs[...], wo[:, cols]).astype(BF16)
        u_scr[:, D:] = lanes_of(squares, 3 * (2 * p + t)).astype(BF16)
        send[...] = u_scr[half_rows(1 - p), :]
        keep[...] = u_scr[half_rows(p), :]

    ins = [(pre, None), (spre, None), (raw, None), (seg, part((1, 1, T), (m, 0, 0)))]
    ins += [(a, None) for a in pars] + [(a, ANY) for a in wos]
    outs = [((T, Q), F32), ((T, Q), BF16), ((HALF, EXT), BF16), ((HALF, EXT), BF16)]
    scratch = [
        pltpu.VMEM((32, Q), F32),
        pltpu.VMEM((Q, D), BF16),
        pltpu.VMEM((T, Q), BF16),
        pltpu.VMEM((T, EXT), BF16),
        pltpu.SemaphoreType.DMA,
    ]
    return kernel_call(body, ins, outs, scratch, f"mix_{layer}_{m}")


def finish_forward(layer, m, chip, arrived, x, cot):
    def body(chip, arrived, x, *rest):
        p = lax.axis_index("pipe")
        out = rest[-1]
        total = chip[:, :D].astype(F32) + arrived[:, :D].astype(F32)
        ext = chip[:, D:].astype(F32) + arrived[:, D:].astype(F32)
        factor = lax.rsqrt(jnp.sum(ext, axis=1, keepdims=True) / DI + EPS)
        if layer == 0:
            before = x[0, half_rows(p), :].astype(F32)
        else:
            before = x[:, :D].astype(F32)
        out[:, :D] = (before + factor * total).astype(BF16)
        tail = lanes_of(factor, 0)
        if layer == 1:
            a = rest[0][0, half_rows(p), :].astype(F32)
            pull = factor * factor * factor * (jnp.sum(a * total, axis=1, keepdims=True) / DI)
            tail = tail + lanes_of(pull, 3)
        out[:, D:] = tail.astype(BF16)

    ins = [(chip, None), (arrived, None)]
    if layer == 0:
        ins += [(x, part((1, T, D), (m, 0, 0)))]
    else:
        ins += [(x, None), (cot, part((1, T, D), (m, 0, 0)))]
    return kernel_call(body, ins, [((HALF, EXT), BF16)], (), f"finish_out_{layer}_{m}", 16)[0]


def gate_back(layer, m, a, scalars, pre, mixed, inner, pars, wos):
    lower = layer == 0

    def body(*refs):
        if lower:
            a_o, a_r, s_o, s_r = refs[:4]
            refs = refs[4:]
        else:
            a_f, s_o, s_r = refs[:3]
            refs = refs[3:]
        pre, mixed, inner, par_o, par_r, wo_o, wo_r = refs[:7]
        d_gate, d_comb, scaled_t, cross, pack = refs[7:12]
        refs = refs[12:]
        if lower:
            a_all = refs[0]
            refs = refs[1:]
        par, wo, ext, ext2, sem = refs
        p = lax.axis_index("pipe")
        mine = p == layer
        own = wo_o.at[pl.ds(pl.multiple_of(p * Q, Q), Q), :]
        start_either(mine, own, wo_r, wo, sem)
        pick(mine, par_o, par_r, par)
        join(p, s_o, s_r, ext)
        factor = scalar_at(ext[...], 0)
        if lower:
            join(p, a_o, a_r, a_all, slice(0, D))
            join(p, a_o, a_r, ext2, slice(D, EXT))
            pull = scalar_at(ext2[...], 3)
            a = a_all[...]
        else:
            pull = scalar_at(ext[...], 3)
            a = a_f[0]
        wait_for(wo_r, wo, sem)
        pack[...] = jnp.zeros(pack.shape, F32)
        for g in range(3):
            cols = slice(g * 256, (g + 1) * 256)
            d_scaled = dot_nt(a, wo[cols, :])
            values = inner[:, cols].astype(F32)
            combined = mixed[:, cols] + par[SKIP : SKIP + 1, cols] * values
            gate = pre[:, cols]
            opened = sigmoid(gate)
            silu = gate * opened
            gated = combined * silu
            normed = gated * factor
            gain = par[GATE : GATE + 1, cols]
            scaled = (normed * gain).T.astype(BF16)
            scaled_t[cols, :] = scaled
            pack[0:1, cols] = jnp.sum(d_scaled * normed, axis=0, keepdims=True)
            d_gated = d_scaled * gain * factor - gated * pull
            d_combined = d_gated * silu
            d_comb[:, cols] = d_combined
            pack[1:2, cols] = jnp.sum(d_combined * values, axis=0, keepdims=True)
            d_open = d_gated * combined * (opened * (1.0 + gate * (1.0 - opened)))
            d_gate[:, cols] = d_open.astype(BF16)
            cross[cols, :] = jnp.where(p == 0, scaled, d_open.T.astype(BF16))

    last = part((HALF, 128), (0, D // 128))
    if lower:
        ins = [(a[0], None), (a[1], None)]
    else:
        ins = [(a, part((1, T, D), (m, 0, 0)))]
    ins += [(s, last) for s in scalars]
    ins += [(pre, part((T, Q), (0, 0))), (mixed, None), (inner, None)]
    ins += [(v, None) for v in pars] + [(v, ANY) for v in wos]
    outs = [((T, Q), BF16), ((T, Q), F32), ((Q, T), BF16), ((Q, T), BF16), ((8, Q), F32)]
    if lower:
        outs.append(((T, D), BF16))
    scratch = [
        pltpu.VMEM((32, Q), F32),
        pltpu.VMEM((Q, D), BF16),
        pltpu.VMEM((T, 128), F32),
        pltpu.VMEM((T, 128), F32),
        pltpu.SemaphoreType.DMA,
    ]
    return kernel_call(body, ins, outs, scratch, f"gate_back_{layer}_{m}")


def per_head(values):
    high = values.astype(BF16)
    rest = (values - high.astype(F32)).astype(BF16)
    owner = (iota((Q, 128), 0) // 64 == iota((Q, 128), 1)).astype(BF16)
    return dot(high, owner) + dot(rest, owner)


def mix_back(layer, m, d_comb, inner, pre, spre, raw, seg, mixed, cross, pack_a, pars):
    def body(d_comb, inner, pre, spre, raw, seg, mixed, cross, pack_a, par_o, par_r, *rest):
        d_tail, d_small, both, d_raw_out, pack, par, gap_prod, col_prod = rest
        p = lax.axis_index("pipe")
        mine = p == layer
        pick(mine, par_o, par_r, par)
        both[:Q, :] = cross[...]
        by_token, by_row = document_ids(seg)
        same = [None] + [same_document(by_token, lag) for lag in range(1, 4)]
        allowed = (by_token == by_row) & (iota((T, T), 1) >= iota((T, T), 0))
        summed_s = convolve(spre[...], par[STAPS : STAPS + 5, :256], same)
        opened_s = sigmoid(summed_s)
        state = (summed_s * opened_s).astype(BF16)
        keys, query = state[:, :128], state[:, 128:]
        crossed = dot_nt(keys, query)
        before, step, total = step_sizes(raw, par)
        total_t, step_t = columns_of(total), columns_of(step)
        low = iota((T, 128), 1) < 64
        d_cross = jnp.zeros((T, T), F32)
        pack[...] = jnp.zeros(pack.shape, F32)
        for g in range(3):
            cols = slice(g * 256, (g + 1) * 256)
            heads = []
            for pair in range(2):
                at = slice(g * 256 + pair * 128, g * 256 + (pair + 1) * 128)
                values = inner[:, at]
                d_mixed = d_comb[:, at].astype(BF16)
                d_heads = None
                for k in range(2):
                    h = g * 4 + pair * 2 + k
                    side = low if k == 0 else ~low
                    gap = total[h : h + 1, :] - total_t[:, h : h + 1]
                    decay = jnp.exp(jnp.where(allowed, gap, NEG)) * step_t[:, h : h + 1]
                    mixing = (crossed * decay).astype(BF16)
                    chosen = jnp.where(side, d_mixed, jnp.zeros_like(d_mixed))
                    d_mixing = dot_nt(values, chosen)
                    d_cross = d_cross + d_mixing * decay
                    term = dot(mixing, chosen)
                    d_heads = term if d_heads is None else d_heads + term
                heads.append(d_heads)
                along = values.astype(F32) * d_heads
                col_prod[:, at] = along
                gap_prod[:, at] = d_mixed.astype(F32) * mixed[:, at] - along
            taps = par[TAPS : TAPS + 5, cols]
            values = pre[:, cols]
            summed = convolve(values, taps, same)
            opened = sigmoid(summed)
            d_inner = jnp.concatenate(heads, axis=1) + par[SKIP : SKIP + 1, cols] * d_comb[:, cols]
            d_sum = d_inner * (opened * (1.0 + summed * (1.0 - opened)))
            d_values, rows = convolve_back(d_sum, values, taps, same)
            d_tail[:, cols] = d_values.astype(BF16)
            pack[0:5, cols] = rows
        pack[5:7, :] = pack_a[0:2, :]
        crossed_b = d_cross.astype(BF16)
        d_keys = dot(crossed_b, query)
        d_query = dot(d_cross.T.astype(BF16), keys)
        d_state = jnp.concatenate([d_keys, d_query], axis=1)
        d_sum = d_state * (opened_s * (1.0 + summed_s * (1.0 - opened_s)))
        d_values, rows = convolve_back(d_sum, spre[...], par[STAPS : STAPS + 5, :256], same)
        d_small[...] = d_values.astype(BF16)
        both[Q : Q + 256, :] = d_values.T.astype(BF16)
        pack[8:13, :256] = rows
        d_gap = per_head(gap_prod[...]).T[:16, :]
        d_col = per_head(col_prod[...]).T[:16, :]
        lane = iota(d_gap.shape, 1)
        shift = 1
        while shift < T:
            d_gap = d_gap + jnp.where(lane < T - shift, pltpu.roll(d_gap, T - shift, 1), 0.0)
            shift *= 2
        rate = par[HEAD : HEAD + 16, 1:2]
        slope = sigmoid_small(before)
        ratio = jnp.where(step > 1e-30, slope / jnp.maximum(step, 1e-30), 1.0)
        d_raw = d_col * ratio + d_gap * rate * slope
        valid = iota((16, T), 0) < HQ
        d_raw = jnp.where(valid, d_raw, 0.0)
        d_log = jnp.where(valid, d_gap * step * rate, 0.0)
        raw_t = columns_of(d_raw)
        d_raw_out[...] = raw_t.astype(BF16)
        both[Q + 256 :, :] = jnp.where(p == 1, pltpu.roll(raw_t, HQ, 1), raw_t).T.astype(BF16)
        bias_row = jnp.broadcast_to(jnp.sum(d_raw, axis=1, keepdims=True), (16, 128))
        log_row = jnp.broadcast_to(jnp.sum(d_log, axis=1, keepdims=True), (16, 128))
        square = jnp.concatenate([bias_row, jnp.zeros((112, 128), F32)], axis=0).T
        pack[7:8, 0:128] = square[0:1, :]
        square = jnp.concatenate([log_row, jnp.zeros((112, 128), F32)], axis=0).T
        pack[7:8, 128:256] = square[0:1, :]

    ins = [(d_comb, None), (inner, None), (pre, part((T, Q), (0, 1))), (spre, None), (raw, None)]
    ins += [(seg, part((1, 1, T), (m, 0, 0))), (mixed, None), (cross, None), (pack_a, None)]
    ins += [(v, None) for v in pars]
    outs = [((T, Q), BF16), ((T, T), BF16), ((PAIR, T), BF16), ((T, 128), BF16), ((16, Q), F32)]
    scratch = [pltpu.VMEM((32, Q), F32), pltpu.VMEM((T, Q), F32), pltpu.VMEM((T, Q), F32)]
    return kernel_call(body, ins, outs, scratch, f"mix_back_{layer}_{m}")


def sigmoid_small(v):
    e = jnp.exp(-jnp.abs(v))
    return jnp.where(v >= 0.0, 1.0, e) / (1.0 + e)


def project_back(layer, m, d_gate, d_inner, d_small, d_raw, x, wds, wss, ws_main):
    def body(d_gate, d_inner, d_small, d_raw, x, wd_o, wd_r, ws_o, ws_r, wm_o, wm_r, send, keep, gain, wd, ws, w_scr, acc, sem):
        p = lax.axis_index("pipe")
        mine = p == layer
        start_either(mine, wm_o, wm_r, w_scr, sem.at[1])
        start_either(mine, ws_o, ws_r, ws, sem.at[0])
        pick(mine, wd_o, wd_r, wd)
        values = (x[0] if layer == 0 else x[...]).astype(F32)
        factor = lax.rsqrt(jnp.mean(values * values, axis=1, keepdims=True) + EPS)
        gain[...] = jnp.zeros(gain.shape, F32)
        wait_for(ws_r, ws, sem.at[0])
        wait_for(wm_r, w_scr, sem.at[1])
        for c in range(6):
            rows = slice(c * 256, (c + 1) * 256)
            out = dot_nt(d_gate[...], w_scr[0, rows, :])
            out = out + dot_nt(d_inner[...], w_scr[1, rows, :])
            out = out + dot_nt(d_small[...], ws[rows, :])
            out = out + dot(d_raw[:, :16], wd[:, rows])
            acc[:, rows] = out.astype(BF16)
            gain[c // 3 : c // 3 + 1, rows.start - c // 3 * Q : rows.stop - c // 3 * Q] = jnp.sum(
                out * (values[:, rows] * factor), axis=0, keepdims=True
            )
        send[...] = acc[half_rows(1 - p), :]
        keep[...] = acc[half_rows(p), :]

    ins = [(d_gate, None), (d_inner, None), (d_small, None), (d_raw, None)]
    ins += [(x, part((1, T, D), (m, 0, 0)) if layer == 0 else None)] + [(a, None) for a in wds]
    ins += [(a, ANY) for a in wss] + [(a, ANY) for a in ws_main]
    outs = [((HALF, D), BF16), ((HALF, D), BF16), ((8, Q), F32)]
    scratch = [
        pltpu.VMEM((16, D), BF16),
        pltpu.VMEM((D, 256), BF16),
        pltpu.VMEM((2, D, Q), BF16),
        pltpu.VMEM((T, D), BF16),
        pltpu.SemaphoreType.DMA((2,)),
    ]
    return kernel_call(body, ins, outs, scratch, f"project_back_{layer}_{m}")


def finish_back(layer, m, chip, arrived, x, a, pars, below):
    def body(*refs):
        chip, arrived, x, a, par_o, par_r = refs[:6]
        refs = refs[6:]
        if layer == 1:
            u_o, u_r, y = refs[:3]
            refs = refs[3:]
        out, par = refs
        p = lax.axis_index("pipe")
        mine = p == layer
        pick(mine, par_o, par_r, par)
        d_rounded = chip[...].astype(F32) + arrived[...].astype(F32)
        if layer == 0:
            xv = x[0, half_rows(p), :].astype(F32)
            av = a[:, :D].astype(F32)
        else:
            xv = x[:, :D].astype(F32)
            av = a[0, half_rows(p), :].astype(F32)
        factor = lax.rsqrt(jnp.mean(xv * xv, axis=1, keepdims=True) + EPS)
        normed = xv * factor
        gain = jnp.concatenate([par[NORM : NORM + 1, :], par[NORM + 1 : NORM + 2, :]], axis=1)
        pulled = d_rounded * gain
        mean = jnp.mean(pulled * normed, axis=1, keepdims=True)
        result = (av + factor * (pulled - normed * mean)).astype(BF16)
        out[:, :D] = result
        if layer == 1:
            branch = u_o[...].astype(F32) + u_r[...].astype(F32)
            gated = scalar_at(y[...].astype(F32), 0)
            total = jnp.sum(result.astype(F32) * branch, axis=1, keepdims=True)
            out[:, D:] = lanes_of(gated * gated * gated * (total / DI), 3).astype(BF16)
        else:
            out[:, D:] = jnp.zeros((HALF, 128), BF16)

    ins = [(chip, None), (arrived, None)]
    if layer == 0:
        ins += [(x, part((1, T, D), (m, 0, 0))), (a, None)]
    else:
        ins += [(x, None), (a, part((1, T, D), (m, 0, 0)))]
    ins += [(v, None) for v in pars]
    if layer == 1:
        narrow = part((HALF, D), (0, 0))
        ins += [(below[0], narrow), (below[1], narrow), (x, part((HALF, 128), (0, D // 128)))]
    outs = [((HALF, EXT), BF16)]
    return kernel_call(body, ins, outs, [pltpu.VMEM((32, Q), F32)], f"finish_back_{layer}_{m}", 16)[0]


def position():
    dp = lax.axis_index("dp")
    return dp // 8, (dp // 2) % 4, dp % 2


UNIT = 384
BLOCK = 256
WIDE = 2 * D - 512
BACK = WIDE // 2


def weight_stage(stage, layer, left, grads, arrived, onto=()):
    ins = [(v, None) for v in left]
    for group in grads:
        ins += [(v, None) for v in group["near"]] + [(v, ANY) for v in group["far"]]
    count = len(ins)

    def body(*refs):
        lefts, per, rest = refs[:2], (refs[2:8], refs[8:14]), refs[count:]
        rest, (gate_s, wide_s, cot_s, sem) = rest[:-4], rest[-4:]
        count_in, count_out = len(arrived), 4 if stage == 2 else 2
        came, far = rest[:count_in], rest[count_in : count_in + count_out]
        near = rest[count_in + count_out : count_in + 2 * count_out]
        total = rest[-1]
        if stage == 2:
            far = [ref.at[layer] for ref in far]
        moves = [pltpu.make_async_copy(near[n], far[n], sem.at[4 + n]) for n in range(count_out)]
        p = lax.axis_index("pipe")
        z, y, x = position()

        def copies(core):
            out = []
            for m in range(2):
                gate, wide, cot = per[m][3:]
                if core == 0:
                    out.append(pltpu.make_async_copy(gate, gate_s.at[m], sem.at[m]))
                else:
                    cot = cot.at[m] if layer == 1 else cot
                    out.append(pltpu.make_async_copy(wide, wide_s.at[m], sem.at[m]))
                    out.append(pltpu.make_async_copy(cot, cot_s.at[m], sem.at[2 + m]))
            return out

        def products(core, offset):
            inner = [per[m][0] for m in range(2)]
            cross = [per[m][2] for m in range(2)]
            shared = slice(Q, Q + 256) if core == 0 else slice(Q + 256, PAIR)
            small = [add_halves(per[m][1][shared, :], per[m][2][shared, :]) for m in range(2)]
            if core == 0:
                rows = [v[lax.rem(z + offset, 4)].reshape(UNIT, T) for v in lefts]
                yield 0, [dot(rows[m], gate_s[m]) for m in range(2)]
                yield Q, [dot_nt(rows[m], cross[m][:Q, :]) for m in range(2)]
                yield 2 * Q, [dot(rows[m], inner[m][...]) for m in range(2)]
                yield 3 * Q, [dot_nt(rows[m], small[m]) for m in range(2)]
            else:
                at = lax.rem(y + offset, 4)
                rows = [v[:, at].reshape(UNIT, T) for v in lefts]
                both = [
                    jnp.concatenate([channels(cross[m], at), wide_s[m, :, at].reshape(UNIT // 2, T)], axis=0)
                    for m in range(2)
                ]
                for n in range(2):
                    yield n * Q, [dot(both[m], cot_s[m, :, n * Q : (n + 1) * Q]) for m in range(2)]
                yield 2 * Q, [dot(rows[m], inner[m][...]) for m in range(2)]
                raw = [dot_nt(rows[m], small[m]) for m in range(2)]
                yield 3 * Q, [jnp.concatenate([v, jnp.zeros((UNIT, 128), F32)], axis=1) for v in raw]

        def channels(ref, at):
            rows = [ref[pl.ds(pl.multiple_of(n * UNIT + at * 96, 16), 96), :] for n in range(2)]
            return jnp.concatenate(rows, axis=0)

        def blocks(core, offset):
            for start, parts in products(core, offset):
                value = parts[0] + parts[1]
                for n in range(value.shape[1] // BLOCK):
                    at = start + n * BLOCK
                    yield slice(at, at + BLOCK), value[:, n * BLOCK : (n + 1) * BLOCK]

        def shifted(cols):
            return slice(cols.start - BACK, cols.stop - BACK)

        def run(core):
            if stage == 0:
                for cols, value in blocks(core, 2):
                    if cols.start < BACK:
                        near[0][:, cols] = value.astype(BF16)
                    else:
                        near[1][:, shifted(cols)] = value.astype(BF16)
                    if cols.stop == BACK:
                        moves[0].start()
                moves[1].start()
            elif stage == 1:
                (from_before, from_after), (to_after, to_before) = came, near
                for cols, value in blocks(core, 1):
                    if cols.start < BACK:
                        value = value + from_before[:, cols].astype(F32)
                    to_after[:, cols] = value.astype(BF16)
                moves[0].start()
                for cols, value in blocks(core, 3):
                    if cols.start >= BACK:
                        value = value + from_after[:, shifted(cols)].astype(F32)
                    to_before[:, cols] = value.astype(BF16)
                moves[1].start()
            else:
                from_before, from_after = came
                for cols, value in blocks(core, 0):
                    value = value + from_before[:, cols].astype(F32) + from_after[:, cols].astype(F32)
                    total[:, :, cols] = value.reshape(4, 96, BLOCK)
                here = y if core == 0 else z
                for offset in range(1, 4):
                    near[offset][...] = total[lax.rem(here + offset, 4)].astype(BF16)
                    moves[offset].start()
                near[0][...] = total[here]
                moves[0].start()

        for core in range(2):
            @pl.when(p == core)
            def _():
                loads = copies(core)
                for load in loads:
                    load.start()
                for load in loads:
                    load.wait()
                run(core)

        for move in moves:
            move.wait()

    if stage == 0:
        outs = [((UNIT, BACK), BF16)] * 2
    elif stage == 1:
        outs = [((UNIT, WIDE), BF16)] * 2
    else:
        outs = [((96, WIDE), F32)] + [((96, WIDE), BF16)] * 3
    scratch = [pltpu.VMEM(shape, dtype) for shape, dtype in outs]
    if stage == 2:
        scratch += [pltpu.VMEM((4, 96, WIDE), F32)]
        outs = [((2, *shape), dtype) for shape, dtype in outs]
    scratch += [
        pltpu.VMEM((2, T, Q), BF16),
        pltpu.VMEM((2, 2, 4, 96, T), BF16),
        pltpu.VMEM((2, T, D), BF16),
        pltpu.SemaphoreType.DMA((8,)),
    ]
    ins += [(a, None) for a in arrived]
    return kernel_call(body, ins, outs, scratch, f"grad_{layer}_{stage}", placed=len(outs), onto=onto)


def cut_rows(own, one, two, three):
    def body(own, one, two, three, mine, other, total):
        _, _, x = position()
        for layer in range(2):
            out = own[layer] + two[layer].astype(F32)
            out = out + (one[layer].astype(F32) + three[layer].astype(F32))
            total[...] = out.reshape(2, 48, WIDE)
            mine[layer] = total[x]
            other[layer] = total[1 - x].astype(BF16)

    outs = [((2, 48, WIDE), F32), ((2, 48, WIDE), BF16)]
    ins = [(a, None) for a in (own, one, two, three)]
    return kernel_call(body, ins, outs, [pltpu.VMEM((2, 48, WIDE), F32)], "grad_cut", 24)


def dp_index(z, y, x):
    return ((z % 4) * 4 + y % 4) * 2 + x % 2


def dp_pairs(move):
    places = [(z, y, x) for z in range(4) for y in range(4) for x in range(2)]
    return [(dp_index(*at), dp_index(*move(*at))) for at in places]


def along(axis, offset):
    if axis == "z":
        return dp_pairs(lambda z, y, x: (z + offset, y, x))
    if axis == "y":
        return dp_pairs(lambda z, y, x: (z, y + offset, x))
    return dp_pairs(lambda z, y, x: (z, y, x + offset))


def pair_shift(value, axes, distance):
    flip = {"z": lambda z, y, x: (z ^ distance, y, x), "y": lambda z, y, x: (z, y ^ distance, x)}
    pairs = [(32 * p + a, 32 * p + b) for p in range(2) for a, b in dp_pairs(flip[axes[p]])]
    return lax.ppermute(value, ("pipe", "dp"), pairs)


def shift(value, axis, offset):
    return lax.ppermute(value, "dp", along(axis, offset))


def core_shift(value, axes, offset):
    pairs = [(32 * p + a, 32 * p + b) for p in range(2) for a, b in along(axes[p], offset)]
    return lax.ppermute(value, ("pipe", "dp"), pairs)


def swap(value, axis="pipe"):
    return lax.ppermute(value, axis, [(0, 1), (1, 0)])


def add_halves(a, b):
    return (a.astype(F32) + b.astype(F32)).astype(BF16)


def scatter(layer, stage, args, arrived=()):
    sent = weight_stage(stage, layer, *args, arrived)
    return core_shift(sent[0], "zy", 1), core_shift(sent[1], "zy", 3)


def sum_rows(own, got):
    def body(own, got, mine, other, state_0, state_1, total):
        p = lax.axis_index("pipe")
        total[...] = own[...] + got[...].astype(F32)
        mine[...] = total[p]
        other[...] = total[1 - p]
        state_0[...] = total[0, :, 3 * Q :]
        state_1[...] = total[1, :, 3 * Q :]

    ins = [(own, None), (got, None)]
    outs = [((48, WIDE), F32), ((48, WIDE), F32), ((48, 256), F32), ((48, 256), F32)]
    scratch = [pltpu.VMEM((2, 48, WIDE), F32)]
    mine, other, state_0, state_1 = kernel_call(body, ins, outs, scratch, "grad_rows", 16)
    shared_0 = lax.ppermute(state_0, ("pipe", "tensor"), [(0, 1), (1, 0)])
    shared_1 = lax.ppermute(state_1, ("pipe", "tensor"), [(0, 3), (1, 2)])
    return mine, swap(other), shared_0, shared_1


def finish_weights(mine, got, shared_0, shared_1):
    def body(mine, got, shared_0, shared_1, main, state, step, out):
        p = lax.axis_index("pipe")
        for layer, (first, second, shared) in enumerate(((mine, got, shared_0), (got, mine, shared_1))):
            @pl.when(p == layer)
            def _():
                main[:, 0, :] = first[:, : 2 * Q]
                main[:, 1, :Q] = first[:, 2 * Q : 3 * Q]
                main[:, 1, Q:] = second[:, 2 * Q : 3 * Q]
                state[...] = first[:, 3 * Q :] + shared[...]
                step[...] = second[:, 3 * Q : 3 * Q + 2 * HQ]
                out[...] = second[:, : 2 * Q]

    ins = [(a, None) for a in (mine, got, shared_0, shared_1)]
    outs = [((48, 2, D), F32), ((48, 256), F32), ((48, 2 * HQ), F32), ((48, D), F32)]
    return kernel_call(body, ins, outs, (), "grad_finish", 24)


def join_sums(layer, m, keep, got):
    def body(keep, got, out):
        out[...] = add_halves(keep[...], got[...])

    return kernel_call(body, [(keep, None), (got, None)], [(keep.shape, BF16)], (), f"add_{layer}_{m}", 16)[0]


def sum_packs(packs):
    def body(*refs):
        out = refs[8]
        for layer in range(2):
            one, gain_one, two, gain_two = refs[4 * layer : 4 * layer + 4]
            out[layer] = one[...] + two[...]
            out[layer, 13:15, :] = gain_one[0:2, :] + gain_two[0:2, :]

    ins = [(a, None) for layer in packs for a in layer]
    return kernel_call(body, ins, [((2, 16, Q), F32)], (), "pack_sum", 16)[0]


def add_neighbour(pack, arrived):
    def body(pack, arrived, out, rows):
        out[...] = pack[...] + arrived[...]
        rows[...] = out[:, 8:16, :]

    return kernel_call(body, [(pack, None), (arrived, None)], [((2, 16, Q), F32), ((2, 8, Q), F32)], (), "pack_x", 16)


def add_shared_rows(pack, rows):
    def body(pack, rows, out):
        out[...] = pack[...]
        for layer in range(2):
            out[layer, 8:15, :] = pack[layer, 8:15, :] + rows[layer, :7, :]

    return kernel_call(body, [(pack, None), (rows, None)], [((2, 16, Q), F32)], (), "pack_shared", 16)[0]


def pack_quarters(pack, arrived):
    def body(pack, arrived, out):
        p = lax.axis_index("pipe")
        out[p] = pack[p]
        out[1 - p] = arrived[p]

    return kernel_call(body, [(pack, None), (arrived, None)], [((2, 16, Q), F32)], (), "pack_quarters", 16)[0]


def finish_packs(pair):
    def body(pair, norm, taps, state, bias, log, skip, gain):
        owner = (iota((Q, 128), 0) // 64 == iota((Q, 128), 1)).astype(F32)
        both = pair[0] + pair[1]
        norm[:, :Q] = both[13:14]
        norm[:, Q:] = both[14:15]
        state[...] = both[8:13, :256]
        for n in range(2):
            taps[:, n * Q : (n + 1) * Q] = pair[n, 0:5]
            gain[:, n * Q : (n + 1) * Q] = pair[n, 5:6]
        sums = [
            lax.dot_general(
                pair[n, 0:8],
                owner,
                (((1,), (0,)), ((), ())),
                precision=lax.Precision.HIGHEST,
                preferred_element_type=F32,
            )
            for n in range(2)
        ]
        skip[...] = jnp.concatenate([sums[0][6:7, :HQ], sums[1][6:7, :HQ]], axis=1)
        bias[...] = jnp.concatenate([pair[0, 7:8, :HQ], pair[1, 7:8, :HQ]], axis=1)
        log[...] = jnp.concatenate([pair[0, 7:8, 128 : 128 + HQ], pair[1, 7:8, 128 : 128 + HQ]], axis=1)

    outs = [(1, D), (5, D), (5, 256), (1, 2 * HQ), (1, 2 * HQ), (1, 2 * HQ), (1, D)]
    return kernel_call(body, [(pair, None)], [(s, F32) for s in outs], (), "pack_finish", 16)


def add_two(a, b, name):
    def body(a, b, out):
        out[...] = a[...] + b[...]

    return kernel_call(body, [(a, None), (b, None)], [(a.shape, F32)], (), name, 16)[0]


def assemble_states(lower, upper):
    def body(l0, l1, uo0, uo1, ur0, ur1, out):
        p = lax.axis_index("pipe")
        for m, (low, own, other) in enumerate(((l0, uo0, ur0), (l1, uo1, ur1))):
            @pl.when(p == 0)
            def _():
                out[m] = low[...]

            @pl.when(p == 1)
            def _():
                join(p, own, other, out.at[m], slice(0, D))

    arrays = list(lower) + [u[0] for u in upper] + [u[1] for u in upper]
    return kernel_call(body, [(a, None) for a in arrays], [((2, T, D), BF16)], (), "hidden_states", 24)[0]


def assemble_grads(lower, upper):
    def body(lo0, lo1, lr0, lr1, u0, u1, out):
        p = lax.axis_index("pipe")
        for m, (own, other, up) in enumerate(((lo0, lr0, u0), (lo1, lr1, u1))):
            @pl.when(p == 0)
            def _():
                join(p, own, other, out.at[m], slice(0, D))

            @pl.when(p == 1)
            def _():
                out[m] = up[...]

    arrays = [l[0] for l in lower] + [l[1] for l in lower] + list(upper)
    return kernel_call(body, [(a, None) for a in arrays], [((2, T, D), BF16)], (), "input_grads", 24)[0]


def local(
    hidden,
    segments,
    cotangent,
    norm_gain,
    main_w,
    state_w,
    step_w,
    conv_main,
    conv_state,
    step_bias,
    decay_log,
    skip_scale,
    gate_gain,
    out_w,
):
    ORDER.clear()
    COST[0] = 30
    p = lax.axis_index("pipe")
    hidden = hidden.reshape(2, T, D)
    cotangent = cotangent.reshape(2, T, D)
    seg = segments.reshape(2, 1, T)

    out_own, state_own = out_w[0], state_w[0]
    state_got = swap(state_own)
    wd = jnp.transpose(step_w[0], (1, 0))
    small = [norm_gain, conv_main[0], conv_state[0], step_bias, decay_log, skip_scale, gate_gain, wd]
    main_sent, main_own = kernel_call(
        slice_kernel,
        [(main_w[0], HBM)],
        [((D, 2, Q), BF16), ((D, 2, Q), BF16)],
        [pltpu.SemaphoreType.DMA((2,))],
        name="slices",
        limit=16,
        placed=2,
    )
    par_own, par_sent, wd_own, wd_sent = kernel_call(
        pack_kernel,
        [(a, None) for a in small],
        [((32, Q), F32), ((32, Q), F32), ((16, D), BF16), ((16, D), BF16)],
        name="pack",
        limit=16,
    )
    main_got = swap(jnp.transpose(main_sent, (1, 0, 2)))
    out_got = swap(lax.dynamic_slice(out_own, ((1 - p) * Q, 0), (Q, D)))
    main_own = jnp.transpose(main_own, (1, 0, 2))
    pars = (par_own, swap(par_sent))
    wds = (wd_own, swap(wd_sent))
    wss = (state_own, state_got)
    mains = (main_own, main_got)
    wos = (out_own, out_got)

    both = lambda: [None, None]
    projected, turned, mixes, chips, sums, result = ([both(), both()] for _ in range(6))
    gates, tails, smalls, back, back_sums, grads, packs = ([both(), both()] for _ in range(7))
    lower_a = both()

    def forward_project(layer, m):
        xs = hidden if layer == 0 else result[0][m]
        projected[layer][m] = project(layer, m, xs, pars, wds, wss, mains)

    def forward_mix(layer, m):
        _, pre, spre, raw = projected[layer][m][:4]
        mixed, inner, send, keep = mix(layer, m, pre, spre, raw, seg, pars, wos)
        mixes[layer][m] = (mixed, inner)
        chips[layer][m] = (keep, swap(send))

    def forward_add(layer, m):
        sums[layer][m] = join_sums(f"out_{layer}", m, *chips[layer][m])

    def forward_finish(layer, m):
        sums[layer][m] = (sums[layer][m], swap(sums[layer][m], "tensor"))
        if layer == 0:
            done = finish_forward(0, m, *sums[0][m], hidden, None)
        else:
            done = finish_forward(1, m, *sums[1][m], result[0][m][0], cotangent)
        result[layer][m] = (done, swap(done))

    def forward_turn(layer, m):
        turned[layer][m] = turn(layer, m, projected[layer][m][0])

    def backward_gate(layer, m):
        pre = projected[layer][m][1]
        mixed, inner = mixes[layer][m]
        if layer == 1:
            outs = gate_back(1, m, cotangent, result[1][m], pre, mixed, inner, pars, wos)
        else:
            *outs, lower_a[m] = gate_back(0, m, grads[1][m], result[0][m], pre, mixed, inner, pars, wos)
        gates[layer][m] = outs

    def backward_mix(layer, m):
        _, pre, spre, raw = projected[layer][m][:4]
        mixed, inner = mixes[layer][m]
        d_comb, cross, pack_a = (gates[layer][m][n] for n in (1, 3, 4))
        tails[layer][m] = mix_back(layer, m, d_comb, inner, pre, spre, raw, seg, mixed, cross, pack_a, pars)
        smalls[layer][m] = swap(tails[layer][m][2])
        packs[layer][m] = [tails[layer][m][4]]

    def backward_project(layer, m):
        d_inner, d_small, _, d_raw, _ = tails[layer][m]
        x = hidden if layer == 0 else projected[1][m][4]
        outs = project_back(layer, m, gates[layer][m][0], d_inner, d_small, d_raw, x, wds, wss, mains)
        send, keep, gain = outs
        packs[layer][m].append(gain)
        back[layer][m] = (keep, swap(send))

    def backward_add(layer, m):
        back_sums[layer][m] = join_sums(f"in_{layer}", m, *back[layer][m])

    def backward_finish(layer, m):
        back_sums[layer][m] = (back_sums[layer][m], swap(back_sums[layer][m], "tensor"))
        if layer == 1:
            done = finish_back(1, m, *back_sums[1][m], result[0][m][0], cotangent, pars, sums[0][m])
        else:
            done = finish_back(0, m, *back_sums[0][m], hidden, grads[1][m][0], pars, None)
        grads[layer][m] = (done, swap(done))

    def operands(layer):
        lefts = [turned[layer][m].reshape(4, 4, 96, T) for m in range(2)]
        groups = []
        for m in range(2):
            d_gate, _, scaled_t = gates[layer][m][:3]
            cot = cotangent if layer == 1 else lower_a[m]
            groups.append(
                {
                    "near": (tails[layer][m][0], tails[layer][m][2], smalls[layer][m]),
                    "far": (d_gate, scaled_t.reshape(2, 4, 96, T), cot),
                }
            )
        return lefts, groups

    forward_project(0, 0)
    forward_mix(0, 0)
    forward_project(0, 1)
    forward_add(0, 0)
    forward_mix(0, 1)
    forward_turn(0, 0)
    forward_add(0, 1)
    forward_finish(0, 0)
    forward_turn(0, 1)
    forward_project(1, 0)
    forward_mix(1, 0)
    forward_finish(0, 1)
    forward_add(1, 0)
    forward_project(1, 1)
    forward_mix(1, 1)
    forward_turn(1, 0)
    forward_add(1, 1)
    forward_finish(1, 0)
    forward_turn(1, 1)
    backward_gate(1, 0)
    backward_mix(1, 0)
    forward_finish(1, 1)
    backward_project(1, 0)
    meanwhile(smalls[1][0])
    backward_gate(1, 1)
    backward_add(1, 0)
    backward_mix(1, 1)
    backward_project(1, 1)
    backward_finish(1, 0)
    backward_add(1, 1)
    upper = operands(1)
    upper_moved = scatter(1, 0, upper)
    backward_gate(0, 0)
    backward_mix(0, 0)
    backward_finish(1, 1)
    meanwhile(smalls[0][0])
    COST[0] = 2
    upper_moved = scatter(1, 1, upper, upper_moved)
    backward_gate(0, 1)
    backward_mix(0, 1)
    backward_project(0, 0)
    lower = operands(0)
    lower_moved = scatter(0, 0, lower)
    backward_add(0, 0)
    backward_project(0, 1)
    pack = sum_packs([packs[layer][0] + packs[layer][1] for layer in range(2)])
    pack_got = shift(pack, "x", 1)
    done = weight_stage(2, 1, *upper, upper_moved)
    pack, pack_rows = add_neighbour(pack, pack_got)
    pack_rows = swap(pack_rows, "tensor")
    backward_add(0, 1)
    COST[0] = 1
    lower_moved = scatter(0, 1, lower, lower_moved)
    pack = add_shared_rows(pack, pack_rows)
    pack_got = swap(pack)
    states = assemble_states([projected[1][m][4] for m in range(2)], result[1])
    pack = pack_quarters(pack, pack_got)
    pack_got = pair_shift(pack, "zy", 2)
    pack = add_two(pack, pack_got, "pack_first")
    done = weight_stage(2, 0, *lower, lower_moved, done)
    done = [done[0]] + [core_shift(done[n], "yz", n) for n in (1, 2, 3)]
    backward_finish(0, 0)
    backward_finish(0, 1)
    input_grads = assemble_grads(grads[0], lower_a)
    pack_got = pair_shift(pack, "zy", 1)
    own, sent = cut_rows(*done)
    sent = core_shift(sent, "xx", 1)
    pack = add_two(pack, pack_got, "pack_first")
    pack = add_two(pack, pair_shift(pack, "yz", 2), "pack_second")
    pack = add_two(pack, pair_shift(pack, "yz", 1), "pack_second")
    done = sum_rows(own, sent)
    outs = finish_packs(pack)
    grad_norm, grad_taps, grad_state_taps, grad_bias, grad_log, grad_skip, grad_gain = outs
    grad_main, grad_state, grad_step, grad_out = finish_weights(*done)
    return (
        states.reshape(1, 2, 1, T, D),
        input_grads.reshape(1, 2, 1, T, D),
        grad_norm,
        grad_main[None],
        grad_state[None],
        grad_step[None],
        grad_taps[None],
        grad_state_taps[None],
        grad_bias,
        grad_log,
        grad_skip,
        grad_gain,
        grad_out[None],
    )


def solution(mesh):
    in_specs = (
        P(None, "dp", None, None),
        P(None, "dp", None),
        P(None, "dp", None, None),
        P("pipe", None),
        P("pipe", None, None, "tensor"),
        P("pipe", None, None),
        P("pipe", None, "tensor"),
        P("pipe", None, "tensor"),
        P("pipe", None, None),
        P("pipe", "tensor"),
        P("pipe", "tensor"),
        P("pipe", "tensor"),
        P("pipe", "tensor"),
        P("pipe", "tensor", None),
    )
    out_specs = (
        P("pipe", None, "dp", None, None),
        P("pipe", None, "dp", None, None),
        P("pipe", None),
        P("pipe", "dp", None, "tensor"),
        P("pipe", "dp", None),
        P("pipe", "dp", "tensor"),
        P("pipe", None, "tensor"),
        P("pipe", None, None),
        P("pipe", "tensor"),
        P("pipe", "tensor"),
        P("pipe", "tensor"),
        P("pipe", "tensor"),
        P("pipe", ("tensor", "dp"), None),
    )
    return jax.shard_map(local, mesh=mesh, in_specs=in_specs, out_specs=out_specs, check_vma=False)
```

```python
import jax
import jax.numpy as jnp
from jax import lax
from jax.experimental import pallas as pl
from jax.experimental.pallas import tpu as pltpu
from jax.sharding import PartitionSpec as P

F32 = jnp.float32
BF16 = jnp.bfloat16
EPS = 1e-05
D = 1536
Q = 768
HQ = 12
DI = 3072
T = 256
HALF = 128
EXT = D + 128
NEG = -1e30
PAIR = Q + 384


def dot(a, b):
    return lax.dot_general(a, b, (((1,), (0,)), ((), ())), preferred_element_type=F32)


def dot_nt(a, b):
    return lax.dot_general(a, b, (((1,), (1,)), ((), ())), preferred_element_type=F32)


def sigmoid(v):
    return 0.5 * jnp.tanh(0.5 * v) + 0.5


def softplus(v):
    e = jnp.exp(-jnp.abs(v))
    small = e * (1.0 - e * (0.5 - e * (1.0 / 3.0 - e * 0.25)))
    return jnp.maximum(v, 0.0) + jnp.where(e < 0.01, small, jnp.log(1.0 + e))


def iota(shape, dim):
    return lax.broadcasted_iota(jnp.int32, shape, dim)


def pieces(v):
    high = v.astype(BF16).astype(F32)
    mid = (v - high).astype(BF16).astype(F32)
    return high, mid, (v - high - mid).astype(BF16).astype(F32)


def lanes_of(v, first):
    lane = iota((v.shape[0], 128), 1)
    out = jnp.zeros((v.shape[0], 128), F32)
    for k, part in enumerate(pieces(v)):
        out = out + jnp.where(lane == first + k, part, 0.0)
    return out


def scalar_at(ext, first, count=3):
    lane = iota(ext.shape, 1)
    keep = (lane >= first) & (lane < first + count)
    return jnp.sum(jnp.where(keep, ext, 0.0), axis=1, keepdims=True)


def half_rows(which):
    return pl.ds(pl.multiple_of(which * HALF, HALF), HALF)


def whole(shape):
    return pl.BlockSpec(shape, lambda i: (0,) * len(shape))


def part(shape, at):
    return pl.BlockSpec(shape, lambda i: at)


ANY = pl.BlockSpec(memory_space=pl.ANY)
HBM = pl.BlockSpec(memory_space=pltpu.HBM)


COST = [30]
ORDER = []


def kernel_call(body, ins, outs, scratch=(), name=None, limit=22, after=(), placed=0, onto=()):
    after = tuple(ORDER) + tuple(after)
    if after or onto:
        inner, count, skip = body, len(ins), len(after) + len(onto)
        body = lambda *refs: inner(*refs[:count], *refs[count + skip :])
        ins = list(ins) + [(a, ANY) for a in after] + [(a, HBM) for a in onto]
    arrays = [a for a, _ in ins]
    specs = [whole(a.shape) if s is None else s for a, s in ins]
    results = pl.pallas_call(
        body,
        grid=(1,),
        in_specs=specs,
        out_specs=[whole(s) for s, _ in outs[: len(outs) - placed]] + [HBM] * placed,
        out_shape=[jax.ShapeDtypeStruct(s, d) for s, d in outs],
        scratch_shapes=list(scratch),
        input_output_aliases={len(ins) - len(onto) + n: len(outs) - placed + n for n in range(len(onto))},
        compiler_params=pltpu.CompilerParams(vmem_limit_bytes=limit * 1024 * 1024),
        cost_estimate=pl.CostEstimate(flops=int(COST[0] * 10**9), bytes_accessed=1 << 10, transcendentals=0),
        name=name,
    )(*arrays)
    ORDER[:] = [min(results, key=lambda r: r.size * r.dtype.itemsize)]
    return results


def meanwhile(*arrays):
    ORDER.extend(arrays)


def start_either(mine, own, other, dst, sem):
    @pl.when(mine)
    def _():
        pltpu.make_async_copy(own, dst, sem).start()

    @pl.when(jnp.logical_not(mine))
    def _():
        pltpu.make_async_copy(other, dst, sem).start()


def wait_for(src, dst, sem):
    pltpu.make_async_copy(src, dst, sem).wait()


def pick(mine, own, other, dst):
    @pl.when(mine)
    def _():
        dst[...] = own[...]

    @pl.when(jnp.logical_not(mine))
    def _():
        dst[...] = other[...]


def join(p, own, other, dst, columns=slice(None)):
    dst[half_rows(p), :] = own[:, columns].astype(dst.dtype)
    dst[half_rows(1 - p), :] = other[:, columns].astype(dst.dtype)


TAPS, GATE, NORM, STAPS, SKIP, HEAD = 0, 5, 6, 8, 13, 16


def slice_kernel(main, sent, mine, sem):
    p = lax.axis_index("pipe")
    far = pl.ds(pl.multiple_of((1 - p) * Q, Q), Q)
    near = pl.ds(pl.multiple_of(p * Q, Q), Q)
    moves = [
        pltpu.make_async_copy(main.at[:, :, far], sent, sem.at[0]),
        pltpu.make_async_copy(main.at[:, :, near], mine, sem.at[1]),
    ]
    for move in moves:
        move.start()
    for move in moves:
        move.wait()


def pack_kernel(ng, cm, cs, sb, dl, ss, gg, wd, own, other, wd_own, wd_other):
    p = lax.axis_index("pipe")
    for target, wd_target, which in ((own, wd_own, p), (other, wd_other, 1 - p)):
        lanes = pl.ds(pl.multiple_of(which * Q, Q), Q)
        target[...] = jnp.zeros(target.shape, F32)
        target[TAPS : TAPS + 5, :] = cm[:, lanes]
        target[GATE : GATE + 1, :] = gg[:, lanes]
        target[NORM : NORM + 1, :] = ng[:, :Q]
        target[NORM + 1 : NORM + 2, :] = ng[:, Q:]
        target[STAPS : STAPS + 5, :256] = cs[...]
        second = which == 1
        head = [jnp.where(second, v[:, HQ : 2 * HQ], v[:, :HQ]) for v in (sb, dl, ss)]
        row = jnp.concatenate([head[2], jnp.zeros((1, 128 - HQ), F32)], axis=1)
        column = jnp.broadcast_to(row, (128, 128)).T
        owner = iota((16, Q), 1) // 64 == iota((16, Q), 0)
        spread = jnp.where(owner, column[:16, :1], 0.0)
        target[SKIP : SKIP + 1, :] = jnp.sum(spread, axis=0, keepdims=True)
        rows = [jnp.concatenate([v, jnp.zeros((1, 128 - HQ), F32)], axis=1) for v in head[:2]]
        square = jnp.concatenate([rows[0], -jnp.exp(rows[1]), jnp.zeros((126, 128), F32)], axis=0)
        target[HEAD : HEAD + 16, :128] = square.T[:16, :]
        wide = wd[...].astype(F32)
        chosen = jnp.where(second, wide[HQ:, :], wide[:HQ, :])
        wd_target[...] = jnp.concatenate([chosen, jnp.zeros((4, D), F32)], axis=0).astype(BF16)


def project_body(layer, p, x, par, wd, ws, w_scr, waits, outs):
    rounded, pre, spre, raw = outs
    factor = lax.rsqrt(jnp.mean(x * x, axis=1, keepdims=True) + EPS)
    scaled = x * factor
    for c in range(2):
        cols = slice(c * Q, (c + 1) * Q)
        normed = scaled[:, cols] * par[NORM + c : NORM + c + 1, :]
        rounded[:, cols] = normed.astype(BF16)
    raw[...] = dot_nt(wd[...], rounded[...])
    waits[0]()
    spre[...] = dot(rounded[...], ws[...])
    waits[1]()
    for u in range(2):
        for c in range(3):
            cols = slice(c * 256, (c + 1) * 256)
            pre[:, u * Q + c * 256 : u * Q + (c + 1) * 256] = dot(rounded[...], w_scr[u, :, cols])


def project(layer, m, xs, pars, wds, wss, ws_main):
    first = layer == 0

    def body(*refs):
        xr = refs[: 1 if first else 2]
        par_o, par_r, wd_o, wd_r, ws_o, ws_r, wm_o, wm_r = refs[len(xr) : len(xr) + 8]
        rest = refs[len(xr) + 8 :]
        outs, scr = rest[: 4 if first else 5], rest[4 if first else 5 :]
        par, wd, ws, w_scr, sem = scr
        p = lax.axis_index("pipe")
        mine = p == layer
        start_either(mine, ws_o, ws_r, ws, sem.at[0])
        start_either(mine, wm_o, wm_r, w_scr, sem.at[1])
        pick(mine, par_o, par_r, par)
        pick(mine, wd_o, wd_r, wd)
        if first:
            x = xr[0][0].astype(F32)
        else:
            join(p, xr[0], xr[1], outs[4], slice(0, D))
            x = outs[4][...].astype(F32)
        waits = (
            lambda: wait_for(ws_r, ws, sem.at[0]),
            lambda: wait_for(wm_r, w_scr, sem.at[1]),
        )
        project_body(layer, p, x, par, wd, ws, w_scr, waits, outs[:4])

    if first:
        ins = [(xs, part((1, T, D), (m, 0, 0)))]
    else:
        ins = [(xs[0], None), (xs[1], None)]
    ins += [(a, None) for a in pars] + [(a, None) for a in wds]
    ins += [(a, ANY) for a in wss] + [(a, ANY) for a in ws_main]
    outs = [((T, D), BF16), ((T, D), F32), ((T, T), F32), ((16, T), F32)]
    if not first:
        outs.append(((T, D), BF16))
    scratch = [
        pltpu.VMEM((32, Q), F32),
        pltpu.VMEM((16, D), BF16),
        pltpu.VMEM((D, 256), BF16),
        pltpu.VMEM((2, D, Q), BF16),
        pltpu.SemaphoreType.DMA((2,)),
    ]
    return kernel_call(body, ins, outs, scratch, f"project_{layer}_{m}")


def turn(layer, m, rounded):
    def body(rounded, out):
        for c in range(6):
            cols = slice(c * 256, (c + 1) * 256)
            out[cols, :] = rounded[:, cols].T

    return kernel_call(body, [(rounded, None)], [((D, T), BF16)], (), f"turn_{layer}_{m}", 16)[0]


def document_ids(seg_ref):
    row = jnp.broadcast_to(seg_ref[0].astype(F32), (T, T))
    return row.T, row


def same_document(by_token, lag):
    position = iota((T, T), 0)
    earlier = pltpu.roll(by_token, lag, 0)
    return jnp.where((earlier == by_token) & (position >= lag), 1.0, 0.0)


def convolve(values, taps, same):
    out = taps[4:5] + taps[3:4] * values
    for lag in range(1, 4):
        out = out + taps[3 - lag : 4 - lag] * (pltpu.roll(values, lag, 0) * same[lag])
    return out


def convolve_back(d_sum, values, taps, same):
    d_values = taps[3:4] * d_sum
    rows = [None] * 5
    rows[4] = jnp.sum(d_sum, axis=0, keepdims=True)
    rows[3] = jnp.sum(d_sum * values, axis=0, keepdims=True)
    for lag in range(1, 4):
        held = d_sum * same[lag]
        d_values = d_values + taps[3 - lag : 4 - lag] * pltpu.roll(held, T - lag, 0)
        moved = pltpu.roll(values, lag, 0)
        rows[3 - lag] = jnp.sum(held * moved, axis=0, keepdims=True)
    return d_values, jnp.concatenate(rows, axis=0)


def step_sizes(raw, par):
    before = raw[...] + par[HEAD : HEAD + 16, 0:1]
    step = softplus(before)
    total = step * par[HEAD : HEAD + 16, 1:2]
    lane = iota(total.shape, 1)
    shift = 1
    while shift < T:
        total = total + jnp.where(lane >= shift, pltpu.roll(total, shift, 1), 0.0)
        shift *= 2
    return before, step, total


def columns_of(rows):
    return jnp.concatenate([rows, jnp.zeros((112, T), F32)], axis=0).T


def mix(layer, m, pre, spre, raw, seg, pars, wos):
    def body(pre, spre, raw, seg, par_o, par_r, wo_o, wo_r, *rest):
        mixed, inner_out, send, keep, par, wo, gs, u_scr, sem = rest
        p, t = lax.axis_index("pipe"), lax.axis_index("tensor")
        mine = p == layer
        own = wo_o.at[pl.ds(pl.multiple_of(p * Q, Q), Q), :]
        start_either(mine, own, wo_r, wo, sem)
        pick(mine, par_o, par_r, par)
        by_token, by_row = document_ids(seg)
        same = [None] + [same_document(by_token, lag) for lag in range(1, 4)]
        allowed = (by_token == by_row) & (iota((T, T), 0) >= iota((T, T), 1))
        state = convolve(spre[...], par[STAPS : STAPS + 5, :256], same)
        state = (state * sigmoid(state)).astype(BF16)
        crossed = dot_nt(state[:, 128:], state[:, :128])
        _, step, total = step_sizes(raw, par)
        total_t = columns_of(total)
        low = iota((T, 128), 1) < 64
        squares = jnp.zeros((T, 1), F32)
        for g in range(3):
            cols = slice(g * 256, (g + 1) * 256)
            summed = convolve(pre[:, Q + g * 256 : Q + (g + 1) * 256], par[TAPS : TAPS + 5, cols], same)
            inner = (summed * sigmoid(summed)).astype(BF16)
            inner_out[:, cols] = inner
            for pair in range(2):
                at = slice(g * 256 + pair * 128, g * 256 + (pair + 1) * 128)
                values = inner[:, pair * 128 : (pair + 1) * 128]
                out = None
                for k in range(2):
                    h = g * 4 + pair * 2 + k
                    gap = total_t[:, h : h + 1] - total[h : h + 1, :]
                    decay = jnp.exp(jnp.where(allowed, gap, NEG))
                    mixing = (crossed * decay * step[h : h + 1, :]).astype(BF16)
                    chosen = jnp.where(low if k == 0 else ~low, values, jnp.zeros_like(values))
                    term = dot(mixing, chosen)
                    out = term if out is None else out + term
                mixed[:, at] = out
            combined = mixed[:, cols] + par[SKIP : SKIP + 1, cols] * inner.astype(F32)
            gate = pre[:, cols]
            gated = combined * (gate * sigmoid(gate))
            squares = squares + jnp.sum(gated * gated, axis=1, keepdims=True)
            gs[:, cols] = (gated * par[GATE : GATE + 1, cols]).astype(BF16)
        wait_for(wo_r, wo, sem)
        for c in range(3):
            cols = slice(c * 512, (c + 1) * 512)
            u_scr[:, cols] = dot(gs[...], wo[:, cols]).astype(BF16)
        u_scr[:, D:] = lanes_of(squares, 3 * (2 * p + t)).astype(BF16)
        send[...] = u_scr[half_rows(1 - p), :]
        keep[...] = u_scr[half_rows(p), :]

    ins = [(pre, None), (spre, None), (raw, None), (seg, part((1, 1, T), (m, 0, 0)))]
    ins += [(a, None) for a in pars] + [(a, ANY) for a in wos]
    outs = [((T, Q), F32), ((T, Q), BF16), ((HALF, EXT), BF16), ((HALF, EXT), BF16)]
    scratch = [
        pltpu.VMEM((32, Q), F32),
        pltpu.VMEM((Q, D), BF16),
        pltpu.VMEM((T, Q), BF16),
        pltpu.VMEM((T, EXT), BF16),
        pltpu.SemaphoreType.DMA,
    ]
    return kernel_call(body, ins, outs, scratch, f"mix_{layer}_{m}")


def finish_forward(layer, m, chip, arrived, x, cot):
    def body(chip, arrived, x, *rest):
        p = lax.axis_index("pipe")
        out = rest[-1]
        total = chip[:, :D].astype(F32) + arrived[:, :D].astype(F32)
        ext = chip[:, D:].astype(F32) + arrived[:, D:].astype(F32)
        factor = lax.rsqrt(jnp.sum(ext, axis=1, keepdims=True) / DI + EPS)
        if layer == 0:
            before = x[0, half_rows(p), :].astype(F32)
        else:
            before = x[:, :D].astype(F32)
        out[:, :D] = (before + factor * total).astype(BF16)
        tail = lanes_of(factor, 0)
        if layer == 1:
            a = rest[0][0, half_rows(p), :].astype(F32)
            pull = factor * factor * factor * (jnp.sum(a * total, axis=1, keepdims=True) / DI)
            tail = tail + lanes_of(pull, 3)
        out[:, D:] = tail.astype(BF16)

    ins = [(chip, None), (arrived, None)]
    if layer == 0:
        ins += [(x, part((1, T, D), (m, 0, 0)))]
    else:
        ins += [(x, None), (cot, part((1, T, D), (m, 0, 0)))]
    return kernel_call(body, ins, [((HALF, EXT), BF16)], (), f"finish_out_{layer}_{m}", 16)[0]


def gate_back(layer, m, a, scalars, pre, mixed, inner, pars, wos):
    lower = layer == 0

    def body(*refs):
        if lower:
            a_o, a_r, s_o, s_r = refs[:4]
            refs = refs[4:]
        else:
            a_f, s_o, s_r = refs[:3]
            refs = refs[3:]
        pre, mixed, inner, par_o, par_r, wo_o, wo_r = refs[:7]
        d_gate, d_comb, scaled_t, cross, pack = refs[7:12]
        refs = refs[12:]
        if lower:
            a_all = refs[0]
            refs = refs[1:]
        par, wo, ext, ext2, sem = refs
        p = lax.axis_index("pipe")
        mine = p == layer
        own = wo_o.at[pl.ds(pl.multiple_of(p * Q, Q), Q), :]
        start_either(mine, own, wo_r, wo, sem)
        pick(mine, par_o, par_r, par)
        join(p, s_o, s_r, ext)
        factor = scalar_at(ext[...], 0)
        if lower:
            join(p, a_o, a_r, a_all, slice(0, D))
            join(p, a_o, a_r, ext2, slice(D, EXT))
            pull = scalar_at(ext2[...], 3)
            a = a_all[...]
        else:
            pull = scalar_at(ext[...], 3)
            a = a_f[0]
        wait_for(wo_r, wo, sem)
        pack[...] = jnp.zeros(pack.shape, F32)
        for g in range(3):
            cols = slice(g * 256, (g + 1) * 256)
            d_scaled = dot_nt(a, wo[cols, :])
            values = inner[:, cols].astype(F32)
            combined = mixed[:, cols] + par[SKIP : SKIP + 1, cols] * values
            gate = pre[:, cols]
            opened = sigmoid(gate)
            silu = gate * opened
            gated = combined * silu
            normed = gated * factor
            gain = par[GATE : GATE + 1, cols]
            scaled = (normed * gain).T.astype(BF16)
            scaled_t[cols, :] = scaled
            pack[0:1, cols] = jnp.sum(d_scaled * normed, axis=0, keepdims=True)
            d_gated = d_scaled * gain * factor - gated * pull
            d_combined = d_gated * silu
            d_comb[:, cols] = d_combined
            pack[1:2, cols] = jnp.sum(d_combined * values, axis=0, keepdims=True)
            d_open = d_gated * combined * (opened * (1.0 + gate * (1.0 - opened)))
            d_gate[:, cols] = d_open.astype(BF16)
            cross[cols, :] = jnp.where(p == 0, scaled, d_open.T.astype(BF16))

    last = part((HALF, 128), (0, D // 128))
    if lower:
        ins = [(a[0], None), (a[1], None)]
    else:
        ins = [(a, part((1, T, D), (m, 0, 0)))]
    ins += [(s, last) for s in scalars]
    ins += [(pre, part((T, Q), (0, 0))), (mixed, None), (inner, None)]
    ins += [(v, None) for v in pars] + [(v, ANY) for v in wos]
    outs = [((T, Q), BF16), ((T, Q), F32), ((Q, T), BF16), ((Q, T), BF16), ((8, Q), F32)]
    if lower:
        outs.append(((T, D), BF16))
    scratch = [
        pltpu.VMEM((32, Q), F32),
        pltpu.VMEM((Q, D), BF16),
        pltpu.VMEM((T, 128), F32),
        pltpu.VMEM((T, 128), F32),
        pltpu.SemaphoreType.DMA,
    ]
    return kernel_call(body, ins, outs, scratch, f"gate_back_{layer}_{m}")


def per_head(values):
    high = values.astype(BF16)
    rest = (values - high.astype(F32)).astype(BF16)
    owner = (iota((Q, 128), 0) // 64 == iota((Q, 128), 1)).astype(BF16)
    return dot(high, owner) + dot(rest, owner)


def mix_back(layer, m, d_comb, inner, pre, spre, raw, seg, mixed, cross, pack_a, pars):
    def body(d_comb, inner, pre, spre, raw, seg, mixed, cross, pack_a, par_o, par_r, *rest):
        d_tail, d_small, both, d_raw_out, pack, par, gap_prod, col_prod = rest
        p = lax.axis_index("pipe")
        mine = p == layer
        pick(mine, par_o, par_r, par)
        both[:Q, :] = cross[...]
        by_token, by_row = document_ids(seg)
        same = [None] + [same_document(by_token, lag) for lag in range(1, 4)]
        allowed = (by_token == by_row) & (iota((T, T), 1) >= iota((T, T), 0))
        summed_s = convolve(spre[...], par[STAPS : STAPS + 5, :256], same)
        opened_s = sigmoid(summed_s)
        state = (summed_s * opened_s).astype(BF16)
        keys, query = state[:, :128], state[:, 128:]
        crossed = dot_nt(keys, query)
        before, step, total = step_sizes(raw, par)
        total_t, step_t = columns_of(total), columns_of(step)
        low = iota((T, 128), 1) < 64
        d_cross = jnp.zeros((T, T), F32)
        pack[...] = jnp.zeros(pack.shape, F32)
        for g in range(3):
            cols = slice(g * 256, (g + 1) * 256)
            heads = []
            for pair in range(2):
                at = slice(g * 256 + pair * 128, g * 256 + (pair + 1) * 128)
                values = inner[:, at]
                d_mixed = d_comb[:, at].astype(BF16)
                d_heads = None
                for k in range(2):
                    h = g * 4 + pair * 2 + k
                    side = low if k == 0 else ~low
                    gap = total[h : h + 1, :] - total_t[:, h : h + 1]
                    decay = jnp.exp(jnp.where(allowed, gap, NEG)) * step_t[:, h : h + 1]
                    mixing = (crossed * decay).astype(BF16)
                    chosen = jnp.where(side, d_mixed, jnp.zeros_like(d_mixed))
                    d_mixing = dot_nt(values, chosen)
                    d_cross = d_cross + d_mixing * decay
                    term = dot(mixing, chosen)
                    d_heads = term if d_heads is None else d_heads + term
                heads.append(d_heads)
                along = values.astype(F32) * d_heads
                col_prod[:, at] = along
                gap_prod[:, at] = d_mixed.astype(F32) * mixed[:, at] - along
            taps = par[TAPS : TAPS + 5, cols]
            values = pre[:, cols]
            summed = convolve(values, taps, same)
            opened = sigmoid(summed)
            d_inner = jnp.concatenate(heads, axis=1) + par[SKIP : SKIP + 1, cols] * d_comb[:, cols]
            d_sum = d_inner * (opened * (1.0 + summed * (1.0 - opened)))
            d_values, rows = convolve_back(d_sum, values, taps, same)
            d_tail[:, cols] = d_values.astype(BF16)
            pack[0:5, cols] = rows
        pack[5:7, :] = pack_a[0:2, :]
        crossed_b = d_cross.astype(BF16)
        d_keys = dot(crossed_b, query)
        d_query = dot(d_cross.T.astype(BF16), keys)
        d_state = jnp.concatenate([d_keys, d_query], axis=1)
        d_sum = d_state * (opened_s * (1.0 + summed_s * (1.0 - opened_s)))
        d_values, rows = convolve_back(d_sum, spre[...], par[STAPS : STAPS + 5, :256], same)
        d_small[...] = d_values.astype(BF16)
        both[Q : Q + 256, :] = d_values.T.astype(BF16)
        pack[8:13, :256] = rows
        d_gap = per_head(gap_prod[...]).T[:16, :]
        d_col = per_head(col_prod[...]).T[:16, :]
        lane = iota(d_gap.shape, 1)
        shift = 1
        while shift < T:
            d_gap = d_gap + jnp.where(lane < T - shift, pltpu.roll(d_gap, T - shift, 1), 0.0)
            shift *= 2
        rate = par[HEAD : HEAD + 16, 1:2]
        slope = sigmoid_small(before)
        ratio = jnp.where(step > 1e-30, slope / jnp.maximum(step, 1e-30), 1.0)
        d_raw = d_col * ratio + d_gap * rate * slope
        valid = iota((16, T), 0) < HQ
        d_raw = jnp.where(valid, d_raw, 0.0)
        d_log = jnp.where(valid, d_gap * step * rate, 0.0)
        raw_t = columns_of(d_raw)
        d_raw_out[...] = raw_t.astype(BF16)
        both[Q + 256 :, :] = jnp.where(p == 1, pltpu.roll(raw_t, HQ, 1), raw_t).T.astype(BF16)
        bias_row = jnp.broadcast_to(jnp.sum(d_raw, axis=1, keepdims=True), (16, 128))
        log_row = jnp.broadcast_to(jnp.sum(d_log, axis=1, keepdims=True), (16, 128))
        square = jnp.concatenate([bias_row, jnp.zeros((112, 128), F32)], axis=0).T
        pack[7:8, 0:128] = square[0:1, :]
        square = jnp.concatenate([log_row, jnp.zeros((112, 128), F32)], axis=0).T
        pack[7:8, 128:256] = square[0:1, :]

    ins = [(d_comb, None), (inner, None), (pre, part((T, Q), (0, 1))), (spre, None), (raw, None)]
    ins += [(seg, part((1, 1, T), (m, 0, 0))), (mixed, None), (cross, None), (pack_a, None)]
    ins += [(v, None) for v in pars]
    outs = [((T, Q), BF16), ((T, T), BF16), ((PAIR, T), BF16), ((T, 128), BF16), ((16, Q), F32)]
    scratch = [pltpu.VMEM((32, Q), F32), pltpu.VMEM((T, Q), F32), pltpu.VMEM((T, Q), F32)]
    return kernel_call(body, ins, outs, scratch, f"mix_back_{layer}_{m}")


def sigmoid_small(v):
    e = jnp.exp(-jnp.abs(v))
    return jnp.where(v >= 0.0, 1.0, e) / (1.0 + e)


def project_back(layer, m, d_gate, d_inner, d_small, d_raw, x, wds, wss, ws_main):
    def body(d_gate, d_inner, d_small, d_raw, x, wd_o, wd_r, ws_o, ws_r, wm_o, wm_r, send, keep, gain, wd, ws, w_scr, acc, sem):
        p = lax.axis_index("pipe")
        mine = p == layer
        start_either(mine, wm_o, wm_r, w_scr, sem.at[1])
        start_either(mine, ws_o, ws_r, ws, sem.at[0])
        pick(mine, wd_o, wd_r, wd)
        values = (x[0] if layer == 0 else x[...]).astype(F32)
        factor = lax.rsqrt(jnp.mean(values * values, axis=1, keepdims=True) + EPS)
        gain[...] = jnp.zeros(gain.shape, F32)
        wait_for(ws_r, ws, sem.at[0])
        wait_for(wm_r, w_scr, sem.at[1])
        for c in range(6):
            rows = slice(c * 256, (c + 1) * 256)
            out = dot_nt(d_gate[...], w_scr[0, rows, :])
            out = out + dot_nt(d_inner[...], w_scr[1, rows, :])
            out = out + dot_nt(d_small[...], ws[rows, :])
            out = out + dot(d_raw[:, :16], wd[:, rows])
            acc[:, rows] = out.astype(BF16)
            gain[c // 3 : c // 3 + 1, rows.start - c // 3 * Q : rows.stop - c // 3 * Q] = jnp.sum(
                out * (values[:, rows] * factor), axis=0, keepdims=True
            )
        send[...] = acc[half_rows(1 - p), :]
        keep[...] = acc[half_rows(p), :]

    ins = [(d_gate, None), (d_inner, None), (d_small, None), (d_raw, None)]
    ins += [(x, part((1, T, D), (m, 0, 0)) if layer == 0 else None)] + [(a, None) for a in wds]
    ins += [(a, ANY) for a in wss] + [(a, ANY) for a in ws_main]
    outs = [((HALF, D), BF16), ((HALF, D), BF16), ((8, Q), F32)]
    scratch = [
        pltpu.VMEM((16, D), BF16),
        pltpu.VMEM((D, 256), BF16),
        pltpu.VMEM((2, D, Q), BF16),
        pltpu.VMEM((T, D), BF16),
        pltpu.SemaphoreType.DMA((2,)),
    ]
    return kernel_call(body, ins, outs, scratch, f"project_back_{layer}_{m}")


def finish_back(layer, m, chip, arrived, x, a, pars, below):
    def body(*refs):
        chip, arrived, x, a, par_o, par_r = refs[:6]
        refs = refs[6:]
        if layer == 1:
            u_o, u_r, y = refs[:3]
            refs = refs[3:]
        out, par = refs
        p = lax.axis_index("pipe")
        mine = p == layer
        pick(mine, par_o, par_r, par)
        d_rounded = chip[...].astype(F32) + arrived[...].astype(F32)
        if layer == 0:
            xv = x[0, half_rows(p), :].astype(F32)
            av = a[:, :D].astype(F32)
        else:
            xv = x[:, :D].astype(F32)
            av = a[0, half_rows(p), :].astype(F32)
        factor = lax.rsqrt(jnp.mean(xv * xv, axis=1, keepdims=True) + EPS)
        normed = xv * factor
        gain = jnp.concatenate([par[NORM : NORM + 1, :], par[NORM + 1 : NORM + 2, :]], axis=1)
        pulled = d_rounded * gain
        mean = jnp.mean(pulled * normed, axis=1, keepdims=True)
        result = (av + factor * (pulled - normed * mean)).astype(BF16)
        out[:, :D] = result
        if layer == 1:
            branch = u_o[...].astype(F32) + u_r[...].astype(F32)
            gated = scalar_at(y[...].astype(F32), 0)
            total = jnp.sum(result.astype(F32) * branch, axis=1, keepdims=True)
            out[:, D:] = lanes_of(gated * gated * gated * (total / DI), 3).astype(BF16)
        else:
            out[:, D:] = jnp.zeros((HALF, 128), BF16)

    ins = [(chip, None), (arrived, None)]
    if layer == 0:
        ins += [(x, part((1, T, D), (m, 0, 0))), (a, None)]
    else:
        ins += [(x, None), (a, part((1, T, D), (m, 0, 0)))]
    ins += [(v, None) for v in pars]
    if layer == 1:
        narrow = part((HALF, D), (0, 0))
        ins += [(below[0], narrow), (below[1], narrow), (x, part((HALF, 128), (0, D // 128)))]
    outs = [((HALF, EXT), BF16)]
    return kernel_call(body, ins, outs, [pltpu.VMEM((32, Q), F32)], f"finish_back_{layer}_{m}", 16)[0]


def position():
    dp = lax.axis_index("dp")
    return dp // 8, (dp // 2) % 4, dp % 2


UNIT = 384
BLOCK = 256
WIDE = 2 * D - 512
BACK = WIDE // 2


def weight_stage(stage, layer, left, grads, arrived, onto=()):
    ins = [(v, None) for v in left]
    for group in grads:
        ins += [(v, None) for v in group["near"]] + [(v, ANY) for v in group["far"]]
    count = len(ins)

    def body(*refs):
        lefts, per, rest = refs[:2], (refs[2:8], refs[8:14]), refs[count:]
        rest, (gate_s, wide_s, cot_s, sem) = rest[:-4], rest[-4:]
        count_in, count_out = len(arrived), 4 if stage == 2 else 2
        came, far = rest[:count_in], rest[count_in : count_in + count_out]
        near = rest[count_in + count_out : count_in + 2 * count_out]
        total = rest[-1]
        if stage == 2:
            far = [ref.at[layer] for ref in far]
        moves = [pltpu.make_async_copy(near[n], far[n], sem.at[4 + n]) for n in range(count_out)]
        p = lax.axis_index("pipe")
        z, y, x = position()

        def copies(core):
            out = []
            for m in range(2):
                gate, wide, cot = per[m][3:]
                if core == 0:
                    out.append(pltpu.make_async_copy(gate, gate_s.at[m], sem.at[m]))
                else:
                    cot = cot.at[m] if layer == 1 else cot
                    out.append(pltpu.make_async_copy(wide, wide_s.at[m], sem.at[m]))
                    out.append(pltpu.make_async_copy(cot, cot_s.at[m], sem.at[2 + m]))
            return out

        def products(core, offset):
            inner = [per[m][0] for m in range(2)]
            cross = [per[m][2] for m in range(2)]
            shared = slice(Q, Q + 256) if core == 0 else slice(Q + 256, PAIR)
            small = [add_halves(per[m][1][shared, :], per[m][2][shared, :]) for m in range(2)]
            if core == 0:
                rows = [v[lax.rem(z + offset, 4)].reshape(UNIT, T) for v in lefts]
                yield 0, [dot(rows[m], gate_s[m]) for m in range(2)]
                yield Q, [dot_nt(rows[m], cross[m][:Q, :]) for m in range(2)]
                yield 2 * Q, [dot(rows[m], inner[m][...]) for m in range(2)]
                yield 3 * Q, [dot_nt(rows[m], small[m]) for m in range(2)]
            else:
                at = lax.rem(y + offset, 4)
                rows = [v[:, at].reshape(UNIT, T) for v in lefts]
                both = [
                    jnp.concatenate([channels(cross[m], at), wide_s[m, :, at].reshape(UNIT // 2, T)], axis=0)
                    for m in range(2)
                ]
                for n in range(2):
                    yield n * Q, [dot(both[m], cot_s[m, :, n * Q : (n + 1) * Q]) for m in range(2)]
                yield 2 * Q, [dot(rows[m], inner[m][...]) for m in range(2)]
                raw = [dot_nt(rows[m], small[m]) for m in range(2)]
                yield 3 * Q, [jnp.concatenate([v, jnp.zeros((UNIT, 128), F32)], axis=1) for v in raw]

        def channels(ref, at):
            rows = [ref[pl.ds(pl.multiple_of(n * UNIT + at * 96, 16), 96), :] for n in range(2)]
            return jnp.concatenate(rows, axis=0)

        def blocks(core, offset):
            for start, parts in products(core, offset):
                value = parts[0] + parts[1]
                for n in range(value.shape[1] // BLOCK):
                    at = start + n * BLOCK
                    yield slice(at, at + BLOCK), value[:, n * BLOCK : (n + 1) * BLOCK]

        def shifted(cols):
            return slice(cols.start - BACK, cols.stop - BACK)

        def run(core):
            if stage == 0:
                for cols, value in blocks(core, 2):
                    if cols.start < BACK:
                        near[0][:, cols] = value.astype(BF16)
                    else:
                        near[1][:, shifted(cols)] = value.astype(BF16)
                    if cols.stop == BACK:
                        moves[0].start()
                moves[1].start()
            elif stage == 1:
                (from_before, from_after), (to_after, to_before) = came, near
                for cols, value in blocks(core, 1):
                    if cols.start < BACK:
                        value = value + from_before[:, cols].astype(F32)
                    to_after[:, cols] = value.astype(BF16)
                moves[0].start()
                for cols, value in blocks(core, 3):
                    if cols.start >= BACK:
                        value = value + from_after[:, shifted(cols)].astype(F32)
                    to_before[:, cols] = value.astype(BF16)
                moves[1].start()
            else:
                from_before, from_after = came
                for cols, value in blocks(core, 0):
                    value = value + from_before[:, cols].astype(F32) + from_after[:, cols].astype(F32)
                    total[:, :, cols] = value.reshape(4, 96, BLOCK)
                here = y if core == 0 else z
                for offset in range(1, 4):
                    near[offset][...] = total[lax.rem(here + offset, 4)].astype(BF16)
                    moves[offset].start()
                near[0][...] = total[here]
                moves[0].start()

        for core in range(2):
            @pl.when(p == core)
            def _():
                loads = copies(core)
                for load in loads:
                    load.start()
                for load in loads:
                    load.wait()
                run(core)

        for move in moves:
            move.wait()

    if stage == 0:
        outs = [((UNIT, BACK), BF16)] * 2
    elif stage == 1:
        outs = [((UNIT, WIDE), BF16)] * 2
    else:
        outs = [((96, WIDE), F32)] + [((96, WIDE), BF16)] * 3
    scratch = [pltpu.VMEM(shape, dtype) for shape, dtype in outs]
    if stage == 2:
        scratch += [pltpu.VMEM((4, 96, WIDE), F32)]
        outs = [((2, *shape), dtype) for shape, dtype in outs]
    scratch += [
        pltpu.VMEM((2, T, Q), BF16),
        pltpu.VMEM((2, 2, 4, 96, T), BF16),
        pltpu.VMEM((2, T, D), BF16),
        pltpu.SemaphoreType.DMA((8,)),
    ]
    ins += [(a, None) for a in arrived]
    return kernel_call(body, ins, outs, scratch, f"grad_{layer}_{stage}", placed=len(outs), onto=onto)


def cut_rows(own, one, two, three):
    def body(own, one, two, three, mine, other, total):
        _, _, x = position()
        for layer in range(2):
            out = own[layer] + two[layer].astype(F32)
            out = out + (one[layer].astype(F32) + three[layer].astype(F32))
            total[...] = out.reshape(2, 48, WIDE)
            mine[layer] = total[x]
            other[layer] = total[1 - x].astype(BF16)

    outs = [((2, 48, WIDE), F32), ((2, 48, WIDE), BF16)]
    ins = [(a, None) for a in (own, one, two, three)]
    return kernel_call(body, ins, outs, [pltpu.VMEM((2, 48, WIDE), F32)], "grad_cut", 24)


def dp_index(z, y, x):
    return ((z % 4) * 4 + y % 4) * 2 + x % 2


def dp_pairs(move):
    places = [(z, y, x) for z in range(4) for y in range(4) for x in range(2)]
    return [(dp_index(*at), dp_index(*move(*at))) for at in places]


def along(axis, offset):
    if axis == "z":
        return dp_pairs(lambda z, y, x: (z + offset, y, x))
    if axis == "y":
        return dp_pairs(lambda z, y, x: (z, y + offset, x))
    return dp_pairs(lambda z, y, x: (z, y, x + offset))


def pair_shift(value, axes, distance):
    flip = {"z": lambda z, y, x: (z ^ distance, y, x), "y": lambda z, y, x: (z, y ^ distance, x)}
    pairs = [(32 * p + a, 32 * p + b) for p in range(2) for a, b in dp_pairs(flip[axes[p]])]
    return lax.ppermute(value, ("pipe", "dp"), pairs)


def shift(value, axis, offset):
    return lax.ppermute(value, "dp", along(axis, offset))


def core_shift(value, axes, offset):
    pairs = [(32 * p + a, 32 * p + b) for p in range(2) for a, b in along(axes[p], offset)]
    return lax.ppermute(value, ("pipe", "dp"), pairs)


def swap(value, axis="pipe"):
    return lax.ppermute(value, axis, [(0, 1), (1, 0)])


def add_halves(a, b):
    return (a.astype(F32) + b.astype(F32)).astype(BF16)


def scatter(layer, stage, args, arrived=()):
    sent = weight_stage(stage, layer, *args, arrived)
    return core_shift(sent[0], "zy", 1), core_shift(sent[1], "zy", 3)


def sum_rows(own, got):
    def body(own, got, mine, other, state_0, state_1, total):
        p = lax.axis_index("pipe")
        total[...] = own[...] + got[...].astype(F32)
        mine[...] = total[p]
        other[...] = total[1 - p]
        state_0[...] = total[0, :, 3 * Q :]
        state_1[...] = total[1, :, 3 * Q :]

    ins = [(own, None), (got, None)]
    outs = [((48, WIDE), F32), ((48, WIDE), F32), ((48, 256), F32), ((48, 256), F32)]
    scratch = [pltpu.VMEM((2, 48, WIDE), F32)]
    mine, other, state_0, state_1 = kernel_call(body, ins, outs, scratch, "grad_rows", 16)
    shared_0 = lax.ppermute(state_0, ("pipe", "tensor"), [(0, 1), (1, 0)])
    shared_1 = lax.ppermute(state_1, ("pipe", "tensor"), [(0, 3), (1, 2)])
    return mine, swap(other), shared_0, shared_1


def finish_weights(mine, got, shared_0, shared_1):
    def body(mine, got, shared_0, shared_1, main, state, step, out):
        p = lax.axis_index("pipe")
        for layer, (first, second, shared) in enumerate(((mine, got, shared_0), (got, mine, shared_1))):
            @pl.when(p == layer)
            def _():
                main[:, 0, :] = first[:, : 2 * Q]
                main[:, 1, :Q] = first[:, 2 * Q : 3 * Q]
                main[:, 1, Q:] = second[:, 2 * Q : 3 * Q]
                state[...] = first[:, 3 * Q :] + shared[...]
                step[...] = second[:, 3 * Q : 3 * Q + 2 * HQ]
                out[...] = second[:, : 2 * Q]

    ins = [(a, None) for a in (mine, got, shared_0, shared_1)]
    outs = [((48, 2, D), F32), ((48, 256), F32), ((48, 2 * HQ), F32), ((48, D), F32)]
    return kernel_call(body, ins, outs, (), "grad_finish", 24)


def join_sums(layer, m, keep, got):
    def body(keep, got, out):
        out[...] = add_halves(keep[...], got[...])

    return kernel_call(body, [(keep, None), (got, None)], [(keep.shape, BF16)], (), f"add_{layer}_{m}", 16)[0]


def sum_packs(packs):
    def body(*refs):
        out = refs[8]
        for layer in range(2):
            one, gain_one, two, gain_two = refs[4 * layer : 4 * layer + 4]
            out[layer] = one[...] + two[...]
            out[layer, 13:15, :] = gain_one[0:2, :] + gain_two[0:2, :]

    ins = [(a, None) for layer in packs for a in layer]
    return kernel_call(body, ins, [((2, 16, Q), F32)], (), "pack_sum", 16)[0]


def add_neighbour(pack, arrived):
    def body(pack, arrived, out, rows):
        out[...] = pack[...] + arrived[...]
        rows[...] = out[:, 8:16, :]

    return kernel_call(body, [(pack, None), (arrived, None)], [((2, 16, Q), F32), ((2, 8, Q), F32)], (), "pack_x", 16)


def add_shared_rows(pack, rows):
    def body(pack, rows, out):
        out[...] = pack[...]
        for layer in range(2):
            out[layer, 8:15, :] = pack[layer, 8:15, :] + rows[layer, :7, :]

    return kernel_call(body, [(pack, None), (rows, None)], [((2, 16, Q), F32)], (), "pack_shared", 16)[0]


def pack_quarters(pack, arrived):
    def body(pack, arrived, out):
        p = lax.axis_index("pipe")
        out[p] = pack[p]
        out[1 - p] = arrived[p]

    return kernel_call(body, [(pack, None), (arrived, None)], [((2, 16, Q), F32)], (), "pack_quarters", 16)[0]


def finish_packs(pair):
    def body(pair, norm, taps, state, bias, log, skip, gain):
        owner = (iota((Q, 128), 0) // 64 == iota((Q, 128), 1)).astype(F32)
        both = pair[0] + pair[1]
        norm[:, :Q] = both[13:14]
        norm[:, Q:] = both[14:15]
        state[...] = both[8:13, :256]
        for n in range(2):
            taps[:, n * Q : (n + 1) * Q] = pair[n, 0:5]
            gain[:, n * Q : (n + 1) * Q] = pair[n, 5:6]
        sums = [
            lax.dot_general(
                pair[n, 0:8],
                owner,
                (((1,), (0,)), ((), ())),
                precision=lax.Precision.HIGHEST,
                preferred_element_type=F32,
            )
            for n in range(2)
        ]
        skip[...] = jnp.concatenate([sums[0][6:7, :HQ], sums[1][6:7, :HQ]], axis=1)
        bias[...] = jnp.concatenate([pair[0, 7:8, :HQ], pair[1, 7:8, :HQ]], axis=1)
        log[...] = jnp.concatenate([pair[0, 7:8, 128 : 128 + HQ], pair[1, 7:8, 128 : 128 + HQ]], axis=1)

    outs = [(1, D), (5, D), (5, 256), (1, 2 * HQ), (1, 2 * HQ), (1, 2 * HQ), (1, D)]
    return kernel_call(body, [(pair, None)], [(s, F32) for s in outs], (), "pack_finish", 16)


def add_two(a, b, name):
    def body(a, b, out):
        out[...] = a[...] + b[...]

    return kernel_call(body, [(a, None), (b, None)], [(a.shape, F32)], (), name, 16)[0]


def assemble_states(lower, upper):
    def body(l0, l1, uo0, uo1, ur0, ur1, out):
        p = lax.axis_index("pipe")
        for m, (low, own, other) in enumerate(((l0, uo0, ur0), (l1, uo1, ur1))):
            @pl.when(p == 0)
            def _():
                out[m] = low[...]

            @pl.when(p == 1)
            def _():
                join(p, own, other, out.at[m], slice(0, D))

    arrays = list(lower) + [u[0] for u in upper] + [u[1] for u in upper]
    return kernel_call(body, [(a, None) for a in arrays], [((2, T, D), BF16)], (), "hidden_states", 24)[0]


def assemble_grads(lower, upper):
    def body(lo0, lo1, lr0, lr1, u0, u1, out):
        p = lax.axis_index("pipe")
        for m, (own, other, up) in enumerate(((lo0, lr0, u0), (lo1, lr1, u1))):
            @pl.when(p == 0)
            def _():
                join(p, own, other, out.at[m], slice(0, D))

            @pl.when(p == 1)
            def _():
                out[m] = up[...]

    arrays = [l[0] for l in lower] + [l[1] for l in lower] + list(upper)
    return kernel_call(body, [(a, None) for a in arrays], [((2, T, D), BF16)], (), "input_grads", 24)[0]


def local(
    hidden,
    segments,
    cotangent,
    norm_gain,
    main_w,
    state_w,
    step_w,
    conv_main,
    conv_state,
    step_bias,
    decay_log,
    skip_scale,
    gate_gain,
    out_w,
):
    ORDER.clear()
    COST[0] = 30
    p = lax.axis_index("pipe")
    hidden = hidden.reshape(2, T, D)
    cotangent = cotangent.reshape(2, T, D)
    seg = segments.reshape(2, 1, T)

    out_own, state_own = out_w[0], state_w[0]
    state_got = swap(state_own)
    wd = jnp.transpose(step_w[0], (1, 0))
    small = [norm_gain, conv_main[0], conv_state[0], step_bias, decay_log, skip_scale, gate_gain, wd]
    main_sent, main_own = kernel_call(
        slice_kernel,
        [(main_w[0], HBM)],
        [((D, 2, Q), BF16), ((D, 2, Q), BF16)],
        [pltpu.SemaphoreType.DMA((2,))],
        name="slices",
        limit=16,
        placed=2,
    )
    par_own, par_sent, wd_own, wd_sent = kernel_call(
        pack_kernel,
        [(a, None) for a in small],
        [((32, Q), F32), ((32, Q), F32), ((16, D), BF16), ((16, D), BF16)],
        name="pack",
        limit=16,
    )
    main_got = swap(jnp.transpose(main_sent, (1, 0, 2)))
    out_got = swap(lax.dynamic_slice(out_own, ((1 - p) * Q, 0), (Q, D)))
    main_own = jnp.transpose(main_own, (1, 0, 2))
    pars = (par_own, swap(par_sent))
    wds = (wd_own, swap(wd_sent))
    wss = (state_own, state_got)
    mains = (main_own, main_got)
    wos = (out_own, out_got)

    both = lambda: [None, None]
    projected, turned, mixes, chips, sums, result = ([both(), both()] for _ in range(6))
    gates, tails, smalls, back, back_sums, grads, packs = ([both(), both()] for _ in range(7))
    lower_a = both()

    def forward_project(layer, m):
        xs = hidden if layer == 0 else result[0][m]
        projected[layer][m] = project(layer, m, xs, pars, wds, wss, mains)

    def forward_mix(layer, m):
        _, pre, spre, raw = projected[layer][m][:4]
        mixed, inner, send, keep = mix(layer, m, pre, spre, raw, seg, pars, wos)
        mixes[layer][m] = (mixed, inner)
        chips[layer][m] = (keep, swap(send))

    def forward_add(layer, m):
        sums[layer][m] = join_sums(f"out_{layer}", m, *chips[layer][m])

    def forward_finish(layer, m):
        sums[layer][m] = (sums[layer][m], swap(sums[layer][m], "tensor"))
        if layer == 0:
            done = finish_forward(0, m, *sums[0][m], hidden, None)
        else:
            done = finish_forward(1, m, *sums[1][m], result[0][m][0], cotangent)
        result[layer][m] = (done, swap(done))

    def forward_turn(layer, m):
        turned[layer][m] = turn(layer, m, projected[layer][m][0])

    def backward_gate(layer, m):
        pre = projected[layer][m][1]
        mixed, inner = mixes[layer][m]
        if layer == 1:
            outs = gate_back(1, m, cotangent, result[1][m], pre, mixed, inner, pars, wos)
        else:
            *outs, lower_a[m] = gate_back(0, m, grads[1][m], result[0][m], pre, mixed, inner, pars, wos)
        gates[layer][m] = outs

    def backward_mix(layer, m):
        _, pre, spre, raw = projected[layer][m][:4]
        mixed, inner = mixes[layer][m]
        d_comb, cross, pack_a = (gates[layer][m][n] for n in (1, 3, 4))
        tails[layer][m] = mix_back(layer, m, d_comb, inner, pre, spre, raw, seg, mixed, cross, pack_a, pars)
        smalls[layer][m] = swap(tails[layer][m][2])
        packs[layer][m] = [tails[layer][m][4]]

    def backward_project(layer, m):
        d_inner, d_small, _, d_raw, _ = tails[layer][m]
        x = hidden if layer == 0 else projected[1][m][4]
        outs = project_back(layer, m, gates[layer][m][0], d_inner, d_small, d_raw, x, wds, wss, mains)
        send, keep, gain = outs
        packs[layer][m].append(gain)
        back[layer][m] = (keep, swap(send))

    def backward_add(layer, m):
        back_sums[layer][m] = join_sums(f"in_{layer}", m, *back[layer][m])

    def backward_finish(layer, m):
        back_sums[layer][m] = (back_sums[layer][m], swap(back_sums[layer][m], "tensor"))
        if layer == 1:
            done = finish_back(1, m, *back_sums[1][m], result[0][m][0], cotangent, pars, sums[0][m])
        else:
            done = finish_back(0, m, *back_sums[0][m], hidden, grads[1][m][0], pars, None)
        grads[layer][m] = (done, swap(done))

    def operands(layer):
        lefts = [turned[layer][m].reshape(4, 4, 96, T) for m in range(2)]
        groups = []
        for m in range(2):
            d_gate, _, scaled_t = gates[layer][m][:3]
            cot = cotangent if layer == 1 else lower_a[m]
            groups.append(
                {
                    "near": (tails[layer][m][0], tails[layer][m][2], smalls[layer][m]),
                    "far": (d_gate, scaled_t.reshape(2, 4, 96, T), cot),
                }
            )
        return lefts, groups

    forward_project(0, 0)
    forward_mix(0, 0)
    forward_project(0, 1)
    forward_add(0, 0)
    forward_mix(0, 1)
    forward_turn(0, 0)
    forward_add(0, 1)
    forward_finish(0, 0)
    forward_turn(0, 1)
    forward_project(1, 0)
    forward_mix(1, 0)
    forward_finish(0, 1)
    forward_add(1, 0)
    forward_project(1, 1)
    forward_mix(1, 1)
    forward_turn(1, 0)
    forward_add(1, 1)
    forward_finish(1, 0)
    forward_turn(1, 1)
    backward_gate(1, 0)
    backward_mix(1, 0)
    forward_finish(1, 1)
    backward_project(1, 0)
    meanwhile(smalls[1][0])
    backward_gate(1, 1)
    backward_add(1, 0)
    backward_mix(1, 1)
    backward_project(1, 1)
    backward_finish(1, 0)
    backward_add(1, 1)
    upper = operands(1)
    upper_moved = scatter(1, 0, upper)
    backward_gate(0, 0)
    backward_mix(0, 0)
    backward_finish(1, 1)
    meanwhile(smalls[0][0])
    COST[0] = 2
    upper_moved = scatter(1, 1, upper, upper_moved)
    backward_gate(0, 1)
    backward_mix(0, 1)
    lower = operands(0)
    COST[0] = 1
    lower_moved = scatter(0, 0, lower)
    backward_project(0, 0)
    backward_project(0, 1)
    backward_add(0, 0)
    pack = sum_packs([packs[layer][0] + packs[layer][1] for layer in range(2)])
    pack_got = shift(pack, "x", 1)
    done = weight_stage(2, 1, *upper, upper_moved)
    pack, pack_rows = add_neighbour(pack, pack_got)
    pack_rows = swap(pack_rows, "tensor")
    backward_add(0, 1)
    lower_moved = scatter(0, 1, lower, lower_moved)
    pack = add_shared_rows(pack, pack_rows)
    pack_got = swap(pack)
    states = assemble_states([projected[1][m][4] for m in range(2)], result[1])
    pack = pack_quarters(pack, pack_got)
    pack_got = pair_shift(pack, "zy", 2)
    pack = add_two(pack, pack_got, "pack_first")
    done = weight_stage(2, 0, *lower, lower_moved, done)
    done = [done[0]] + [core_shift(done[n], "yz", n) for n in (1, 2, 3)]
    backward_finish(0, 0)
    backward_finish(0, 1)
    input_grads = assemble_grads(grads[0], lower_a)
    pack_got = pair_shift(pack, "zy", 1)
    own, sent = cut_rows(*done)
    sent = core_shift(sent, "xx", 1)
    pack = add_two(pack, pack_got, "pack_first")
    pack = add_two(pack, pair_shift(pack, "yz", 2), "pack_second")
    pack = add_two(pack, pair_shift(pack, "yz", 1), "pack_second")
    done = sum_rows(own, sent)
    outs = finish_packs(pack)
    grad_norm, grad_taps, grad_state_taps, grad_bias, grad_log, grad_skip, grad_gain = outs
    grad_main, grad_state, grad_step, grad_out = finish_weights(*done)
    return (
        states.reshape(1, 2, 1, T, D),
        input_grads.reshape(1, 2, 1, T, D),
        grad_norm,
        grad_main[None],
        grad_state[None],
        grad_step[None],
        grad_taps[None],
        grad_state_taps[None],
        grad_bias,
        grad_log,
        grad_skip,
        grad_gain,
        grad_out[None],
    )


def solution(mesh):
    in_specs = (
        P(None, "dp", None, None),
        P(None, "dp", None),
        P(None, "dp", None, None),
        P("pipe", None),
        P("pipe", None, None, "tensor"),
        P("pipe", None, None),
        P("pipe", None, "tensor"),
        P("pipe", None, "tensor"),
        P("pipe", None, None),
        P("pipe", "tensor"),
        P("pipe", "tensor"),
        P("pipe", "tensor"),
        P("pipe", "tensor"),
        P("pipe", "tensor", None),
    )
    out_specs = (
        P("pipe", None, "dp", None, None),
        P("pipe", None, "dp", None, None),
        P("pipe", None),
        P("pipe", "dp", None, "tensor"),
        P("pipe", "dp", None),
        P("pipe", "dp", "tensor"),
        P("pipe", None, "tensor"),
        P("pipe", None, None),
        P("pipe", "tensor"),
        P("pipe", "tensor"),
        P("pipe", "tensor"),
        P("pipe", "tensor"),
        P("pipe", ("tensor", "dp"), None),
    )
    return jax.shard_map(local, mesh=mesh, in_specs=in_specs, out_specs=out_specs, check_vma=False)
```
